32 devices in a mesh: lm: 8 (over y, x, core), cam: 4 (over z).
Axes of the slice: x: 2, y: 2, z: 4, core: 2. Of those that a mesh axis runs over, the one named last changes fastest.
Arguments:
- panels: bfloat16 [64, 16, 64, 384], P(('lm', 'cam')), may hold values from -0.59765625 to 0.59765625
- curvature: float32 [3, 3, 8192], P(None, None, ('lm', 'cam')), as said below
- visible_blocks: int32 [64, 16], P(('lm', 'cam')), may hold values from 0 to 31, as said below
- counts: int32 [64], P(('lm', 'cam')), may hold values from 2 to 16
- camera_hessian: float32 [32, 64, 64], P('lm'), may hold values from -6 to 6
Outputs:
- reduced_system: float32 [2048, 2048], P('lm', 'cam')
The draws below stay inside these ranges and needn't reach their ends.
Inputs may be any that keep to these rules, and one draw needn't show every extreme that they name: `visible_blocks`: the 16 ids of a tile are distinct and lie in a window of 16 consecutive camera blocks, counted cyclically. `curvature`: each landmark's block is symmetric and strictly diagonally dominant.
All inputs are finite; a program needn't handle non-finite values.
Results may differ from the reference program's by a relative error of at most 0.0003.
Values may be sent and summed in bfloat16 or wider, within the bound.
No kernel may reach another device: no remote copies, remote signals or barrier semaphores. Data moves between devices by JAX's collectives and lax.ppermute only.
A program may use at most 128 MiB of HBM per device.

```python
import jax
import jax.numpy as jnp
from jax import lax

CB = 64
LMB = 128
K = 16
NCAMB = 32
CAMS = 2048
NLB = 64


def window_ids(single_key):
    return jax.random.permutation(single_key, NCAMB // 2)[:K]


def draw_visible_blocks(key, part):
    key = jax.random.fold_in(key, 11)
    centre_key, window_key = jax.random.split(key)
    centre = jax.random.randint(centre_key, (NLB, 1), 0, NCAMB)
    offsets = jax.vmap(window_ids)(jax.random.split(window_key, NLB))
    return ((centre + offsets) % NCAMB).astype(jnp.int32)


def draw_curvature(key, part):
    key = jax.random.fold_in(key, 7)
    diag_key, off_key = jax.random.split(key)
    count = NLB * LMB
    diagonal = jnp.exp(jax.random.uniform(diag_key, (3, count), jnp.float32, jnp.log(1.0), jnp.log(10.0)))
    factors = jax.random.uniform(off_key, (3, count), jnp.float32, -0.45, 0.45)
    upper01 = factors[0] * jnp.minimum(diagonal[0], diagonal[1])
    upper02 = factors[1] * jnp.minimum(diagonal[0], diagonal[2])
    upper12 = factors[2] * jnp.minimum(diagonal[1], diagonal[2])
    first = jnp.stack([diagonal[0], upper01, upper02])
    second = jnp.stack([upper01, diagonal[1], upper12])
    third = jnp.stack([upper02, upper12, diagonal[2]])
    return jnp.stack([first, second, third]).astype(jnp.float32)


def place_ends(array, key, low, high):
    longest = array.shape.index(max(array.shape))
    spots = []
    for shift in (0, 1):
        where = [jax.random.randint(jax.random.fold_in(key, axis), (), 0, length) for axis, length in enumerate(array.shape)]
        where[longest] = (where[longest] + shift) % array.shape[longest]
        spots.append(tuple(where))
    return array.at[spots[0]].set(low).at[spots[1]].set(high)


def steps_of(key, extent, shards, smallest, largest):
    def one(position, blocks):
        steps = jax.random.uniform(jax.random.fold_in(jax.random.fold_in(key, 6), position), (blocks,), jnp.float32, smallest / len(shards), largest / len(shards))
        return jnp.repeat(jnp.exp(steps), extent[position] // blocks).reshape((-1,) + (1,) * (len(extent) - position - 1))

    loudness = one(*shards[0])
    for cut in shards[1:]:
        loudness = loudness * one(*cut)
    return loudness


def scatter_about(rng, dims, deviation, bound, shards=(), held_as=jnp.bfloat16):
    values = jax.random.normal(rng, dims, jnp.float32) * deviation
    if len(shards) > 0:
        values = steps_of(rng, dims, shards, -0.22, 0.18) * values
    return jnp.clip(values, min=-bound, max=bound).astype(held_as)


def setup_inputs(seed: int = 0) -> dict:
    key_list = jax.random.split(jax.random.key(seed), 6)
    return {
        "panels": scatter_about(key_list[0], (NLB, K, CB, 3 * LMB), 0.1, 0.59765625, ((0, 32),)),
        "curvature": draw_curvature(jax.random.fold_in(key_list[5], 71), 0),
        "visible_blocks": draw_visible_blocks(jax.random.fold_in(key_list[5], 71), 0),
        "counts": place_ends(jax.random.randint(key_list[3], (NLB,), 2, K + 1), jax.random.fold_in(key_list[3], 1), 2, K).astype(jnp.int32),
        "camera_hessian": scatter_about(key_list[4], (NCAMB, CB, CB), 1.0, 6.0, ((0, 8),), jnp.float32),
    }


def invert_three(matrix):
    entry = [[matrix[row_pos, col_pos] for col_pos in range(3)] for row_pos in range(3)]
    cofactor = [[entry[(row_pos + 1) % 3][(col_pos + 1) % 3] * entry[(row_pos + 2) % 3][(col_pos + 2) % 3] - entry[(row_pos + 1) % 3][(col_pos + 2) % 3] * entry[(row_pos + 2) % 3][(col_pos + 1) % 3] for col_pos in range(3)] for row_pos in range(3)]
    determ = entry[0][0] * cofactor[0][0] + entry[0][1] * cofactor[0][1] + entry[0][2] * cofactor[0][2]
    return jnp.stack([jnp.stack([cofactor[col_pos][row_pos] / determ for col_pos in range(3)]) for row_pos in range(3)])


def form_panel(block_panel, inverse):
    split = block_panel.astype(jnp.float32).reshape(block_panel.shape[:-1] + (3, LMB))
    pieces = []
    for target in range(3):
        pieces.append(split[..., 0, :] * inverse[0, target] + split[..., 1, :] * inverse[1, target] + split[..., 2, :] * inverse[2, target])
    return jnp.stack(pieces, axis=-2).reshape(block_panel.shape)


def reference(panels, curvature, visible_blocks, counts, camera_hessian):
    live = jnp.arange(K, dtype=jnp.int32)[None, :] < counts[:, None]
    masked = jnp.where(live[:, :, None, None], panels, jnp.zeros_like(panels))
    inverse = invert_three(curvature).reshape(3, 3, NLB, LMB)
    tile_inverse = jnp.transpose(inverse, (2, 0, 1, 3))

    def one_tile(total, inputs):
        block_panel, block_inverse, block_ids = inputs
        formed = form_panel(block_panel, block_inverse)
        product = jnp.dot(formed.reshape(K * CB, 3 * LMB), block_panel.astype(jnp.float32).reshape(K * CB, 3 * LMB).T, precision=lax.Precision.HIGHEST, preferred_element_type=jnp.float32)
        product = jnp.transpose(product.reshape(K, CB, K, CB), (0, 2, 1, 3))
        total = total.at[block_ids[:, None], block_ids[None, :]].add(product)
        return total, None

    start_total = jnp.zeros((NCAMB, NCAMB, CB, CB), jnp.float32)
    total, unused = lax.scan(one_tile, start_total, (masked, tile_inverse, visible_blocks))
    reduced = jnp.transpose(total, (0, 2, 1, 3)).reshape(CAMS, CAMS)
    identity = jnp.eye(NCAMB, dtype=jnp.float32)
    hessian = (identity[:, None, :, None] * camera_hessian[:, :, None, :]).reshape(CAMS, CAMS)
    return hessian - reduced
```

```python
import functools
import math

import jax
import jax.numpy as jnp
from jax import lax
from jax.experimental import pallas as pl
from jax.experimental.pallas import tpu as pltpu
from jax.sharding import PartitionSpec as P

CB = 64
LMB = 128
K = 16
WIDTH = 3 * LMB
STRIP = 16
VMEM = pl.BlockSpec(memory_space=pltpu.VMEM)
SMEM = pl.BlockSpec(memory_space=pltpu.SMEM)
PARAMS = pltpu.CompilerParams(vmem_limit_bytes=56 * 1024 * 1024)


def invert_rows(cur_ref, tile):
    lanes = slice(tile * LMB, (tile + 1) * LMB)
    entry = [[cur_ref[row, col : col + 1, lanes] for col in range(3)] for row in range(3)]
    cofactor = [
        [
            entry[(row + 1) % 3][(col + 1) % 3] * entry[(row + 2) % 3][(col + 2) % 3]
            - entry[(row + 1) % 3][(col + 2) % 3] * entry[(row + 2) % 3][(col + 1) % 3]
            for col in range(3)
        ]
        for row in range(3)
    ]
    determ = (
        entry[0][0] * cofactor[0][0] + entry[0][1] * cofactor[0][1] + entry[0][2] * cofactor[0][2]
    )
    return [[cofactor[col][row] / determ for col in range(3)] for row in range(3)]


def encode(dst, values, blocks):
    columns = values.shape[1]
    row = lax.broadcasted_iota(jnp.int32, (STRIP, columns), 0)
    strip = jnp.zeros((STRIP, columns), jnp.float32)
    for block in range(blocks):
        part = values[block * CB : (block + 1) * CB]
        top = jnp.max(jnp.abs(part), axis=0, keepdims=True)
        power = jnp.ceil(jnp.log2(jnp.maximum(top, 2.0**-100)) - 14.99)
        dst[pl.ds(block * CB, CB), :] = (
            jnp.round(part * jnp.exp2(-power)).astype(jnp.int32).astype(jnp.int16)
        )
        strip = jnp.where(row == block, power, strip)
    dst[pl.ds(blocks * CB, STRIP), :] = strip.astype(jnp.int32).astype(jnp.int16)


def decode(src, blocks):
    strip = src[pl.ds(blocks * CB, STRIP), :].astype(jnp.int32).astype(jnp.float32)
    scale = jnp.exp2(strip)
    return [
        src[pl.ds(block * CB, CB), :].astype(jnp.int32).astype(jnp.float32)
        * scale[block : block + 1]
        for block in range(blocks)
    ]


def partial_kernel(plan, me_ref, ids_a, ids_b, pan_a, pan_b, cur_a, cur_b, *rest):
    pieces, n_cam, row_blocks, chips, orders, tiles = plan
    sends, keeps = rest[:pieces], rest[pieces : 2 * pieces]
    cols, rows, acc, row_live, col_live = rest[2 * pieces :]
    piece, half, kind = pl.program_id(0), pl.program_id(1), pl.program_id(2)
    chip, core, cam = me_ref[0], me_ref[1], me_ref[2]
    group = acc.shape[1] // n_cam
    per = group // CB

    @pl.when((piece == 0) & (half == 0) & (kind == 0))
    def prepare():
        cols[...] = jnp.zeros_like(cols)
        rows[...] = jnp.zeros_like(rows)
        for tile in range(2 * tiles):
            for spot in range(chips):
                row_live[tile, spot] = 0
            for spot in range(pieces * n_cam):
                col_live[tile, spot] = 0
        for tile in range(2 * tiles):
            ids, pan, cur = (ids_a, pan_a, cur_a) if tile < tiles else (ids_b, pan_b, cur_b)
            here = tile % tiles
            inverse = invert_rows(cur, here)

            def place(slot, carry):
                ident = ids[here, slot]

                @pl.when(ident >= 0)
                def live():
                    panel = pan[here, slot]
                    inner = ident % (per * pieces)
                    column = (inner // per) * n_cam + ((ident // (per * pieces)) ^ cam)
                    start = pl.multiple_of((column * per + inner % per) * CB, CB)
                    cols[tile, pl.ds(start, CB), :] = panel
                    col_live[tile, column] = 1
                    owner = ident // row_blocks

                    @pl.when(owner % 2 == core)
                    def mine():
                        spot = (owner // 2) ^ chip
                        row_live[tile, spot] = 1
                        first = pl.multiple_of((spot * row_blocks + ident % row_blocks) * CB, CB)
                        wide = panel.astype(jnp.float32)
                        split = [wide[:, c * LMB : (c + 1) * LMB] for c in range(3)]
                        for target in range(3):
                            formed = (
                                split[0] * inverse[0][target]
                                + split[1] * inverse[1][target]
                                + split[2] * inverse[2][target]
                            )
                            high = formed.astype(jnp.bfloat16)
                            low = (formed - high.astype(jnp.float32)).astype(jnp.bfloat16)
                            lanes = slice(target * LMB, (target + 1) * LMB)
                            rows[tile, 0, pl.ds(first, CB), lanes] = high
                            rows[tile, 1, pl.ds(first, CB), lanes] = low

                return carry

            lax.fori_loop(0, K, place, 0)

    index = half + (1 - kind) * (chips // 2)
    bits = int(math.log2(chips))
    spot = jnp.int32(0)
    for which in range(pieces):
        value = jnp.int32(0)
        for place_of, bit in enumerate(orders[which]):
            value = value + (((index >> (bits - 1 - place_of)) & 1) << bit)
        spot = jnp.where(piece == which, value, spot)
    extent = row_blocks * CB
    first = pl.multiple_of(spot * extent, extent)
    acc[...] = jnp.zeros_like(acc)

    def columns_of(other, carry):
        column = piece * n_cam + other
        lanes = pl.ds(pl.multiple_of(other * group, group), group)
        start = pl.multiple_of(column * group, group)
        for tile in range(2 * tiles):

            @pl.when((row_live[tile, spot] > 0) & (col_live[tile, column] > 0))
            def add():
                right = cols[tile, pl.ds(start, group), :]
                total = acc[:, lanes]
                for level in range(2):
                    total = total + lax.dot_general(
                        rows[tile, level, pl.ds(first, extent), :],
                        right,
                        (((1,), (1,)), ((), ())),
                        preferred_element_type=jnp.float32,
                    )
                acc[:, lanes] = total

        return carry

    lax.fori_loop(0, n_cam, columns_of, 0)
    for which in range(pieces):

        @pl.when((piece == which) & (kind == 0))
        def send():
            encode(sends[which].at[0], acc[...], row_blocks)

        @pl.when((piece == which) & (kind == 1))
        def keep():
            keeps[which][0] = acc[...]


def relay_kernel(row_blocks, keep_ref, *rest):
    dst = rest[-1]
    total = keep_ref[0]
    for came in rest[:-1]:
        total = total + jnp.concatenate(decode(came.at[0], row_blocks), axis=0)
    encode(dst.at[0], total, row_blocks)


def finish_kernel(plan, me_ref, wide_ref, *rest):
    pieces, row_blocks, row_shift, col_blocks, counts = plan
    out_ref = rest[-1]
    cursor = 0
    group = out_ref.shape[1] // pieces
    first_row = (me_ref[0] * 2 + me_ref[1]) * row_blocks
    first_col = me_ref[2] * col_blocks
    for piece in range(pieces):
        keep = rest[cursor]
        came = rest[cursor + 1 : cursor + counts]
        cursor += counts
        parts = [decode(ref.at[0], row_blocks) for ref in came]
        for block in range(row_blocks):
            total = keep[0, pl.ds(block * CB, CB), :]
            for part in parts:
                total = total + part[block]
            for pair in range(group // (2 * CB)):
                lane = lax.broadcasted_iota(jnp.int32, (CB, 2 * CB), 1)
                base = first_col + (piece * group) // CB + 2 * pair
                hit = base + lane // CB == first_row + block
                wide = jnp.where(hit, wide_ref[block], 0.0)
                start = piece * group + pair * 2 * CB
                out_ref[pl.ds(block * CB, CB), pl.ds(start, 2 * CB)] = (
                    wide - total[:, pair * 2 * CB : (pair + 1) * 2 * CB]
                )


def body(panels, curvature, visible_blocks, counts, camera_hessian):
    tiles = panels.shape[0]
    n_lm, n_cam = lax.axis_size("lm"), lax.axis_size("cam")
    chips = n_lm // 2
    bits = int(math.log2(chips))
    row_blocks = camera_hessian.shape[0]
    extent = row_blocks * CB
    col_blocks = row_blocks * n_lm // n_cam
    pieces = 2
    group = col_blocks * CB // pieces
    columns = group * n_cam
    coded = extent + STRIP
    orders = [list(range(bits)), list(reversed(range(bits)))]
    lm, cam = lax.axis_index("lm"), lax.axis_index("cam")
    me = jnp.stack([lm // 2, lm % 2, cam]).astype(jnp.int32)

    live = jnp.arange(K, dtype=jnp.int32)[None, :] < counts[:, None]
    ids = jnp.where(live, visible_blocks, -1)

    def swap(value, bit):
        return lax.ppermute(value, "lm", [(i, i ^ (1 << bit)) for i in range(n_lm)])

    ids_other, cur_other, pan_other = swap(ids, 0), swap(curvature, 0), swap(panels, 0)

    def place_of(which):
        def index(piece, half, kind):
            inside = jnp.where(piece == which, half, jnp.where(piece < which, 0, chips // 2 - 1))
            return (inside, 0, 0)

        return index

    outs = pl.pallas_call(
        functools.partial(
            partial_kernel, (pieces, n_cam, row_blocks, chips, orders, tiles)
        ),
        grid=(pieces, chips // 2, 2),
        in_specs=[SMEM] * 3 + [VMEM] * 4,
        out_specs=[pl.BlockSpec((1, coded, columns), place_of(which)) for which in range(pieces)]
        + [pl.BlockSpec((1, extent, columns), place_of(which)) for which in range(pieces)],
        out_shape=[jax.ShapeDtypeStruct((chips // 2, coded, columns), jnp.int16)] * pieces
        + [jax.ShapeDtypeStruct((chips // 2, extent, columns), jnp.float32)] * pieces,
        scratch_shapes=[
            pltpu.VMEM((2 * tiles, pieces * columns, WIDTH), jnp.bfloat16),
            pltpu.VMEM((2 * tiles, 2, chips * extent, WIDTH), jnp.bfloat16),
            pltpu.VMEM((extent, columns), jnp.float32),
            pltpu.SMEM((2 * tiles, chips), jnp.int32),
            pltpu.SMEM((2 * tiles, pieces * n_cam), jnp.int32),
        ],
        compiler_params=PARAMS,
        name="partial",
    )(me, ids, ids_other, panels, pan_other, curvature, cur_other)
    sends, keeps = list(outs[:pieces]), outs[pieces:]

    came = [[] for _ in range(pieces)]
    for stage in range(bits):
        for piece in range(pieces):
            came[piece].append(swap(sends[piece], orders[piece][stage] + 1))
        size = chips >> (stage + 1)
        if size == 1:
            break
        for piece in range(pieces):
            arrays = [keeps[piece]] + came[piece]

            def later(half, block):
                return (size // 2 + half, 0, block)

            def out_at(half, block):
                return (half, 0, block)

            lanes = 256
            sends[piece] = pl.pallas_call(
                functools.partial(relay_kernel, row_blocks),
                grid=(size // 2, columns // lanes),
                in_specs=[pl.BlockSpec((1, extent, lanes), later)]
                + [pl.BlockSpec((1, coded, lanes), later)] * len(came[piece]),
                out_specs=pl.BlockSpec((1, coded, lanes), out_at),
                out_shape=jax.ShapeDtypeStruct((size // 2, coded, columns), jnp.int16),
                compiler_params=PARAMS,
                name="relay",
            )(*arrays)

    finals = []
    for piece in range(pieces):
        arrays = [keeps[piece]] + came[piece]

        def far(other):
            return (0, 0, other + 1)

        crossed = pl.pallas_call(
            functools.partial(relay_kernel, row_blocks),
            grid=(n_cam - 1,),
            in_specs=[pl.BlockSpec((1, extent, group), far)]
            + [pl.BlockSpec((1, coded, group), far)] * len(came[piece]),
            out_specs=pl.BlockSpec((1, coded, group), lambda other: (other, 0, 0)),
            out_shape=jax.ShapeDtypeStruct((n_cam - 1, coded, group), jnp.int16),
            compiler_params=PARAMS,
            name="cross",
        )(*arrays)
        last = [
            lax.ppermute(
                crossed[other - 1 : other], "cam", [(i, i ^ other) for i in range(n_cam)]
            )
            for other in range(1, n_cam)
        ]
        finals.append(arrays + last)

    wide = jnp.concatenate([camera_hessian, camera_hessian], axis=-1)
    specs, flat = [], []
    for piece in range(pieces):
        for pos, array in enumerate(finals[piece]):
            shape = (1, extent if pos == 0 else coded, group)
            specs.append(pl.BlockSpec(shape, lambda step: (0, 0, 0)))
            flat.append(array)
    return pl.pallas_call(
        functools.partial(
            finish_kernel, (pieces, row_blocks, chips, col_blocks, len(finals[0]))
        ),
        grid=(1,),
        in_specs=[SMEM, VMEM] + specs,
        out_specs=pl.BlockSpec((extent, col_blocks * CB), lambda step: (0, 0)),
        out_shape=jax.ShapeDtypeStruct((extent, col_blocks * CB), jnp.float32),
        compiler_params=PARAMS,
        name="finish",
    )(me, wide, *flat)


def solution(mesh):
    return jax.shard_map(
        body,
        mesh=mesh,
        in_specs=(
            P(("lm", "cam"), None, None, None),
            P(None, None, ("lm", "cam")),
            P(("lm", "cam"), None),
            P(("lm", "cam")),
            P("lm", None, None),
        ),
        out_specs=P("lm", "cam"),
        check_vma=False,
    )
```

```python
import functools
import math

import jax
import jax.numpy as jnp
from jax import lax
from jax.experimental import pallas as pl
from jax.experimental.pallas import tpu as pltpu
from jax.sharding import PartitionSpec as P

CB = 64
LMB = 128
K = 16
WIDTH = 3 * LMB
STRIP = 16
LANES = 128
CHUNK = 256
QUAD = CHUNK // CB
VMEM = pl.BlockSpec(memory_space=pltpu.VMEM)
SMEM = pl.BlockSpec(memory_space=pltpu.SMEM)
PARAMS = pltpu.CompilerParams(vmem_limit_bytes=32 * 1024 * 1024)


def invert_rows(cur_ref, tile):
    lanes = slice(tile * LMB, (tile + 1) * LMB)
    entry = [[cur_ref[row, col : col + 1, lanes] for col in range(3)] for row in range(3)]
    cofactor = [
        [
            entry[(row + 1) % 3][(col + 1) % 3] * entry[(row + 2) % 3][(col + 2) % 3]
            - entry[(row + 1) % 3][(col + 2) % 3] * entry[(row + 2) % 3][(col + 1) % 3]
            for col in range(3)
        ]
        for row in range(3)
    ]
    determ = (
        entry[0][0] * cofactor[0][0] + entry[0][1] * cofactor[0][1] + entry[0][2] * cofactor[0][2]
    )
    return [[cofactor[col][row] / determ for col in range(3)] for row in range(3)]


def encode(dst, lanes, parts):
    blocks = len(parts)
    row = lax.broadcasted_iota(jnp.int32, (8, LANES), 0)
    tops = jnp.full((8, LANES), 2.0**-100, jnp.float32)
    for block, part in enumerate(parts):
        top = jnp.max(jnp.abs(part), axis=0, keepdims=True)
        tops = jnp.where(row == block, jnp.maximum(top, tops), tops)
    power = jnp.ceil(jnp.log2(tops) - 14.99)
    inverse = jnp.exp2(-power)
    for block, part in enumerate(parts):
        coded = jnp.round(part * inverse[block : block + 1])
        dst[pl.ds(block * CB, CB), lanes] = coded.astype(jnp.int32).astype(jnp.int16)
    strip = jnp.concatenate([power, power], axis=0).astype(jnp.int32)
    dst[pl.ds(blocks * CB, STRIP), lanes] = strip.astype(jnp.int16)


def decode(src, lanes, blocks):
    strip = src[pl.ds(blocks * CB, STRIP), lanes].astype(jnp.int32).astype(jnp.float32)
    scale = jnp.exp2(strip)
    return [
        src[pl.ds(block * CB, CB), lanes].astype(jnp.int32).astype(jnp.float32)
        * scale[block : block + 1]
        for block in range(blocks)
    ]


def gathered(keep, came, lanes, blocks):
    parts = [keep[pl.ds(block * CB, CB), lanes] for block in range(blocks)]
    for src in came:
        parts = [part + other for part, other in zip(parts, decode(src, lanes, blocks))]
    return parts


def spot_of(index, order):
    bits = len(order)
    return sum(((index >> (bits - 1 - pos)) & 1) << bit for pos, bit in enumerate(order))


def partial_kernel(plan, me_ref, ids_a, ids_b, pan_a, pan_b, cur_a, cur_b, *rest):
    turn, per, pieces, n_cam, row_blocks, chips, orders, tiles, chunks = plan
    sends, keeps = rest[:2], rest[2:4]
    rows, right, acc, slot_at, row_at, many, busy = rest[4:]
    step = pl.program_id(0)
    chip, core, cam = me_ref[0], me_ref[1], me_ref[2]
    extent = row_blocks * CB
    total_chunks = 2 * chunks

    @pl.when(step == 0)
    def prepare():
        def clear(spot, carry):
            for tile in range(2 * tiles):
                slot_at[tile, spot] = -1
            return carry

        lax.fori_loop(0, total_chunks * QUAD, clear, 0)
        for tile in range(2 * tiles):
            for chunk in range(total_chunks):
                busy[tile, chunk] = 0
        for tile in range(2 * tiles):
            ids, pan, cur = (ids_a, pan_a, cur_a) if tile < tiles else (ids_b, pan_b, cur_b)
            here = tile % tiles
            inverse = invert_rows(cur, here)

            def place(slot, count):
                ident = ids[here, slot]
                live = ident >= 0
                known = jnp.maximum(ident, 0)
                inner = known % (per * pieces)
                piece = inner // per - 2 * turn
                column = piece * n_cam + ((known // (per * pieces)) ^ cam)
                spot = column * per + inner % per

                @pl.when(live & (piece >= 0) & (piece < 2))
                def listed():
                    slot_at[tile, spot] = slot
                    busy[tile, spot // QUAD] = 1

                owner = known // row_blocks
                mine = live & (owner % 2 == core)

                @pl.when(mine)
                def form():
                    group = (owner // 2) ^ chip
                    row_at[tile, count] = (group * row_blocks + known % row_blocks) * CB
                    first = pl.multiple_of(count * CB, CB)
                    wide = pan[here, slot].astype(jnp.float32)
                    split = [wide[:, c * LMB : (c + 1) * LMB] for c in range(3)]
                    for target in range(3):
                        formed = (
                            split[0] * inverse[0][target]
                            + split[1] * inverse[1][target]
                            + split[2] * inverse[2][target]
                        )
                        high = formed.astype(jnp.bfloat16)
                        low = (formed - high.astype(jnp.float32)).astype(jnp.bfloat16)
                        at = target * LMB
                        rows[tile, pl.ds(first, CB), at : at + LMB] = high
                        rows[tile, pl.ds(first, CB), WIDTH + at : WIDTH + at + LMB] = low

                return count + jnp.where(mine, 1, 0)

            count = lax.fori_loop(0, K, place, jnp.int32(0))
            many[tile] = (count + QUAD - 1) // QUAD
            for extra in range(QUAD):
                row_at[tile, count + extra] = chips * extent

    acc[...] = jnp.zeros_like(acc)
    for tile in range(2 * tiles):
        pan, here = (pan_a if tile < tiles else pan_b), tile % tiles

        @pl.when(busy[tile, step] > 0)
        def add():
            for quarter in range(QUAD):
                slot = slot_at[tile, step * QUAD + quarter]
                lines = slice(quarter * CB, (quarter + 1) * CB)

                @pl.when(slot >= 0)
                def fill():
                    panel = pan[here, slot]
                    right[tile % 2, lines, :WIDTH] = panel
                    right[tile % 2, lines, WIDTH:] = panel

                @pl.when(slot < 0)
                def blank():
                    right[tile % 2, lines, :] = jnp.zeros((CB, 2 * WIDTH), jnp.bfloat16)

            def product(group, carry):
                first = pl.multiple_of(group * QUAD * CB, QUAD * CB)
                result = lax.dot_general(
                    rows[tile, pl.ds(first, QUAD * CB), :],
                    right[tile % 2],
                    (((1,), (1,)), ((), ())),
                    preferred_element_type=jnp.float32,
                )
                for quarter in range(QUAD):
                    at = pl.multiple_of(row_at[tile, group * QUAD + quarter], CB)
                    acc[pl.ds(at, CB), :] += result[quarter * CB : (quarter + 1) * CB]
                return carry

            lax.fori_loop(0, many[tile], product, 0)

    for which in range(2):

        @pl.when(step // chunks == which)
        def store():
            for half in range(chips // 2):
                first = spot_of(half + chips // 2, orders[which]) * extent
                for start in range(0, CHUNK, LANES):
                    lanes = pl.ds(start, LANES)
                    parts = [
                        acc[pl.ds(first + block * CB, CB), lanes] for block in range(row_blocks)
                    ]
                    encode(sends[which].at[half], lanes, parts)
                first = spot_of(half, orders[which]) * extent
                keeps[which][half] = acc[pl.ds(first, extent), :]


def relay_kernel(row_blocks, keep_ref, *rest):
    dst = rest[-1].at[0]
    for start in range(0, dst.shape[1], LANES):
        lanes = pl.ds(start, LANES)
        came = [ref.at[0] for ref in rest[:-1]]
        encode(dst, lanes, gathered(keep_ref.at[0], came, lanes, row_blocks))


def cross_kernel(row_blocks, group, arrays, *rest):
    dsts = rest[2 * arrays :]
    for piece in range(2):
        keep = rest[piece * arrays].at[0]
        came = [ref.at[0] for ref in rest[piece * arrays + 1 : (piece + 1) * arrays]]
        for other, dst in enumerate(dsts):
            for start in range(0, group, LANES):
                lanes = pl.ds((other + 1) * group + start, LANES)
                parts = gathered(keep, came, lanes, row_blocks)
                encode(dst.at[piece], pl.ds(start, LANES), parts)


def finish_kernel(plan, me_ref, wide_ref, *rest):
    turn, row_blocks, col_blocks, arrays, far = plan
    out_ref = rest[-1]
    group = out_ref.shape[1] // 2
    first_row = (me_ref[0] * 2 + me_ref[1]) * row_blocks
    first_col = me_ref[2] * col_blocks
    lane = lax.broadcasted_iota(jnp.int32, (CB, LANES), 1) // CB
    for piece in range(2):
        keep = rest[piece * arrays].at[0]
        came = [ref.at[0] for ref in rest[piece * arrays + 1 : (piece + 1) * arrays]]
        came += [ref.at[piece] for ref in rest[2 * arrays : 2 * arrays + far]]
        for start in range(0, group, LANES):
            parts = gathered(keep, came, pl.ds(start, LANES), row_blocks)
            base = first_col + ((2 * turn + piece) * group + start) // CB
            for block in range(row_blocks):
                wide = jnp.where(base + lane == first_row + block, wide_ref[block], 0.0)
                out_ref[pl.ds(block * CB, CB), pl.ds(piece * group + start, LANES)] = (
                    wide - parts[block]
                )


def body(panels, curvature, visible_blocks, counts, camera_hessian):
    tiles = panels.shape[0]
    n_lm, n_cam = lax.axis_size("lm"), lax.axis_size("cam")
    chips = n_lm // 2
    bits = int(math.log2(chips))
    row_blocks = camera_hessian.shape[0]
    extent = row_blocks * CB
    col_blocks = row_blocks * n_lm // n_cam
    turns = col_blocks * CB // (2 * LANES)
    pieces = 2 * turns
    group = col_blocks * CB // pieces
    columns = group * n_cam
    chunks = columns // CHUNK
    coded = extent + STRIP
    orders = [list(range(bits)), list(reversed(range(bits)))]
    lm, cam = lax.axis_index("lm"), lax.axis_index("cam")
    me = jnp.stack([lm // 2, lm % 2, cam]).astype(jnp.int32)

    live = jnp.arange(K, dtype=jnp.int32)[None, :] < counts[:, None]
    ids = jnp.where(live, visible_blocks, -1)

    def swap(value, bit):
        return lax.ppermute(value, "lm", [(i, i ^ (1 << bit)) for i in range(n_lm)])

    ids_other, cur_other, pan_other = swap(ids, 0), swap(curvature, 0), swap(panels, 0)
    wide = jnp.concatenate([camera_hessian, camera_hessian], axis=-1)

    def piece_block(which):
        return lambda step: (0, 0, jnp.clip(step - which * chunks, 0, chunks - 1))

    sends, keeps = [], []
    for turn in range(turns):
        outs = pl.pallas_call(
            functools.partial(
                partial_kernel,
                (
                    turn,
                    group // CB,
                    pieces,
                    n_cam,
                    row_blocks,
                    chips,
                    orders,
                    tiles,
                    chunks,
                ),
            ),
            grid=(2 * chunks,),
            in_specs=[SMEM] * 3 + [VMEM] * 4,
            out_specs=[pl.BlockSpec((chips // 2, coded, CHUNK), piece_block(w)) for w in range(2)]
            + [pl.BlockSpec((chips // 2, extent, CHUNK), piece_block(w)) for w in range(2)],
            out_shape=[jax.ShapeDtypeStruct((chips // 2, coded, columns), jnp.int16)] * 2
            + [jax.ShapeDtypeStruct((chips // 2, extent, columns), jnp.float32)] * 2,
            scratch_shapes=[
                pltpu.VMEM((2 * tiles, K * CB, 2 * WIDTH), jnp.bfloat16),
                pltpu.VMEM((2, CHUNK, 2 * WIDTH), jnp.bfloat16),
                pltpu.VMEM((chips * extent + CB, CHUNK), jnp.float32),
                pltpu.SMEM((2 * tiles, 2 * chunks * QUAD), jnp.int32),
                pltpu.SMEM((2 * tiles, K + QUAD), jnp.int32),
                pltpu.SMEM((2 * tiles,), jnp.int32),
                pltpu.SMEM((2 * tiles, 2 * chunks), jnp.int32),
            ],
            compiler_params=PARAMS,
            name="partial",
        )(me, ids, ids_other, panels, pan_other, curvature, cur_other)
        sends.append(list(outs[:2]))
        keeps.append(outs[2:])

    came = [[[], []] for _ in range(turns)]
    result = None
    for turn in range(turns):
        for stage in range(bits):
            for piece in range(2):
                came[turn][piece].append(swap(sends[turn][piece], orders[piece][stage] + 1))
            size = chips >> (stage + 1)
            if size == 1:
                break
            for piece in range(2):
                arrays = [keeps[turn][piece]] + came[turn][piece]

                def later(half, block, size=size):
                    return (size // 2 + half, 0, block)

                sends[turn][piece] = pl.pallas_call(
                    functools.partial(relay_kernel, row_blocks),
                    grid=(size // 2, columns // CHUNK),
                    in_specs=[pl.BlockSpec((1, extent, CHUNK), later)]
                    + [pl.BlockSpec((1, coded, CHUNK), later)] * (len(arrays) - 1),
                    out_specs=pl.BlockSpec((1, coded, CHUNK), lambda half, block: (half, 0, block)),
                    out_shape=jax.ShapeDtypeStruct((size // 2, coded, columns), jnp.int16),
                    compiler_params=PARAMS,
                    name="relay",
                )(*arrays)

        near = [array for piece in range(2) for array in [keeps[turn][piece]] + came[turn][piece]]
        arrays = len(near) // 2

        def first(width):
            return [
                pl.BlockSpec((1, coded if pos % arrays else extent, width), lambda step: (0, 0, 0))
                for pos in range(2 * arrays)
            ]

        crossed = pl.pallas_call(
            functools.partial(cross_kernel, row_blocks, group, arrays),
            grid=(1,),
            in_specs=first(columns),
            out_specs=[pl.BlockSpec((2, coded, group), lambda step: (0, 0, 0))] * (n_cam - 1),
            out_shape=[jax.ShapeDtypeStruct((2, coded, group), jnp.int16)] * (n_cam - 1),
            compiler_params=PARAMS,
            name="cross",
        )(*near)
        far = [
            lax.ppermute(value, "cam", [(i, i ^ (pos + 1)) for i in range(n_cam)])
            for pos, value in enumerate(crossed)
        ]
        before = [] if result is None else [result]
        result = pl.pallas_call(
            functools.partial(finish_kernel, (turn, row_blocks, col_blocks, arrays, n_cam - 1)),
            grid=(1,),
            in_specs=[SMEM, VMEM]
            + first(group)
            + [pl.BlockSpec((2, coded, group), lambda step: (0, 0, 0))] * (n_cam - 1)
            + [pl.BlockSpec(memory_space=pl.ANY)] * len(before),
            out_specs=pl.BlockSpec((extent, 2 * group), lambda step, turn=turn: (0, turn)),
            out_shape=jax.ShapeDtypeStruct((extent, col_blocks * CB), jnp.float32),
            input_output_aliases={2 + len(near) + len(far): 0} if before else {},
            compiler_params=PARAMS,
            name="finish",
        )(me, wide, *near, *far, *before)
    return result


def solution(mesh):
    return jax.shard_map(
        body,
        mesh=mesh,
        in_specs=(
            P(("lm", "cam"), None, None, None),
            P(None, None, ("lm", "cam")),
            P(("lm", "cam"), None),
            P(("lm", "cam")),
            P("lm", None, None),
        ),
        out_specs=P("lm", "cam"),
        check_vma=False,
    )
```

```python
import functools
import math

import jax
import jax.numpy as jnp
from jax import lax
from jax.experimental import pallas as pl
from jax.experimental.pallas import tpu as pltpu
from jax.sharding import PartitionSpec as P

CB = 64
LMB = 128
K = 16
WIDTH = 3 * LMB
STRIP = 16
LANES = 128
CHUNK = 512
VMEM = pl.BlockSpec(memory_space=pltpu.VMEM)
SMEM = pl.BlockSpec(memory_space=pltpu.SMEM)
PARAMS = pltpu.CompilerParams(vmem_limit_bytes=32 * 1024 * 1024)


def invert_rows(cur_ref, start):
    lanes = slice(start, start + LMB)
    entry = [[cur_ref[row, col : col + 1, lanes] for col in range(3)] for row in range(3)]
    cofactor = [
        [
            entry[(row + 1) % 3][(col + 1) % 3] * entry[(row + 2) % 3][(col + 2) % 3]
            - entry[(row + 1) % 3][(col + 2) % 3] * entry[(row + 2) % 3][(col + 1) % 3]
            for col in range(3)
        ]
        for row in range(3)
    ]
    determ = (
        entry[0][0] * cofactor[0][0] + entry[0][1] * cofactor[0][1] + entry[0][2] * cofactor[0][2]
    )
    return [[cofactor[col][row] / determ for col in range(3)] for row in range(3)]


def encode(dst, lanes, parts):
    blocks = len(parts)
    row = lax.broadcasted_iota(jnp.int32, (8, LANES), 0)
    tops = jnp.full((8, LANES), 2.0**-100, jnp.float32)
    for block, part in enumerate(parts):
        top = jnp.max(jnp.abs(part), axis=0, keepdims=True)
        tops = jnp.where(row == block, jnp.maximum(top, tops), tops)
    power = jnp.ceil(jnp.log2(tops) - 14.99)
    inverse = jnp.exp2(-power)
    for block, part in enumerate(parts):
        coded = jnp.round(part * inverse[block : block + 1])
        dst[pl.ds(block * CB, CB), lanes] = coded.astype(jnp.int32).astype(jnp.int16)
    strip = jnp.concatenate([power, power], axis=0).astype(jnp.int32)
    dst[pl.ds(blocks * CB, STRIP), lanes] = strip.astype(jnp.int16)


def decode(src, lanes, blocks):
    strip = src[pl.ds(blocks * CB, STRIP), lanes].astype(jnp.int32).astype(jnp.float32)
    scale = jnp.exp2(strip)
    return [
        src[pl.ds(block * CB, CB), lanes].astype(jnp.int32).astype(jnp.float32)
        * scale[block : block + 1]
        for block in range(blocks)
    ]


def gathered(keep, came, lanes, blocks):
    parts = [keep[pl.ds(block * CB, CB), lanes] for block in range(blocks)]
    for src in came:
        parts = [part + other for part, other in zip(parts, decode(src, lanes, blocks))]
    return parts


def spot_of(index, order):
    bits = len(order)
    return sum(((index >> (bits - 1 - pos)) & 1) << bit for pos, bit in enumerate(order))


def invert_kernel(cur_ref, out_ref):
    for start in range(0, cur_ref.shape[2], LMB):
        table = invert_rows(cur_ref, start)
        for row in range(3):
            for col in range(3):
                out_ref[row, col : col + 1, start : start + LMB] = table[row][col]


def piece_kernel(plan, table, pan_a, pan_b, inv_a, inv_b, out, left, right, *scratch):
    sending, base, order, total, row_blocks, halves, tiles, chunks = plan
    acc = scratch[0] if sending else out
    acc[...] = jnp.zeros_like(acc)
    spots = [spot_of(half + (halves if sending else 0), order) for half in range(halves)]
    for tile in range(2 * tiles):
        pan, inv = (pan_a, inv_a) if tile < tiles else (pan_b, inv_b)
        here = tile % tiles
        slots = [
            [table[tile, total + spot * row_blocks + block] for block in range(row_blocks)]
            for spot in spots
        ]
        used = [functools.reduce(jnp.maximum, group) for group in slots]

        @pl.when(functools.reduce(jnp.maximum, used) >= 0)
        def one_tile():
            inverse = [
                [inv[c, q : q + 1, here * LMB : (here + 1) * LMB] for q in range(3)]
                for c in range(3)
            ]
            for half in range(halves):
                for block, slot in enumerate(slots[half]):
                    lines = slice(block * CB, (block + 1) * CB)

                    @pl.when(slot >= 0)
                    def form():
                        wide = pan[here, slot].astype(jnp.float32)
                        split = [wide[:, c * LMB : (c + 1) * LMB] for c in range(3)]
                        for q in range(3):
                            formed = (
                                split[0] * inverse[0][q]
                                + split[1] * inverse[1][q]
                                + split[2] * inverse[2][q]
                            )
                            high = formed.astype(jnp.bfloat16)
                            low = (formed - high.astype(jnp.float32)).astype(jnp.bfloat16)
                            at = q * LMB
                            left[half, lines, at : at + LMB] = high
                            left[half, lines, WIDTH + at : WIDTH + at + LMB] = low

                    @pl.when((slot < 0) & (used[half] >= 0))
                    def no_row():
                        left[half, lines, :] = jnp.zeros((CB, 2 * WIDTH), jnp.bfloat16)

            def one_chunk(chunk, carry):
                for place in range(CHUNK // CB):
                    slot = table[tile, base + chunk * (CHUNK // CB) + place]
                    lines = slice(place * CB, (place + 1) * CB)

                    @pl.when(slot >= 0)
                    def fill():
                        panel = pan[here, slot]
                        right[lines, :WIDTH] = panel
                        right[lines, WIDTH:] = panel

                    @pl.when(slot < 0)
                    def no_column():
                        right[lines, :] = jnp.zeros((CB, 2 * WIDTH), jnp.bfloat16)

                lanes = pl.ds(pl.multiple_of(chunk * CHUNK, CHUNK), CHUNK)
                for half in range(halves):

                    @pl.when(used[half] >= 0)
                    def add():
                        acc[half, :, lanes] += lax.dot_general(
                            left[half],
                            right[...],
                            (((1,), (1,)), ((), ())),
                            preferred_element_type=jnp.float32,
                        )

                return carry

            lax.fori_loop(0, chunks, one_chunk, 0)

    if sending:
        for half in range(halves):
            for start in range(0, out.shape[2], LANES):
                lanes = pl.ds(start, LANES)
                parts = [
                    acc[half, pl.ds(block * CB, CB), lanes] for block in range(row_blocks)
                ]
                encode(out.at[half], lanes, parts)


def relay_kernel(row_blocks, keep_ref, *rest):
    dst = rest[-1].at[0]
    for start in range(0, dst.shape[1], LANES):
        lanes = pl.ds(start, LANES)
        came = [ref.at[0] for ref in rest[:-1]]
        encode(dst, lanes, gathered(keep_ref.at[0], came, lanes, row_blocks))


def cross_kernel(row_blocks, group, arrays, *rest):
    dsts = rest[2 * arrays :]
    for piece in range(2):
        keep = rest[piece * arrays].at[0]
        came = [ref.at[0] for ref in rest[piece * arrays + 1 : (piece + 1) * arrays]]
        for other, dst in enumerate(dsts):
            for start in range(0, group, LANES):
                lanes = pl.ds((other + 1) * group + start, LANES)
                parts = gathered(keep, came, lanes, row_blocks)
                encode(dst.at[piece], pl.ds(start, LANES), parts)


def base_kernel(plan, me_ref, wide_ref, *rest):
    turn, row_blocks, col_blocks, arrays = plan
    out_ref = rest[-1]
    group = out_ref.shape[1] // 2
    first_row = (me_ref[0] * 2 + me_ref[1]) * row_blocks
    first_col = me_ref[2] * col_blocks
    lane = lax.broadcasted_iota(jnp.int32, (CB, LANES), 1) // CB
    for piece in range(2):
        keep = rest[piece * arrays].at[0]
        came = [ref.at[0] for ref in rest[piece * arrays + 1 : (piece + 1) * arrays]]
        for start in range(0, group, LANES):
            parts = gathered(keep, came, pl.ds(start, LANES), row_blocks)
            base = first_col + ((2 * turn + piece) * group + start) // CB
            for block in range(row_blocks):
                wide = jnp.where(base + lane == first_row + block, wide_ref[block], 0.0)
                out_ref[pl.ds(block * CB, CB), pl.ds(piece * group + start, LANES)] = (
                    wide - parts[block]
                )


def finish_kernel(row_blocks, far, base_ref, *rest):
    out_ref = rest[-1]
    group = out_ref.shape[1] // 2
    for piece in range(2):
        came = [ref.at[piece] for ref in rest[:far]]
        for start in range(0, group, LANES):
            total = [0.0] * row_blocks
            for src in came:
                parts = decode(src, pl.ds(start, LANES), row_blocks)
                total = [left + right for left, right in zip(total, parts)]
            lanes = pl.ds(piece * group + start, LANES)
            for block in range(row_blocks):
                lines = pl.ds(block * CB, CB)
                out_ref[lines, lanes] = base_ref[lines, lanes] - total[block]


def body(panels, curvature, visible_blocks, counts, camera_hessian):
    tiles = panels.shape[0]
    n_lm, n_cam = lax.axis_size("lm"), lax.axis_size("cam")
    chips = n_lm // 2
    bits = int(math.log2(chips))
    row_blocks = camera_hessian.shape[0]
    extent = row_blocks * CB
    col_blocks = row_blocks * n_lm // n_cam
    turns = col_blocks * CB // (2 * LANES)
    pieces = 2 * turns
    group = col_blocks * CB // pieces
    columns = group * n_cam
    total = row_blocks * n_lm
    coded = extent + STRIP
    orders = [list(range(bits)), list(reversed(range(bits)))]
    lm, cam = lax.axis_index("lm"), lax.axis_index("cam")
    me = jnp.stack([lm // 2, lm % 2, cam]).astype(jnp.int32)

    live = jnp.arange(K, dtype=jnp.int32)[None, :] < counts[:, None]
    ids = jnp.where(live, visible_blocks, -1)

    def swap(value, bit):
        return lax.ppermute(value, "lm", [(i, i ^ (1 << bit)) for i in range(n_lm)])

    inverse = pl.pallas_call(
        invert_kernel,
        in_specs=[VMEM],
        out_specs=VMEM,
        out_shape=jax.ShapeDtypeStruct(curvature.shape, jnp.float32),
        name="invert",
    )(curvature)
    pan_other, ids_other, inv_other = swap(panels, 0), swap(ids, 0), swap(inverse, 0)
    wide = jnp.concatenate([camera_hessian, camera_hessian], axis=-1)

    both = jnp.concatenate([ids, ids_other], axis=0)
    per = group // CB
    inner = both % col_blocks
    spot = ((inner // per) * n_cam + ((both // col_blocks) ^ cam)) * per + inner % per
    owner = both // row_blocks
    line = total + ((owner // 2) ^ (lm // 2)) * row_blocks + both % row_blocks
    spot = jnp.where(both >= 0, spot, -1)
    line = jnp.where((both >= 0) & (owner % 2 == lm % 2), line, -1)
    places = jnp.arange(total + chips * row_blocks, dtype=jnp.int32)
    found = (spot[:, :, None] == places) | (line[:, :, None] == places)
    table = jnp.max(jnp.where(found, jnp.arange(K, dtype=jnp.int32)[None, :, None], -1), axis=1)

    def piece_call(sending, turn, which, table):
        height, kind = (coded, jnp.int16) if sending else (extent, jnp.float32)
        plan = (
            sending,
            (2 * turn + which) * n_cam * per,
            orders[which],
            total,
            row_blocks,
            chips // 2,
            tiles,
            columns // CHUNK,
        )
        return pl.pallas_call(
            functools.partial(piece_kernel, plan),
            in_specs=[SMEM] + [VMEM] * 4,
            out_specs=VMEM,
            out_shape=jax.ShapeDtypeStruct((chips // 2, height, columns), kind),
            scratch_shapes=[
                pltpu.VMEM((chips // 2, extent, 2 * WIDTH), jnp.bfloat16),
                pltpu.VMEM((CHUNK, 2 * WIDTH), jnp.bfloat16),
            ]
            + [pltpu.VMEM((chips // 2, extent, columns), jnp.float32)] * sending,
            compiler_params=PARAMS,
            name="send" if sending else "keep",
        )(table, panels, pan_other, inverse, inv_other)

    sends = [[piece_call(True, turn, which, table) for which in range(2)] for turn in range(turns)]
    after = lax.optimization_barrier((table, sends))[0]
    keeps = [[piece_call(False, turn, which, after) for which in range(2)] for turn in range(turns)]

    came = [[[], []] for _ in range(turns)]
    result = None
    for turn in range(turns):
        for stage in range(bits):
            for piece in range(2):
                came[turn][piece].append(swap(sends[turn][piece], orders[piece][stage] + 1))
            size = chips >> (stage + 1)
            if size == 1:
                break
            for piece in range(2):
                arrays = [keeps[turn][piece]] + came[turn][piece]

                def later(half, block, size=size):
                    return (size // 2 + half, 0, block)

                sends[turn][piece] = pl.pallas_call(
                    functools.partial(relay_kernel, row_blocks),
                    grid=(size // 2, columns // CHUNK),
                    in_specs=[pl.BlockSpec((1, extent, CHUNK), later)]
                    + [pl.BlockSpec((1, coded, CHUNK), later)] * (len(arrays) - 1),
                    out_specs=pl.BlockSpec((1, coded, CHUNK), lambda half, block: (half, 0, block)),
                    out_shape=jax.ShapeDtypeStruct((size // 2, coded, columns), jnp.int16),
                    compiler_params=PARAMS,
                    name="relay",
                )(*arrays)

        near = [array for piece in range(2) for array in [keeps[turn][piece]] + came[turn][piece]]
        arrays = len(near) // 2

        def first(width):
            return [
                pl.BlockSpec((1, coded if pos % arrays else extent, width), lambda step: (0, 0, 0))
                for pos in range(2 * arrays)
            ]

        crossed = pl.pallas_call(
            functools.partial(cross_kernel, row_blocks, group, arrays),
            grid=(1,),
            in_specs=first(columns),
            out_specs=[pl.BlockSpec((2, coded, group), lambda step: (0, 0, 0))] * (n_cam - 1),
            out_shape=[jax.ShapeDtypeStruct((2, coded, group), jnp.int16)] * (n_cam - 1),
            compiler_params=PARAMS,
            name="cross",
        )(*near)
        far = [
            lax.ppermute(value, "cam", [(i, i ^ (pos + 1)) for i in range(n_cam)])
            for pos, value in enumerate(crossed)
        ]
        base = pl.pallas_call(
            functools.partial(base_kernel, (turn, row_blocks, col_blocks, arrays)),
            grid=(1,),
            in_specs=[SMEM, VMEM] + first(group),
            out_specs=pl.BlockSpec((extent, 2 * group), lambda step: (0, 0)),
            out_shape=jax.ShapeDtypeStruct((extent, 2 * group), jnp.float32),
            compiler_params=PARAMS,
            name="base",
        )(me, wide, *near)
        before = [] if result is None else [result]
        result = pl.pallas_call(
            functools.partial(finish_kernel, row_blocks, n_cam - 1),
            grid=(1,),
            in_specs=[VMEM] * n_cam + [pl.BlockSpec(memory_space=pl.ANY)] * len(before),
            out_specs=pl.BlockSpec((extent, 2 * group), lambda step, turn=turn: (0, turn)),
            out_shape=jax.ShapeDtypeStruct((extent, col_blocks * CB), jnp.float32),
            input_output_aliases={n_cam: 0} if before else {},
            compiler_params=PARAMS,
            name="finish",
        )(base, *far, *before)
    return result


def solution(mesh):
    return jax.shard_map(
        body,
        mesh=mesh,
        in_specs=(
            P(("lm", "cam"), None, None, None),
            P(None, None, ("lm", "cam")),
            P(("lm", "cam"), None),
            P(("lm", "cam")),
            P("lm", None, None),
        ),
        out_specs=P("lm", "cam"),
        check_vma=False,
    )
```

```python
import functools
import math

import jax
import jax.numpy as jnp
from jax import lax
from jax.experimental import pallas as pl
from jax.experimental.pallas import tpu as pltpu
from jax.sharding import PartitionSpec as P

CB = 64
LMB = 128
K = 16
WIDTH = 3 * LMB
STRIP = 16
LANES = 128
CHUNK = 512
VMEM = pl.BlockSpec(memory_space=pltpu.VMEM)
SMEM = pl.BlockSpec(memory_space=pltpu.SMEM)
PARAMS = pltpu.CompilerParams(vmem_limit_bytes=32 * 1024 * 1024)


def invert_rows(cur_ref, start):
    lanes = pl.ds(start, LMB)
    entry = [[cur_ref[row, col : col + 1, lanes] for col in range(3)] for row in range(3)]
    cofactor = [
        [
            entry[(row + 1) % 3][(col + 1) % 3] * entry[(row + 2) % 3][(col + 2) % 3]
            - entry[(row + 1) % 3][(col + 2) % 3] * entry[(row + 2) % 3][(col + 1) % 3]
            for col in range(3)
        ]
        for row in range(3)
    ]
    determ = (
        entry[0][0] * cofactor[0][0] + entry[0][1] * cofactor[0][1] + entry[0][2] * cofactor[0][2]
    )
    return [[cofactor[col][row] / determ for col in range(3)] for row in range(3)]


def encode(dst, lanes, parts):
    blocks = len(parts)
    row = lax.broadcasted_iota(jnp.int32, (8, LANES), 0)
    tops = jnp.full((8, LANES), 2.0**-100, jnp.float32)
    for block, part in enumerate(parts):
        top = jnp.max(jnp.abs(part), axis=0, keepdims=True)
        tops = jnp.where(row == block, jnp.maximum(top, tops), tops)
    power = jnp.ceil(jnp.log2(tops) - 14.99)
    inverse = jnp.exp2(-power)
    for block, part in enumerate(parts):
        coded = jnp.round(part * inverse[block : block + 1])
        dst[pl.ds(block * CB, CB), lanes] = coded.astype(jnp.int32).astype(jnp.int16)
    strip = jnp.concatenate([power, power], axis=0).astype(jnp.int32)
    dst[pl.ds(blocks * CB, STRIP), lanes] = strip.astype(jnp.int16)


def decode(src, lanes, blocks):
    strip = src[pl.ds(blocks * CB, STRIP), lanes].astype(jnp.int32).astype(jnp.float32)
    scale = jnp.exp2(strip)
    return [
        src[pl.ds(block * CB, CB), lanes].astype(jnp.int32).astype(jnp.float32)
        * scale[block : block + 1]
        for block in range(blocks)
    ]


def gathered(keep, came, lanes, blocks):
    parts = [keep[pl.ds(block * CB, CB), lanes] for block in range(blocks)]
    for src in came:
        parts = [part + other for part, other in zip(parts, decode(src, lanes, blocks))]
    return parts


def spot_of(index, order):
    bits = len(order)
    return sum(((index >> (bits - 1 - pos)) & 1) << bit for pos, bit in enumerate(order))


def form_kernel(total, table, pan, cur, rows):
    tiles, height, _ = rows.shape

    def one_tile(tile, carry):
        inverse = invert_rows(cur, pl.multiple_of(tile * LMB, LMB))

        def one_place(place, carry):
            slot = table[tile, total + place]
            lines = pl.ds(pl.multiple_of(place * CB, CB), CB)

            @pl.when(slot >= 0)
            def form():
                wide = pan[tile, slot].astype(jnp.float32)
                split = [wide[:, c * LMB : (c + 1) * LMB] for c in range(3)]
                for q in range(3):
                    formed = (
                        split[0] * inverse[0][q]
                        + split[1] * inverse[1][q]
                        + split[2] * inverse[2][q]
                    )
                    high = formed.astype(jnp.bfloat16)
                    low = (formed - high.astype(jnp.float32)).astype(jnp.bfloat16)
                    at = q * LMB
                    rows[tile, lines, at : at + LMB] = high
                    rows[tile, lines, WIDTH + at : WIDTH + at + LMB] = low

            @pl.when(slot < 0)
            def blank():
                rows[tile, lines, :] = jnp.zeros((CB, 2 * WIDTH), jnp.bfloat16)

            return carry

        return lax.fori_loop(0, height // CB, one_place, carry)

    lax.fori_loop(0, tiles, one_tile, 0)


def piece_kernel(plan, table_a, table_b, pan_a, pan_b, rows_a, rows_b, out, right, *scratch):
    sending, base, order, total, row_blocks, halves, tiles, chunks = plan
    acc = scratch[0] if sending else out
    acc[...] = jnp.zeros_like(acc)
    spots = [spot_of(half + (halves if sending else 0), order) for half in range(halves)]
    extent = row_blocks * CB
    for table, pan, rows in ((table_a, pan_a, rows_a), (table_b, pan_b, rows_b)):

        def one_tile(tile, carry):
            used = [
                functools.reduce(
                    jnp.maximum,
                    [table[tile, total + spot * row_blocks + block] for block in range(row_blocks)],
                )
                for spot in spots
            ]

            @pl.when(functools.reduce(jnp.maximum, used) >= 0)
            def some():
                def one_chunk(chunk, carry):
                    def one_place(place, carry):
                        slot = table[tile, base + chunk * (CHUNK // CB) + place]
                        lines = pl.ds(pl.multiple_of(place * CB, CB), CB)

                        @pl.when(slot >= 0)
                        def fill():
                            panel = pan[tile, slot]
                            right[lines, :WIDTH] = panel
                            right[lines, WIDTH:] = panel

                        @pl.when(slot < 0)
                        def blank():
                            right[lines, :] = jnp.zeros((CB, 2 * WIDTH), jnp.bfloat16)

                        return carry

                    lax.fori_loop(0, CHUNK // CB, one_place, 0)
                    lanes = pl.ds(pl.multiple_of(chunk * CHUNK, CHUNK), CHUNK)
                    for half, spot in enumerate(spots):

                        @pl.when(used[half] >= 0)
                        def add():
                            acc[half, :, lanes] += lax.dot_general(
                                rows[tile, spot * extent : (spot + 1) * extent, :],
                                right[...],
                                (((1,), (1,)), ((), ())),
                                preferred_element_type=jnp.float32,
                            )

                    return carry

                lax.fori_loop(0, chunks, one_chunk, 0)

            return carry

        lax.fori_loop(0, tiles, one_tile, 0)

    if sending:

        def code(start, carry):
            lanes = pl.ds(pl.multiple_of(start * LANES, LANES), LANES)
            for half in range(halves):
                parts = [acc[half, pl.ds(block * CB, CB), lanes] for block in range(row_blocks)]
                encode(out.at[half], lanes, parts)
            return carry

        lax.fori_loop(0, out.shape[2] // LANES, code, 0)


def relay_kernel(row_blocks, keep_ref, *rest):
    dst = rest[-1].at[0]

    def code(start, carry):
        lanes = pl.ds(pl.multiple_of(start * LANES, LANES), LANES)
        came = [ref.at[0] for ref in rest[:-1]]
        encode(dst, lanes, gathered(keep_ref.at[0], came, lanes, row_blocks))
        return carry

    lax.fori_loop(0, dst.shape[1] // LANES, code, 0)


def cross_kernel(row_blocks, group, arrays, *rest):
    dsts = rest[2 * arrays :]
    for piece in range(2):
        keep = rest[piece * arrays].at[0]
        came = [ref.at[0] for ref in rest[piece * arrays + 1 : (piece + 1) * arrays]]
        for other, dst in enumerate(dsts):
            for start in range(0, group, LANES):
                lanes = pl.ds((other + 1) * group + start, LANES)
                parts = gathered(keep, came, lanes, row_blocks)
                encode(dst.at[piece], pl.ds(start, LANES), parts)


def base_kernel(plan, me_ref, wide_ref, *rest):
    turn, row_blocks, col_blocks, arrays = plan
    out_ref = rest[-1]
    group = out_ref.shape[1] // 2
    first_row = (me_ref[0] * 2 + me_ref[1]) * row_blocks
    first_col = me_ref[2] * col_blocks
    lane = lax.broadcasted_iota(jnp.int32, (CB, LANES), 1) // CB
    for piece in range(2):
        keep = rest[piece * arrays].at[0]
        came = [ref.at[0] for ref in rest[piece * arrays + 1 : (piece + 1) * arrays]]
        for start in range(0, group, LANES):
            parts = gathered(keep, came, pl.ds(start, LANES), row_blocks)
            base = first_col + ((2 * turn + piece) * group + start) // CB
            for block in range(row_blocks):
                wide = jnp.where(base + lane == first_row + block, wide_ref[block], 0.0)
                out_ref[pl.ds(block * CB, CB), pl.ds(piece * group + start, LANES)] = (
                    wide - parts[block]
                )


def finish_kernel(row_blocks, far, base_ref, *rest):
    out_ref = rest[-1]
    group = out_ref.shape[1] // 2
    for piece in range(2):
        came = [ref.at[piece] for ref in rest[:far]]
        for start in range(0, group, LANES):
            total = [0.0] * row_blocks
            for src in came:
                parts = decode(src, pl.ds(start, LANES), row_blocks)
                total = [left + right for left, right in zip(total, parts)]
            lanes = pl.ds(piece * group + start, LANES)
            for block in range(row_blocks):
                lines = pl.ds(block * CB, CB)
                out_ref[lines, lanes] = base_ref[lines, lanes] - total[block]


def body(panels, curvature, visible_blocks, counts, camera_hessian):
    tiles = panels.shape[0]
    n_lm, n_cam = lax.axis_size("lm"), lax.axis_size("cam")
    chips = n_lm // 2
    bits = int(math.log2(chips))
    row_blocks = camera_hessian.shape[0]
    extent = row_blocks * CB
    col_blocks = row_blocks * n_lm // n_cam
    turns = col_blocks * CB // (2 * LANES)
    pieces = 2 * turns
    group = col_blocks * CB // pieces
    columns = group * n_cam
    total = row_blocks * n_lm
    coded = extent + STRIP
    orders = [list(range(bits)), list(reversed(range(bits)))]
    lm, cam = lax.axis_index("lm"), lax.axis_index("cam")
    me = jnp.stack([lm // 2, lm % 2, cam]).astype(jnp.int32)

    live = jnp.arange(K, dtype=jnp.int32)[None, :] < counts[:, None]
    ids = jnp.where(live, visible_blocks, -1)

    def swap(value, bit):
        return lax.ppermute(value, "lm", [(i, i ^ (1 << bit)) for i in range(n_lm)])

    pan_other, cur_other, ids_other = swap(panels, 0), swap(curvature, 0), swap(ids, 0)
    wide = jnp.concatenate([camera_hessian, camera_hessian], axis=-1)
    per = group // CB
    slots = jnp.arange(K, dtype=jnp.int32)[None, :, None]
    places = jnp.arange(total + chips * row_blocks, dtype=jnp.int32)

    def table_of(ids):
        inner = ids % col_blocks
        spot = ((inner // per) * n_cam + ((ids // col_blocks) ^ cam)) * per + inner % per
        owner = ids // row_blocks
        line = total + ((owner // 2) ^ (lm // 2)) * row_blocks + ids % row_blocks
        spot = jnp.where(ids >= 0, spot, -1)
        line = jnp.where((ids >= 0) & (owner % 2 == lm % 2), line, -1)
        found = (spot[:, :, None] == places) | (line[:, :, None] == places)
        return jnp.max(jnp.where(found, slots, -1), axis=1)

    def form_call(table, panels, curvature):
        return pl.pallas_call(
            functools.partial(form_kernel, total),
            in_specs=[SMEM, VMEM, VMEM],
            out_specs=VMEM,
            out_shape=jax.ShapeDtypeStruct((tiles, chips * extent, 2 * WIDTH), jnp.bfloat16),
            compiler_params=PARAMS,
            name="form",
        )(table, panels, curvature)

    tables = (table_of(ids), table_of(ids_other))
    rows = (
        form_call(tables[0], panels, curvature),
        form_call(tables[1], pan_other, cur_other),
    )

    def piece_call(sending, turn, which, tables):
        height, kind = (coded, jnp.int16) if sending else (extent, jnp.float32)
        plan = (
            sending,
            (2 * turn + which) * n_cam * per,
            orders[which],
            total,
            row_blocks,
            chips // 2,
            tiles,
            columns // CHUNK,
        )
        return pl.pallas_call(
            functools.partial(piece_kernel, plan),
            in_specs=[SMEM] * 2 + [VMEM] * 4,
            out_specs=VMEM,
            out_shape=jax.ShapeDtypeStruct((chips // 2, height, columns), kind),
            scratch_shapes=[pltpu.VMEM((CHUNK, 2 * WIDTH), jnp.bfloat16)]
            + [pltpu.VMEM((chips // 2, extent, columns), jnp.float32)] * sending,
            compiler_params=PARAMS,
            name="send" if sending else "keep",
        )(*tables, panels, pan_other, *rows)

    sends, keeps = [], []
    for turn in range(turns):
        for sending, made in ((True, sends), (False, keeps)):
            made.append([piece_call(sending, turn, which, tables) for which in range(2)])
            tables = lax.optimization_barrier((tables, made[-1]))[0]

    came = [[[], []] for _ in range(turns)]
    result = None
    for turn in range(turns):
        if turn:
            first_came = [arrays[0] for arrays in came[turn - 1]]
            sends[turn] = lax.optimization_barrier((sends[turn], first_came))[0]
        for stage in range(bits):
            for piece in range(2):
                came[turn][piece].append(swap(sends[turn][piece], orders[piece][stage] + 1))
            size = chips >> (stage + 1)
            if size == 1:
                break
            for piece in range(2):
                arrays = [keeps[turn][piece]] + came[turn][piece]

                def later(half, block, size=size):
                    return (size // 2 + half, 0, block)

                sends[turn][piece] = pl.pallas_call(
                    functools.partial(relay_kernel, row_blocks),
                    grid=(size // 2, columns // CHUNK),
                    in_specs=[pl.BlockSpec((1, extent, CHUNK), later)]
                    + [pl.BlockSpec((1, coded, CHUNK), later)] * (len(arrays) - 1),
                    out_specs=pl.BlockSpec((1, coded, CHUNK), lambda half, block: (half, 0, block)),
                    out_shape=jax.ShapeDtypeStruct((size // 2, coded, columns), jnp.int16),
                    compiler_params=PARAMS,
                    name="relay",
                )(*arrays)

        near = [array for piece in range(2) for array in [keeps[turn][piece]] + came[turn][piece]]
        arrays = len(near) // 2

        def first(width):
            return [
                pl.BlockSpec((1, coded if pos % arrays else extent, width), lambda step: (0, 0, 0))
                for pos in range(2 * arrays)
            ]

        crossed = pl.pallas_call(
            functools.partial(cross_kernel, row_blocks, group, arrays),
            grid=(1,),
            in_specs=first(columns),
            out_specs=[pl.BlockSpec((2, coded, group), lambda step: (0, 0, 0))] * (n_cam - 1),
            out_shape=[jax.ShapeDtypeStruct((2, coded, group), jnp.int16)] * (n_cam - 1),
            compiler_params=PARAMS,
            name="cross",
        )(*near)
        far = [
            lax.ppermute(value, "cam", [(i, i ^ (pos + 1)) for i in range(n_cam)])
            for pos, value in enumerate(crossed)
        ]
        base = pl.pallas_call(
            functools.partial(base_kernel, (turn, row_blocks, col_blocks, arrays)),
            grid=(1,),
            in_specs=[SMEM, VMEM] + first(group),
            out_specs=pl.BlockSpec((extent, 2 * group), lambda step: (0, 0)),
            out_shape=jax.ShapeDtypeStruct((extent, 2 * group), jnp.float32),
            compiler_params=PARAMS,
            name="base",
        )(me, wide, *near)
        before = [] if result is None else [result]
        result = pl.pallas_call(
            functools.partial(finish_kernel, row_blocks, n_cam - 1),
            grid=(1,),
            in_specs=[VMEM] * n_cam + [pl.BlockSpec(memory_space=pl.ANY)] * len(before),
            out_specs=pl.BlockSpec((extent, 2 * group), lambda step, turn=turn: (0, turn)),
            out_shape=jax.ShapeDtypeStruct((extent, col_blocks * CB), jnp.float32),
            input_output_aliases={n_cam: 0} if before else {},
            compiler_params=PARAMS,
            name="finish",
        )(base, *far, *before)
    return result


def solution(mesh):
    return jax.shard_map(
        body,
        mesh=mesh,
        in_specs=(
            P(("lm", "cam"), None, None, None),
            P(None, None, ("lm", "cam")),
            P(("lm", "cam"), None),
            P(("lm", "cam")),
            P("lm", None, None),
        ),
        out_specs=P("lm", "cam"),
        check_vma=False,
    )
```

```python
import functools
import math

import jax
import jax.numpy as jnp
from jax import lax
from jax.experimental import pallas as pl
from jax.experimental.pallas import tpu as pltpu
from jax.sharding import PartitionSpec as P

CB = 64
LMB = 128
K = 16
WIDTH = 3 * LMB
STRIP = 16
LANES = 128
CHUNK = 512
VMEM = pl.BlockSpec(memory_space=pltpu.VMEM)
SMEM = pl.BlockSpec(memory_space=pltpu.SMEM)
PARAMS = pltpu.CompilerParams(vmem_limit_bytes=32 * 1024 * 1024)


def invert_rows(cur_ref, start):
    lanes = pl.ds(start, LMB)
    entry = [[cur_ref[row, col : col + 1, lanes] for col in range(3)] for row in range(3)]
    cofactor = [
        [
            entry[(row + 1) % 3][(col + 1) % 3] * entry[(row + 2) % 3][(col + 2) % 3]
            - entry[(row + 1) % 3][(col + 2) % 3] * entry[(row + 2) % 3][(col + 1) % 3]
            for col in range(3)
        ]
        for row in range(3)
    ]
    determ = (
        entry[0][0] * cofactor[0][0] + entry[0][1] * cofactor[0][1] + entry[0][2] * cofactor[0][2]
    )
    return [[cofactor[col][row] / determ for col in range(3)] for row in range(3)]


def encode(dst, lanes, parts):
    blocks = len(parts)
    row = lax.broadcasted_iota(jnp.int32, (8, LANES), 0)
    tops = jnp.full((8, LANES), 2.0**-100, jnp.float32)
    for block, part in enumerate(parts):
        top = jnp.max(jnp.abs(part), axis=0, keepdims=True)
        tops = jnp.where(row == block, jnp.maximum(top, tops), tops)
    power = jnp.ceil(jnp.log2(tops) - 14.99)
    inverse = jnp.exp2(-power)
    for block, part in enumerate(parts):
        coded = jnp.round(part * inverse[block : block + 1])
        dst[pl.ds(block * CB, CB), lanes] = coded.astype(jnp.int32).astype(jnp.int16)
    strip = jnp.concatenate([power, power], axis=0).astype(jnp.int32)
    dst[pl.ds(blocks * CB, STRIP), lanes] = strip.astype(jnp.int16)


def decode(src, lanes, blocks):
    strip = src[pl.ds(blocks * CB, STRIP), lanes].astype(jnp.int32).astype(jnp.float32)
    scale = jnp.exp2(strip)
    return [
        src[pl.ds(block * CB, CB), lanes].astype(jnp.int32).astype(jnp.float32)
        * scale[block : block + 1]
        for block in range(blocks)
    ]


def gathered(keep, came, lanes, blocks):
    parts = [keep[pl.ds(block * CB, CB), lanes] for block in range(blocks)]
    for src in came:
        parts = [part + other for part, other in zip(parts, decode(src, lanes, blocks))]
    return parts


def spot_of(index, order):
    bits = len(order)
    return sum(((index >> (bits - 1 - pos)) & 1) << bit for pos, bit in enumerate(order))


def form_tile(total, table, tile, pan, cur, rows):
    inverse = invert_rows(cur, tile * LMB)

    def one_place(place, carry):
        slot = table[tile, total + place]
        lines = pl.ds(pl.multiple_of(place * CB, CB), CB)

        @pl.when(slot >= 0)
        def form():
            wide = pan[tile, slot].astype(jnp.float32)
            split = [wide[:, c * LMB : (c + 1) * LMB] for c in range(3)]
            for q in range(3):
                formed = (
                    split[0] * inverse[0][q] + split[1] * inverse[1][q] + split[2] * inverse[2][q]
                )
                high = formed.astype(jnp.bfloat16)
                low = (formed - high.astype(jnp.float32)).astype(jnp.bfloat16)
                at = q * LMB
                rows[tile, lines, at : at + LMB] = high
                rows[tile, lines, WIDTH + at : WIDTH + at + LMB] = low

        @pl.when(slot < 0)
        def blank():
            rows[tile, lines, :] = jnp.zeros((CB, 2 * WIDTH), jnp.bfloat16)

        return carry

    lax.fori_loop(0, rows.shape[1] // CB, one_place, 0)


def form_own_kernel(total, table, pan_ref, cur_ref, rows, pan, cur, pan_sem, cur_sem):
    tiles = rows.shape[0]
    copies = [
        pltpu.make_async_copy(pan_ref.at[tile], pan.at[tile], pan_sem.at[tile])
        for tile in range(tiles)
    ]
    small = pltpu.make_async_copy(cur_ref, cur, cur_sem)
    small.start()
    for copy in copies:
        copy.start()
    small.wait()
    for tile, copy in enumerate(copies):
        copy.wait()
        form_tile(total, table, tile, pan, cur, rows)


def form_kernel(total, table, pan, cur, rows):
    for tile in range(rows.shape[0]):
        form_tile(total, table, tile, pan, cur, rows)


def round_kernel(plan, table_a, table_b, pan_a, pan_b, rows_a, rows_b, *rest):
    sending, bases, orders, total, row_blocks, halves, tiles, pairs = plan
    outs, right, pair_at, acc = rest[:2], rest[2], rest[3], rest[4]
    extent = row_blocks * CB
    columns = pairs * LANES
    for base, order, out in zip(bases, orders, outs):
        acc[...] = jnp.zeros_like(acc)
        spots = [spot_of(half + (halves if sending else 0), order) for half in range(halves)]
        for table, pan, rows in ((table_a, pan_a, rows_a), (table_b, pan_b, rows_b)):

            def one_tile(tile, carry):
                used = [
                    functools.reduce(
                        jnp.maximum,
                        [
                            table[tile, total + spot * row_blocks + block]
                            for block in range(row_blocks)
                        ],
                    )
                    for spot in spots
                ]

                @pl.when(functools.reduce(jnp.maximum, used) >= 0)
                def some():
                    def one_pair(pair, count):
                        slots = [table[tile, base + 2 * pair + side] for side in range(2)]
                        live = jnp.maximum(slots[0], slots[1]) >= 0

                        @pl.when(live)
                        def stage():
                            pair_at[count] = pair * LANES
                            for side, slot in enumerate(slots):
                                first = pl.multiple_of(count * LANES + side * CB, CB)
                                lines = pl.ds(first, CB)

                                @pl.when(slot >= 0)
                                def fill():
                                    panel = pan[tile, slot]
                                    right[lines, :WIDTH] = panel
                                    right[lines, WIDTH:] = panel

                                @pl.when(slot < 0)
                                def blank():
                                    right[lines, :] = jnp.zeros((CB, 2 * WIDTH), jnp.bfloat16)

                        return count + jnp.where(live, 1, 0)

                    count = lax.fori_loop(0, pairs, one_pair, jnp.int32(0))
                    pair_at[count] = columns

                    def one_dot(double, carry):
                        first = pl.multiple_of(double * 2 * LANES, 2 * LANES)
                        for half, spot in enumerate(spots):

                            @pl.when(used[half] >= 0)
                            def add():
                                result = lax.dot_general(
                                    rows[tile, spot * extent : (spot + 1) * extent, :],
                                    right[pl.ds(first, 2 * LANES), :],
                                    (((1,), (1,)), ((), ())),
                                    preferred_element_type=jnp.float32,
                                )
                                for side in range(2):
                                    at = pl.multiple_of(pair_at[2 * double + side], LANES)
                                    acc[half, :, pl.ds(at, LANES)] += result[
                                        :, side * LANES : (side + 1) * LANES
                                    ]

                        return carry

                    lax.fori_loop(0, (count + 1) // 2, one_dot, 0)

                return carry

            lax.fori_loop(0, tiles, one_tile, 0)

        def store(start, carry):
            lanes = pl.ds(pl.multiple_of(start * LANES, LANES), LANES)
            for half in range(halves):
                if sending:
                    parts = [acc[half, pl.ds(block * CB, CB), lanes] for block in range(row_blocks)]
                    encode(out.at[half], lanes, parts)
                else:
                    out[half, :, lanes] = acc[half, :, lanes]
            return carry

        lax.fori_loop(0, pairs, store, 0)


def relay_kernel(row_blocks, keep_ref, *rest):
    dst = rest[-1].at[0]

    def code(start, carry):
        lanes = pl.ds(pl.multiple_of(start * LANES, LANES), LANES)
        came = [ref.at[0] for ref in rest[:-1]]
        encode(dst, lanes, gathered(keep_ref.at[0], came, lanes, row_blocks))
        return carry

    lax.fori_loop(0, dst.shape[1] // LANES, code, 0)


def cross_kernel(row_blocks, group, arrays, *rest):
    dsts = rest[2 * arrays :]
    for piece in range(2):
        keep = rest[piece * arrays].at[0]
        came = [ref.at[0] for ref in rest[piece * arrays + 1 : (piece + 1) * arrays]]
        for other, dst in enumerate(dsts):
            for start in range(0, group, LANES):
                lanes = pl.ds((other + 1) * group + start, LANES)
                parts = gathered(keep, came, lanes, row_blocks)
                encode(dst.at[piece], pl.ds(start, LANES), parts)


def base_kernel(plan, me_ref, wide_ref, *rest):
    turn, row_blocks, col_blocks, arrays = plan
    out_ref = rest[-1]
    group = out_ref.shape[1] // 2
    first_row = (me_ref[0] * 2 + me_ref[1]) * row_blocks
    first_col = me_ref[2] * col_blocks
    lane = lax.broadcasted_iota(jnp.int32, (CB, LANES), 1) // CB
    for piece in range(2):
        keep = rest[piece * arrays].at[0]
        came = [ref.at[0] for ref in rest[piece * arrays + 1 : (piece + 1) * arrays]]
        for start in range(0, group, LANES):
            parts = gathered(keep, came, pl.ds(start, LANES), row_blocks)
            base = first_col + ((2 * turn + piece) * group + start) // CB
            for block in range(row_blocks):
                wide = jnp.where(base + lane == first_row + block, wide_ref[block], 0.0)
                out_ref[pl.ds(block * CB, CB), pl.ds(piece * group + start, LANES)] = (
                    wide - parts[block]
                )


def finish_kernel(row_blocks, far, base_ref, *rest):
    out_ref = rest[-1]
    group = out_ref.shape[1] // 2
    for piece in range(2):
        came = [ref.at[piece] for ref in rest[:far]]
        for start in range(0, group, LANES):
            total = [0.0] * row_blocks
            for src in came:
                parts = decode(src, pl.ds(start, LANES), row_blocks)
                total = [left + right for left, right in zip(total, parts)]
            lanes = pl.ds(piece * group + start, LANES)
            for block in range(row_blocks):
                lines = pl.ds(block * CB, CB)
                out_ref[lines, lanes] = base_ref[lines, lanes] - total[block]


def body(panels, curvature, visible_blocks, counts, camera_hessian):
    tiles = panels.shape[0]
    n_lm, n_cam = lax.axis_size("lm"), lax.axis_size("cam")
    chips = n_lm // 2
    bits = int(math.log2(chips))
    row_blocks = camera_hessian.shape[0]
    extent = row_blocks * CB
    col_blocks = row_blocks * n_lm // n_cam
    turns = col_blocks * CB // (2 * LANES)
    pieces = 2 * turns
    group = col_blocks * CB // pieces
    columns = group * n_cam
    total = row_blocks * n_lm
    coded = extent + STRIP
    orders = [list(range(bits)), list(reversed(range(bits)))]
    lm, cam = lax.axis_index("lm"), lax.axis_index("cam")
    me = jnp.stack([lm // 2, lm % 2, cam]).astype(jnp.int32)

    live = jnp.arange(K, dtype=jnp.int32)[None, :] < counts[:, None]
    ids = jnp.where(live, visible_blocks, -1)

    def swap(value, bit):
        return lax.ppermute(value, "lm", [(i, i ^ (1 << bit)) for i in range(n_lm)])

    pan_other, cur_other, ids_other = swap(panels, 0), swap(curvature, 0), swap(ids, 0)
    wide = jnp.concatenate([camera_hessian, camera_hessian], axis=-1)
    per = group // CB
    slots = jnp.arange(K, dtype=jnp.int32)[None, :, None]
    places = jnp.arange(total + chips * row_blocks, dtype=jnp.int32)

    def table_of(ids):
        inner = ids % col_blocks
        spot = ((inner // per) * n_cam + ((ids // col_blocks) ^ cam)) * per + inner % per
        owner = ids // row_blocks
        line = total + ((owner // 2) ^ (lm // 2)) * row_blocks + ids % row_blocks
        spot = jnp.where(ids >= 0, spot, -1)
        line = jnp.where((ids >= 0) & (owner % 2 == lm % 2), line, -1)
        found = (spot[:, :, None] == places) | (line[:, :, None] == places)
        return jnp.max(jnp.where(found, slots, -1), axis=1)

    table_a, table_b = table_of(ids), table_of(ids_other)
    formed = jax.ShapeDtypeStruct((tiles, chips * extent, 2 * WIDTH), jnp.bfloat16)
    whole = pl.BlockSpec(memory_space=pltpu.HBM)
    rows_a, pan_here = pl.pallas_call(
        functools.partial(form_own_kernel, total),
        in_specs=[SMEM, whole, whole],
        out_specs=[VMEM, VMEM],
        out_shape=[formed, jax.ShapeDtypeStruct(panels.shape, panels.dtype)],
        scratch_shapes=[
            pltpu.VMEM(curvature.shape, jnp.float32),
            pltpu.SemaphoreType.DMA((tiles,)),
            pltpu.SemaphoreType.DMA,
        ],
        compiler_params=PARAMS,
        name="form_own",
    )(table_a, panels, curvature)
    rows_b = pl.pallas_call(
        functools.partial(form_kernel, total),
        in_specs=[SMEM, VMEM, VMEM],
        out_specs=VMEM,
        out_shape=formed,
        compiler_params=PARAMS,
        name="form_other",
    )(table_b, pan_other, cur_other)

    def round_call(sending, turn, tables):
        height, kind = (coded, jnp.int16) if sending else (extent, jnp.float32)
        bases = [(2 * turn + which) * n_cam * per for which in range(2)]
        pairs = columns // LANES
        plan = (sending, bases, orders, total, row_blocks, chips // 2, tiles, pairs)
        return pl.pallas_call(
            functools.partial(round_kernel, plan),
            in_specs=[SMEM] * 2 + [VMEM] * 4,
            out_specs=[VMEM] * 2,
            out_shape=[jax.ShapeDtypeStruct((chips // 2, height, columns), kind)] * 2,
            scratch_shapes=[
                pltpu.VMEM((columns + LANES, 2 * WIDTH), jnp.bfloat16),
                pltpu.SMEM((pairs + 1,), jnp.int32),
                pltpu.VMEM((chips // 2, extent, columns + LANES), jnp.float32),
            ],
            compiler_params=PARAMS,
            name="send" if sending else "keep",
        )(*tables, pan_here, pan_other, rows_a, rows_b)

    tables = (table_a, table_b)
    sends, keeps = [], []
    for turn in range(turns):
        for sending, made in ((True, sends), (False, keeps)):
            made.append(list(round_call(sending, turn, tables)))
            tables = lax.optimization_barrier((tables, made[-1]))[0]

    came = [[[], []] for _ in range(turns)]
    result = None
    for turn in range(turns):
        if turn:
            first_came = [arrays[0] for arrays in came[turn - 1]]
            sends[turn] = lax.optimization_barrier((sends[turn], first_came))[0]
        for stage in range(bits):
            for piece in range(2):
                came[turn][piece].append(swap(sends[turn][piece], orders[piece][stage] + 1))
            size = chips >> (stage + 1)
            if size == 1:
                break
            for piece in range(2):
                arrays = [keeps[turn][piece]] + came[turn][piece]

                def later(half, block, size=size):
                    return (size // 2 + half, 0, block)

                sends[turn][piece] = pl.pallas_call(
                    functools.partial(relay_kernel, row_blocks),
                    grid=(size // 2, columns // CHUNK),
                    in_specs=[pl.BlockSpec((1, extent, CHUNK), later)]
                    + [pl.BlockSpec((1, coded, CHUNK), later)] * (len(arrays) - 1),
                    out_specs=pl.BlockSpec((1, coded, CHUNK), lambda half, block: (half, 0, block)),
                    out_shape=jax.ShapeDtypeStruct((size // 2, coded, columns), jnp.int16),
                    compiler_params=PARAMS,
                    name="relay",
                )(*arrays)

        near = [array for piece in range(2) for array in [keeps[turn][piece]] + came[turn][piece]]
        arrays = len(near) // 2

        def first(width):
            return [
                pl.BlockSpec((1, coded if pos % arrays else extent, width), lambda step: (0, 0, 0))
                for pos in range(2 * arrays)
            ]

        crossed = pl.pallas_call(
            functools.partial(cross_kernel, row_blocks, group, arrays),
            grid=(1,),
            in_specs=first(columns),
            out_specs=[pl.BlockSpec((2, coded, group), lambda step: (0, 0, 0))] * (n_cam - 1),
            out_shape=[jax.ShapeDtypeStruct((2, coded, group), jnp.int16)] * (n_cam - 1),
            compiler_params=PARAMS,
            name="cross",
        )(*near)
        far = [
            lax.ppermute(value, "cam", [(i, i ^ (pos + 1)) for i in range(n_cam)])
            for pos, value in enumerate(crossed)
        ]
        base = pl.pallas_call(
            functools.partial(base_kernel, (turn, row_blocks, col_blocks, arrays)),
            grid=(1,),
            in_specs=[SMEM, VMEM] + first(group),
            out_specs=pl.BlockSpec((extent, 2 * group), lambda step: (0, 0)),
            out_shape=jax.ShapeDtypeStruct((extent, 2 * group), jnp.float32),
            compiler_params=PARAMS,
            name="base",
        )(me, wide, *near)
        before = [] if result is None else [result]
        result = pl.pallas_call(
            functools.partial(finish_kernel, row_blocks, n_cam - 1),
            grid=(1,),
            in_specs=[VMEM] * n_cam + [pl.BlockSpec(memory_space=pl.ANY)] * len(before),
            out_specs=pl.BlockSpec((extent, 2 * group), lambda step, turn=turn: (0, turn)),
            out_shape=jax.ShapeDtypeStruct((extent, col_blocks * CB), jnp.float32),
            input_output_aliases={n_cam: 0} if before else {},
            compiler_params=PARAMS,
            name="finish",
        )(base, *far, *before)
    return result


def solution(mesh):
    return jax.shard_map(
        body,
        mesh=mesh,
        in_specs=(
            P(("lm", "cam"), None, None, None),
            P(None, None, ("lm", "cam")),
            P(("lm", "cam"), None),
            P(("lm", "cam")),
            P("lm", None, None),
        ),
        out_specs=P("lm", "cam"),
        check_vma=False,
    )
```

```python
import functools
import math

import jax
import jax.numpy as jnp
from jax import lax
from jax.experimental import pallas as pl
from jax.experimental.pallas import tpu as pltpu
from jax.sharding import PartitionSpec as P

CB = 64
LMB = 128
K = 16
WIDTH = 3 * LMB
STRIP = 16
LANES = 128
VMEM = pl.BlockSpec(memory_space=pltpu.VMEM)
SMEM = pl.BlockSpec(memory_space=pltpu.SMEM)
PARAMS = pltpu.CompilerParams(vmem_limit_bytes=32 * 1024 * 1024)


def invert_rows(cur_ref, start):
    lanes = pl.ds(start, LMB)
    entry = [[cur_ref[row, col : col + 1, lanes] for col in range(3)] for row in range(3)]
    cofactor = [
        [
            entry[(row + 1) % 3][(col + 1) % 3] * entry[(row + 2) % 3][(col + 2) % 3]
            - entry[(row + 1) % 3][(col + 2) % 3] * entry[(row + 2) % 3][(col + 1) % 3]
            for col in range(3)
        ]
        for row in range(3)
    ]
    determ = (
        entry[0][0] * cofactor[0][0] + entry[0][1] * cofactor[0][1] + entry[0][2] * cofactor[0][2]
    )
    return [[cofactor[col][row] / determ for col in range(3)] for row in range(3)]


def encode(dst, lanes, parts):
    blocks = len(parts)
    row = lax.broadcasted_iota(jnp.int32, (STRIP, LANES), 0)
    tops = jnp.full((STRIP, LANES), 2.0**-100, jnp.float32)
    for block, part in enumerate(parts):
        top = jnp.max(jnp.abs(part()), axis=0, keepdims=True)
        tops = jnp.where(row == block, jnp.maximum(top, tops), tops)
    power = jnp.ceil(jnp.log2(tops) - 14.99)
    inverse = jnp.exp2(-power)
    for block, part in enumerate(parts):
        coded = jnp.floor(part() * inverse[block : block + 1] + 0.5)
        dst[pl.ds(block * CB, CB), lanes] = coded.astype(jnp.int32).astype(jnp.int16)
    dst[pl.ds(blocks * CB, STRIP), lanes] = power.astype(jnp.int32).astype(jnp.int16)


def decode(src, lanes, first, blocks):
    below = src.shape[0] - STRIP
    strip = src[pl.ds(below, STRIP), lanes].astype(jnp.int32).astype(jnp.float32)
    scale = jnp.exp2(strip)
    return [
        src[pl.ds(block * CB, CB), lanes].astype(jnp.int32).astype(jnp.float32)
        * scale[block : block + 1]
        for block in range(first, first + blocks)
    ]


def gathered(place, keep, came, lanes, blocks):
    parts = [keep[place, pl.ds(block * CB, CB), lanes] for block in range(blocks)]
    for src in came:
        here = decode(src, lanes, place * blocks, blocks)
        parts = [part + other for part, other in zip(parts, here)]
    return parts


def given(values):
    return [functools.partial(lambda value: value, value) for value in values]


def spot_of(index, order):
    bits = len(order)
    return sum(((index >> (bits - 1 - pos)) & 1) << bit for pos, bit in enumerate(order))


def form_tile(plan, table, tile, pan, cur, rows):
    total, row_blocks = plan
    inverse = invert_rows(cur, tile * LMB)

    def one_group(group, carry):
        places = [group * row_blocks + block for block in range(row_blocks)]
        slots = [table[tile, total + place] for place in places]

        @pl.when(functools.reduce(jnp.maximum, slots) >= 0)
        def some():
            for place, slot in zip(places, slots):
                lines = pl.ds(pl.multiple_of(place * CB, CB), CB)

                @pl.when(slot >= 0)
                def form():
                    wide = pan[tile, slot].astype(jnp.float32)
                    split = [wide[:, c * LMB : (c + 1) * LMB] for c in range(3)]
                    for q in range(3):
                        formed = (
                            split[0] * inverse[0][q]
                            + split[1] * inverse[1][q]
                            + split[2] * inverse[2][q]
                        )
                        high = formed.astype(jnp.bfloat16)
                        low = (formed - high.astype(jnp.float32)).astype(jnp.bfloat16)
                        at = q * LMB
                        rows[tile, lines, at : at + LMB] = high
                        rows[tile, lines, WIDTH + at : WIDTH + at + LMB] = low

                @pl.when(slot < 0)
                def blank():
                    rows[tile, lines, :] = jnp.zeros((CB, 2 * WIDTH), jnp.bfloat16)

        return carry

    lax.fori_loop(0, rows.shape[1] // (row_blocks * CB), one_group, 0)


def form_own_kernel(plan, table, pan_ref, cur_ref, rows, pan, cur, pan_sem, cur_sem):
    tiles = rows.shape[0]
    copies = [
        pltpu.make_async_copy(pan_ref.at[tile], pan.at[tile], pan_sem.at[tile])
        for tile in range(tiles)
    ]
    small = pltpu.make_async_copy(cur_ref, cur, cur_sem)
    small.start()
    for copy in copies:
        copy.start()
    small.wait()
    for tile, copy in enumerate(copies):
        copy.wait()
        form_tile(plan, table, tile, pan, cur, rows)


def form_kernel(plan, table, pan, cur, rows):
    for tile in range(rows.shape[0]):
        form_tile(plan, table, tile, pan, cur, rows)


def round_kernel(plan, table_a, table_b, pan_a, pan_b, rows_a, rows_b, *rest):
    sending, bases, orders, total, row_blocks, halves, tiles, pairs = plan
    outs, right, pair_at, acc = rest[:2], rest[2], rest[3], rest[4]
    extent = row_blocks * CB
    columns = pairs * LANES
    for base, order, out in zip(bases, orders, outs):
        acc[...] = jnp.zeros_like(acc)
        spots = [spot_of(half + (halves if sending else 0), order) for half in range(halves)]
        for table, pan, rows in ((table_a, pan_a, rows_a), (table_b, pan_b, rows_b)):

            def one_tile(tile, carry):
                used = [
                    functools.reduce(
                        jnp.maximum,
                        [
                            table[tile, total + spot * row_blocks + block]
                            for block in range(row_blocks)
                        ],
                    )
                    for spot in spots
                ]

                @pl.when(functools.reduce(jnp.maximum, used) >= 0)
                def some():
                    def one_pair(pair, count):
                        slots = [table[tile, base + 2 * pair + side] for side in range(2)]
                        live = jnp.maximum(slots[0], slots[1]) >= 0

                        @pl.when(live)
                        def stage():
                            pair_at[count] = pair * LANES
                            for side, slot in enumerate(slots):
                                first = pl.multiple_of(count * LANES + side * CB, CB)
                                lines = pl.ds(first, CB)

                                @pl.when(slot >= 0)
                                def fill():
                                    panel = pan[tile, slot]
                                    right[lines, :WIDTH] = panel
                                    right[lines, WIDTH:] = panel

                                @pl.when(slot < 0)
                                def blank():
                                    right[lines, :] = jnp.zeros((CB, 2 * WIDTH), jnp.bfloat16)

                        return count + jnp.where(live, 1, 0)

                    count = lax.fori_loop(0, pairs, one_pair, jnp.int32(0))
                    pair_at[count] = columns

                    def one_dot(double, carry):
                        first = pl.multiple_of(double * 2 * LANES, 2 * LANES)
                        for half, spot in enumerate(spots):

                            @pl.when(used[half] >= 0)
                            def add():
                                result = lax.dot_general(
                                    rows[tile, spot * extent : (spot + 1) * extent, :],
                                    right[pl.ds(first, 2 * LANES), :],
                                    (((1,), (1,)), ((), ())),
                                    preferred_element_type=jnp.float32,
                                )
                                for side in range(2):
                                    at = pl.multiple_of(pair_at[2 * double + side], LANES)
                                    acc[half, :, pl.ds(at, LANES)] += result[
                                        :, side * LANES : (side + 1) * LANES
                                    ]

                        return carry

                    lax.fori_loop(0, (count + 1) // 2, one_dot, 0)

                return carry

            lax.fori_loop(0, tiles, one_tile, 0)

        def store(start, carry):
            lanes = pl.ds(pl.multiple_of(start * LANES, LANES), LANES)
            if sending:
                parts = [
                    functools.partial(
                        lambda half, block: acc[half, pl.ds(block * CB, CB), lanes], half, block
                    )
                    for half in range(halves)
                    for block in range(row_blocks)
                ]
                encode(out, lanes, parts)
            else:
                for half in range(halves):
                    out[half, :, lanes] = acc[half, :, lanes]
            return carry

        lax.fori_loop(0, pairs, store, 0)


def relay_kernel(plan, keep, *rest):
    row_blocks, size = plan
    dst = rest[-1]

    def code(start, carry):
        lanes = pl.ds(pl.multiple_of(start * LANES, LANES), LANES)
        parts = []
        for place in range(size // 2, size):
            parts += given(gathered(place, keep, rest[:-1], lanes, row_blocks))
        encode(dst, lanes, parts)
        return carry

    lax.fori_loop(0, dst.shape[1] // LANES, code, 0)


def cross_kernel(row_blocks, group, arrays, *rest):
    dsts = rest[2 * arrays :]
    for other, dst in enumerate(dsts):
        for start in range(0, group, LANES):
            parts = []
            for piece in range(2):
                keep, *came = rest[piece * arrays : (piece + 1) * arrays]
                lanes = pl.ds((other + 1) * group + start, LANES)
                parts += given(gathered(0, keep, came, lanes, row_blocks))
            encode(dst, pl.ds(start, LANES), parts)


def base_kernel(plan, me_ref, wide_ref, *rest):
    turn, row_blocks, col_blocks, arrays = plan
    out_ref = rest[-1]
    group = out_ref.shape[1] // 2
    first_row = (me_ref[0] * 2 + me_ref[1]) * row_blocks
    first_col = me_ref[2] * col_blocks
    lane = lax.broadcasted_iota(jnp.int32, (CB, LANES), 1) // CB
    for piece in range(2):
        keep, *came = rest[piece * arrays : (piece + 1) * arrays]
        for start in range(0, group, LANES):
            parts = gathered(0, keep, came, pl.ds(start, LANES), row_blocks)
            base = first_col + ((2 * turn + piece) * group + start) // CB
            for block in range(row_blocks):
                wide = jnp.where(base + lane == first_row + block, wide_ref[block], 0.0)
                out_ref[pl.ds(block * CB, CB), pl.ds(piece * group + start, LANES)] = (
                    wide - parts[block]
                )


def finish_kernel(row_blocks, far, base_ref, *rest):
    out_ref = rest[-1]
    group = out_ref.shape[1] // 2
    for piece in range(2):
        for start in range(0, group, LANES):
            total = [0.0] * row_blocks
            for src in rest[:far]:
                parts = decode(src, pl.ds(start, LANES), piece * row_blocks, row_blocks)
                total = [left + right for left, right in zip(total, parts)]
            lanes = pl.ds(piece * group + start, LANES)
            for block in range(row_blocks):
                lines = pl.ds(block * CB, CB)
                out_ref[lines, lanes] = base_ref[lines, lanes] - total[block]


def body(panels, curvature, visible_blocks, counts, camera_hessian):
    tiles = panels.shape[0]
    n_lm, n_cam = lax.axis_size("lm"), lax.axis_size("cam")
    chips = n_lm // 2
    bits = int(math.log2(chips))
    row_blocks = camera_hessian.shape[0]
    extent = row_blocks * CB
    col_blocks = row_blocks * n_lm // n_cam
    turns = col_blocks * CB // (2 * LANES)
    pieces = 2 * turns
    group = col_blocks * CB // pieces
    columns = group * n_cam
    total = row_blocks * n_lm
    orders = [list(range(bits)), list(reversed(range(bits)))]
    lm, cam = lax.axis_index("lm"), lax.axis_index("cam")
    me = jnp.stack([lm // 2, lm % 2, cam]).astype(jnp.int32)

    live = jnp.arange(K, dtype=jnp.int32)[None, :] < counts[:, None]
    ids = jnp.where(live, visible_blocks, -1)

    def swap(value, bit):
        return lax.ppermute(value, "lm", [(i, i ^ (1 << bit)) for i in range(n_lm)])

    pan_other, cur_other, ids_other = swap(panels, 0), swap(curvature, 0), swap(ids, 0)
    wide = jnp.concatenate([camera_hessian, camera_hessian], axis=-1)
    per = group // CB
    slots = jnp.arange(K, dtype=jnp.int32)[None, :, None]
    places = jnp.arange(total + chips * row_blocks, dtype=jnp.int32)

    def table_of(ids):
        inner = ids % col_blocks
        spot = ((inner // per) * n_cam + ((ids // col_blocks) ^ cam)) * per + inner % per
        owner = ids // row_blocks
        line = total + ((owner // 2) ^ (lm // 2)) * row_blocks + ids % row_blocks
        spot = jnp.where(ids >= 0, spot, -1)
        line = jnp.where((ids >= 0) & (owner % 2 == lm % 2), line, -1)
        found = (spot[:, :, None] == places) | (line[:, :, None] == places)
        return jnp.max(jnp.where(found, slots, -1), axis=1)

    table_a, table_b = table_of(ids), table_of(ids_other)
    formed = jax.ShapeDtypeStruct((tiles, chips * extent, 2 * WIDTH), jnp.bfloat16)
    whole = pl.BlockSpec(memory_space=pltpu.HBM)
    rows_a, pan_here = pl.pallas_call(
        functools.partial(form_own_kernel, (total, row_blocks)),
        in_specs=[SMEM, whole, whole],
        out_specs=[VMEM, VMEM],
        out_shape=[formed, jax.ShapeDtypeStruct(panels.shape, panels.dtype)],
        scratch_shapes=[
            pltpu.VMEM(curvature.shape, jnp.float32),
            pltpu.SemaphoreType.DMA((tiles,)),
            pltpu.SemaphoreType.DMA,
        ],
        compiler_params=PARAMS,
        name="form_own",
    )(table_a, panels, curvature)
    rows_b = pl.pallas_call(
        functools.partial(form_kernel, (total, row_blocks)),
        in_specs=[SMEM, VMEM, VMEM],
        out_specs=VMEM,
        out_shape=formed,
        compiler_params=PARAMS,
        name="form_other",
    )(table_b, pan_other, cur_other)

    def round_call(sending, turn, tables):
        if sending:
            made = jax.ShapeDtypeStruct((chips // 2 * extent + STRIP, columns), jnp.int16)
        else:
            made = jax.ShapeDtypeStruct((chips // 2, extent, columns), jnp.float32)
        bases = [(2 * turn + which) * n_cam * per for which in range(2)]
        pairs = columns // LANES
        plan = (sending, bases, orders, total, row_blocks, chips // 2, tiles, pairs)
        return pl.pallas_call(
            functools.partial(round_kernel, plan),
            in_specs=[SMEM] * 2 + [VMEM] * 4,
            out_specs=[VMEM] * 2,
            out_shape=[made] * 2,
            scratch_shapes=[
                pltpu.VMEM((columns + LANES, 2 * WIDTH), jnp.bfloat16),
                pltpu.SMEM((pairs + 1,), jnp.int32),
                pltpu.VMEM((chips // 2, extent, columns + LANES), jnp.float32),
            ],
            compiler_params=PARAMS,
            name="send" if sending else "keep",
        )(*tables, pan_here, pan_other, rows_a, rows_b)

    tables = (table_a, table_b)
    sends, keeps = [], []
    for turn in range(turns):
        for sending, made in ((True, sends), (False, keeps)):
            made.append(list(round_call(sending, turn, tables)))
            tables = lax.optimization_barrier((tables, made[-1]))[0]

    came = [[[], []] for _ in range(turns)]
    result = None
    for turn in range(turns):
        if turn:
            sends[turn] = lax.optimization_barrier((sends[turn], crossed))[0]
        for stage in range(bits):
            for piece in range(2):
                came[turn][piece].append(swap(sends[turn][piece], orders[piece][stage] + 1))
            size = chips >> (stage + 1)
            if size == 1:
                break
            for piece in range(2):
                arrays = [keeps[turn][piece]] + came[turn][piece]
                sends[turn][piece] = pl.pallas_call(
                    functools.partial(relay_kernel, (row_blocks, size)),
                    in_specs=[VMEM] * len(arrays),
                    out_specs=VMEM,
                    out_shape=jax.ShapeDtypeStruct((size // 2 * extent + STRIP, columns), jnp.int16),
                    compiler_params=PARAMS,
                    name="relay",
                )(*arrays)

        near = [array for piece in range(2) for array in [keeps[turn][piece]] + came[turn][piece]]
        arrays = len(near) // 2
        crossed = pl.pallas_call(
            functools.partial(cross_kernel, row_blocks, group, arrays),
            in_specs=[VMEM] * len(near),
            out_specs=[VMEM] * (n_cam - 1),
            out_shape=[jax.ShapeDtypeStruct((2 * extent + STRIP, group), jnp.int16)] * (n_cam - 1),
            compiler_params=PARAMS,
            name="cross",
        )(*near)
        far = [
            lax.ppermute(value, "cam", [(i, i ^ (pos + 1)) for i in range(n_cam)])
            for pos, value in enumerate(crossed)
        ]
        base = pl.pallas_call(
            functools.partial(base_kernel, (turn, row_blocks, col_blocks, arrays)),
            in_specs=[SMEM, VMEM] + [VMEM] * len(near),
            out_specs=VMEM,
            out_shape=jax.ShapeDtypeStruct((extent, 2 * group), jnp.float32),
            compiler_params=PARAMS,
            name="base",
        )(me, wide, *near)
        before = [] if result is None else [result]
        result = pl.pallas_call(
            functools.partial(finish_kernel, row_blocks, n_cam - 1),
            grid=(1,),
            in_specs=[VMEM] * n_cam + [pl.BlockSpec(memory_space=pl.ANY)] * len(before),
            out_specs=pl.BlockSpec((extent, 2 * group), lambda step, turn=turn: (0, turn)),
            out_shape=jax.ShapeDtypeStruct((extent, col_blocks * CB), jnp.float32),
            input_output_aliases={n_cam: 0} if before else {},
            compiler_params=PARAMS,
            name="finish",
        )(base, *far, *before)
    return result


def solution(mesh):
    return jax.shard_map(
        body,
        mesh=mesh,
        in_specs=(
            P(("lm", "cam"), None, None, None),
            P(None, None, ("lm", "cam")),
            P(("lm", "cam"), None),
            P(("lm", "cam")),
            P("lm", None, None),
        ),
        out_specs=P("lm", "cam"),
        check_vma=False,
    )
```

```python
import functools
import math

import jax
import jax.numpy as jnp
from jax import lax
from jax.experimental import pallas as pl
from jax.experimental.pallas import tpu as pltpu
from jax.sharding import PartitionSpec as P

CB = 64
LMB = 128
K = 16
WIDTH = 3 * LMB
LANES = 128
QUAD = 4
VMEM = pl.BlockSpec(memory_space=pltpu.VMEM)
SMEM = pl.BlockSpec(memory_space=pltpu.SMEM)
PARAMS = pltpu.CompilerParams(vmem_limit_bytes=32 * 1024 * 1024)


def invert_rows(cur_ref, start):
    lanes = pl.ds(start, LMB)
    entry = [[cur_ref[row, col : col + 1, lanes] for col in range(3)] for row in range(3)]
    cofactor = [
        [
            entry[(row + 1) % 3][(col + 1) % 3] * entry[(row + 2) % 3][(col + 2) % 3]
            - entry[(row + 1) % 3][(col + 2) % 3] * entry[(row + 2) % 3][(col + 1) % 3]
            for col in range(3)
        ]
        for row in range(3)
    ]
    determ = (
        entry[0][0] * cofactor[0][0] + entry[0][1] * cofactor[0][1] + entry[0][2] * cofactor[0][2]
    )
    return [[cofactor[col][row] / determ for col in range(3)] for row in range(3)]


def strip_of(blocks):
    return -(-blocks // 16) * 16


def encode(dst, lanes, parts):
    blocks = len(parts)
    strip = strip_of(blocks)
    row = lax.broadcasted_iota(jnp.int32, (strip, LANES), 0)
    tops = jnp.full((strip, LANES), 2.0**-100, jnp.float32)
    for block, part in enumerate(parts):
        top = jnp.max(jnp.abs(part()), axis=0, keepdims=True)
        tops = jnp.where(row == block, jnp.maximum(top, tops), tops)
    power = jnp.ceil(jnp.log2(tops) - 14.99)
    inverse = jnp.exp2(-power)
    for block, part in enumerate(parts):
        coded = jnp.floor(part() * inverse[block : block + 1] + 0.5)
        dst[pl.ds(block * CB, CB), lanes] = coded.astype(jnp.int32).astype(jnp.int16)
    dst[pl.ds(blocks * CB, strip), lanes] = power.astype(jnp.int32).astype(jnp.int16)


def scales(src, lanes):
    blocks = src.shape[0] // CB
    strip = src[pl.ds(blocks * CB, strip_of(blocks)), lanes]
    return jnp.exp2(strip.astype(jnp.int32).astype(jnp.float32))


def decode(src, lanes, scale, block):
    coded = src[pl.ds(block * CB, CB), lanes].astype(jnp.int32).astype(jnp.float32)
    return coded * scale[block : block + 1]


def gathered(keep, came, lanes, first, place, blocks):
    parts = [keep[pl.ds(first + block * CB, CB), lanes] for block in range(blocks)]
    for src in came:
        scale = scales(src, lanes)
        parts = [
            part + decode(src, lanes, scale, place * blocks + block)
            for block, part in enumerate(parts)
        ]
    return parts


def given(values):
    return [functools.partial(lambda value: value, value) for value in values]


def index_of(spot, order):
    bits = len(order)
    return sum(((spot >> bit) & 1) << (bits - 1 - pos) for pos, bit in enumerate(order))


def place_of(spot, block, orders, half_blocks, halves):
    half = block // half_blocks
    index = index_of(spot, orders[half])
    region = 0 if index >= halves else 1
    row = (half * halves + index % halves) * half_blocks + block % half_blocks
    return region * 2 * halves * half_blocks + row


def form_tile(plan, table, tile, pan, cur, rows, line_at, many):
    total, region_size = plan
    inverse = invert_rows(cur, tile * LMB)
    for region in range(2):
        list_at = region * (region_size + QUAD)

        def one_place(place, count):
            slot = table[tile, total + region * region_size + place]

            @pl.when(slot >= 0)
            def form():
                line_at[tile, list_at + count] = (region * region_size + place) * CB
                lines = pl.ds(pl.multiple_of((region * region_size + count) * CB, CB), CB)
                wide = pan[tile, slot].astype(jnp.float32)
                split = [wide[:, c * LMB : (c + 1) * LMB] for c in range(3)]
                for q in range(3):
                    formed = (
                        split[0] * inverse[0][q]
                        + split[1] * inverse[1][q]
                        + split[2] * inverse[2][q]
                    )
                    high = formed.astype(jnp.bfloat16)
                    low = (formed - high.astype(jnp.float32)).astype(jnp.bfloat16)
                    at = q * LMB
                    rows[tile, lines, at : at + LMB] = high
                    rows[tile, lines, WIDTH + at : WIDTH + at + LMB] = low

            return count + jnp.where(slot >= 0, 1, 0)

        count = lax.fori_loop(0, region_size, one_place, jnp.int32(0))
        many[tile, region] = (count + QUAD - 1) // QUAD
        for extra in range(QUAD):
            line_at[tile, list_at + count + extra] = 2 * region_size * CB


def form_own_kernel(plan, table, pan_ref, cur_ref, rows, line_at, many, pan, cur, sems):
    tiles = rows.shape[0]
    copies = [
        pltpu.make_async_copy(pan_ref.at[tile], pan.at[tile], sems.at[tile])
        for tile in range(tiles)
    ]
    small = pltpu.make_async_copy(cur_ref, cur, sems.at[tiles])
    small.start()
    for copy in copies:
        copy.start()
    small.wait()
    for tile, copy in enumerate(copies):
        copy.wait()
        form_tile(plan, table, tile, pan, cur, rows, line_at, many)


def form_kernel(plan, table, pan, cur, rows, line_at, many):
    for tile in range(rows.shape[0]):
        form_tile(plan, table, tile, pan, cur, rows, line_at, many)


def accumulate(plan, sides, right, pair_at, acc):
    base, pairs, regions, region_size = plan
    acc[...] = jnp.zeros_like(acc)
    dump = acc.shape[0] - CB
    for table, line_at, many, pan, rows in sides:

        def one_tile(tile, carry):
            used = functools.reduce(jnp.maximum, [many[tile, region] for region in regions])

            @pl.when(used > 0)
            def some():
                def one_pair(pair, count):
                    slots = [table[tile, base + 2 * pair + side] for side in range(2)]
                    live = jnp.maximum(slots[0], slots[1]) >= 0

                    @pl.when(live)
                    def stage():
                        pair_at[count] = pair * LANES
                        for side, slot in enumerate(slots):
                            first = pl.multiple_of(count * LANES + side * CB, CB)
                            lines = pl.ds(first, CB)

                            @pl.when(slot >= 0)
                            def fill():
                                panel = pan[tile, slot]
                                right[lines, :WIDTH] = panel
                                right[lines, WIDTH:] = panel

                            @pl.when(slot < 0)
                            def blank():
                                right[lines, :] = jnp.zeros((CB, 2 * WIDTH), jnp.bfloat16)

                    return count + jnp.where(live, 1, 0)

                count = lax.fori_loop(0, pairs, one_pair, jnp.int32(0))
                pair_at[count] = pairs * LANES
                for region in regions:
                    shift = region * region_size * CB if len(regions) == 1 else 0

                    def one_group(group, carry):
                        start = (region * region_size + group * QUAD) * CB
                        lines = pl.ds(pl.multiple_of(start, QUAD * CB), QUAD * CB)
                        list_at = region * (region_size + QUAD) + group * QUAD

                        def one_dot(double, carry):
                            first = pl.multiple_of(double * 2 * LANES, 2 * LANES)
                            result = lax.dot_general(
                                rows[tile, lines, :],
                                right[pl.ds(first, 2 * LANES), :],
                                (((1,), (1,)), ((), ())),
                                preferred_element_type=jnp.float32,
                            )
                            for block in range(QUAD):
                                line = jnp.minimum(line_at[tile, list_at + block] - shift, dump)
                                line = pl.multiple_of(line, CB)
                                for side in range(2):
                                    lane = pl.multiple_of(pair_at[2 * double + side], LANES)
                                    acc[pl.ds(line, CB), pl.ds(lane, LANES)] += result[
                                        block * CB : (block + 1) * CB,
                                        side * LANES : (side + 1) * LANES,
                                    ]
                            return carry

                        return lax.fori_loop(0, (count + 1) // 2, one_dot, carry)

                    lax.fori_loop(0, many[tile, region], one_group, 0)

            return carry

        lax.fori_loop(0, rows.shape[0], one_tile, 0)


def each_tile(columns, work):
    def one(start, carry):
        work(pl.ds(pl.multiple_of(start * LANES, LANES), LANES))
        return carry

    lax.fori_loop(0, columns // LANES, one, 0)


def blocks_at(acc, first, blocks, lanes):
    return [
        functools.partial(lambda block: acc[pl.ds(first + block * CB, CB), lanes], block)
        for block in range(blocks)
    ]


def sides_of(refs):
    return [refs[:5], refs[5:10]]


def send_kernel(plan, *refs):
    outs, (right, pair_at, acc) = refs[10:12], refs[12:]
    accumulate(plan, sides_of(refs), right, pair_at, acc)
    blocks = plan[3] // 2

    def code(lanes):
        for half, out in enumerate(outs):
            encode(out, lanes, blocks_at(acc, half * blocks * CB, blocks, lanes))

    each_tile(outs[0].shape[1], code)


def keep_kernel(plan, *refs):
    acc, right, pair_at = refs[10:]
    accumulate(plan, sides_of(refs), right, pair_at, acc)


def chain_kernel(plan, *refs):
    acc, to_right, to_left, right, pair_at = refs[10:]
    accumulate(plan, sides_of(refs), right, pair_at, acc)
    _, n_cam, _, region_size = plan
    for group, out in ((n_cam - 1, to_right), (1, to_left)):
        lanes = pl.ds(group * LANES, LANES)
        encode(out, pl.ds(0, LANES), blocks_at(acc, 0, 2 * region_size, lanes))


def link_kernel(groups, acc, from_left, from_right, to_right, to_left):
    for group, src, out in zip(groups, (from_left, from_right), (to_right, to_left)):
        blocks = src.shape[0] // CB
        here = pl.ds(0, LANES)
        lanes = pl.ds(group * LANES, LANES)
        scale = scales(src, here)
        parts = [
            functools.partial(
                lambda block, src, lanes, scale: acc[pl.ds(block * CB, CB), lanes]
                + decode(src, here, scale, block),
                block,
                src,
                lanes,
                scale,
            )
            for block in range(blocks)
        ]
        encode(out, here, parts)


def spread_kernel(places, acc, from_left, from_right, *outs):
    here = pl.ds(0, LANES)
    left, right = scales(from_left, here), scales(from_right, here)
    for spot, out in enumerate(outs):
        parts = [
            acc[pl.ds(place * CB, CB), here]
            + decode(from_left, here, left, place)
            + decode(from_right, here, right, place)
            for place in places[spot]
        ]
        if spot:
            encode(out, here, given(parts))
        else:
            for block, part in enumerate(parts):
                out[pl.ds(block * CB, CB), :] = part


def relay_kernel(plan, keep, *rest):
    first, blocks, size = plan
    dst = rest[-1]

    def code(lanes):
        parts = []
        for place in range(size // 2, size):
            line = first + place * blocks * CB
            parts += given(gathered(keep, rest[:-1], lanes, line, place, blocks))
        encode(dst, lanes, parts)

    each_tile(dst.shape[1], code)


def own_rows(firsts, blocks, keep, came, lanes):
    parts = []
    for first, arrays in zip(firsts, came):
        parts += gathered(keep, arrays, lanes, first, 0, blocks)
    return parts


def cross_kernel(plan, keep, *rest):
    firsts, blocks, arrays = plan
    came = [rest[half * arrays : (half + 1) * arrays] for half in range(2)]
    dsts = rest[2 * arrays :]
    group = dsts[0].shape[1]
    for other, dst in enumerate(dsts):

        def code(start, carry, other=other, dst=dst):
            at = pl.multiple_of(start * LANES, LANES)
            lanes = pl.ds(pl.multiple_of((other + 1) * group + at, LANES), LANES)
            encode(dst, pl.ds(at, LANES), given(own_rows(firsts, blocks, keep, came, lanes)))
            return carry

        lax.fori_loop(0, group // LANES, code, 0)


def hessian_part(me_ref, wide_ref, plan, start, block):
    row_blocks, col_blocks = plan
    row = (me_ref[0] * 2 + me_ref[1]) * row_blocks + block
    lane = lax.broadcasted_iota(jnp.int32, (CB, LANES), 1) // CB
    return jnp.where(me_ref[2] * col_blocks + start // CB + lane == row, wide_ref[block], 0.0)


def base_kernel(plan, me_ref, wide_ref, keep, *rest):
    sizes, firsts, blocks, arrays = plan
    came = [rest[half * arrays : (half + 1) * arrays] for half in range(2)]
    out = rest[-1]
    for start in range(0, out.shape[1], LANES):
        lanes = pl.ds(start, LANES)
        for block, part in enumerate(own_rows(firsts, blocks, keep, came, lanes)):
            out[pl.ds(block * CB, CB), lanes] = (
                hessian_part(me_ref, wide_ref, sizes, start, block) - part
            )


def small_kernel(plan, me_ref, wide_ref, own, *rest):
    sizes, start = plan
    out = rest[-1]
    here = pl.ds(0, LANES)
    parts = gathered(own, rest[:-1], here, 0, 0, sizes[0])
    for block, part in enumerate(parts):
        out[pl.ds(block * CB, CB), :] = hessian_part(me_ref, wide_ref, sizes, start, block) - part


def finish_kernel(blocks, base, small, *rest):
    out = rest[-1]
    step = pl.program_id(0)
    last = base.shape[1] // LANES

    @pl.when(step < last)
    def large():
        lanes = pl.ds(pl.multiple_of(step * LANES, LANES), LANES)
        factors = [scales(src, lanes) for src in rest[:-1]]
        for block in range(blocks):
            total = base[pl.ds(block * CB, CB), lanes]
            for src, scale in zip(rest[:-1], factors):
                total = total - decode(src, lanes, scale, block)
            out[pl.ds(block * CB, CB), :] = total

    @pl.when(step == last)
    def rest_of_it():
        out[...] = small[...]


def body(panels, curvature, visible_blocks, counts, camera_hessian):
    tiles = panels.shape[0]
    n_lm, n_cam = lax.axis_size("lm"), lax.axis_size("cam")
    chips = n_lm // 2
    halves = chips // 2
    bits = int(math.log2(chips))
    row_blocks = camera_hessian.shape[0]
    half_blocks = row_blocks // 2
    extent = row_blocks * CB
    total = row_blocks * n_lm
    col_blocks = total // n_cam
    large = col_blocks * CB - LANES
    per = large // CB
    columns = large * n_cam
    region_size = chips * half_blocks
    orders = [list(range(bits)), list(reversed(range(bits)))]
    lm, cam = lax.axis_index("lm"), lax.axis_index("cam")
    me = jnp.stack([lm // 2, lm % 2, cam]).astype(jnp.int32)

    live = jnp.arange(K, dtype=jnp.int32)[None, :] < counts[:, None]
    ids = jnp.where(live, visible_blocks, -1)

    def swap(value, step):
        return lax.ppermute(value, "lm", [(i, i ^ step) for i in range(n_lm)])

    pan_other, cur_other, ids_other = swap(panels, 1), swap(curvature, 1), swap(ids, 1)
    wide = jnp.concatenate([camera_hessian, camera_hessian], axis=-1)
    slots = jnp.arange(K, dtype=jnp.int32)[None, :, None]
    places = jnp.arange(total + 2 * region_size, dtype=jnp.int32)

    def table_of(ids):
        inner, owner = ids % col_blocks, ids // col_blocks
        spot = jnp.where(
            inner < per,
            (owner ^ cam) * per + inner,
            n_cam * per + ((owner - cam) % n_cam) * (col_blocks - per) + inner - per,
        )
        owner = ids // row_blocks
        group, block = (owner // 2) ^ (lm // 2), ids % row_blocks
        half = block // half_blocks
        index = jnp.where(half == 0, index_of(group, orders[0]), index_of(group, orders[1]))
        line = (half * halves + index % halves) * half_blocks + block % half_blocks
        line = total + line + jnp.where(index >= halves, 0, region_size)
        spot = jnp.where(ids >= 0, spot, -1)
        line = jnp.where((ids >= 0) & (owner % 2 == lm % 2), line, -1)
        found = (spot[:, :, None] == places) | (line[:, :, None] == places)
        return jnp.max(jnp.where(found, slots, -1), axis=1)

    def call(kernel, name, outs, scratch=(), **options):
        return pl.pallas_call(
            kernel,
            out_shape=outs,
            scratch_shapes=list(scratch),
            compiler_params=PARAMS,
            name=name,
            **options,
        )

    def coded(blocks, columns):
        return jax.ShapeDtypeStruct((blocks * CB + strip_of(blocks), columns), jnp.int16)

    def exact(rows, columns):
        return jax.ShapeDtypeStruct((rows, columns), jnp.float32)

    table_a, table_b = table_of(ids), table_of(ids_other)
    formed = [
        jax.ShapeDtypeStruct((tiles, 2 * region_size * CB, 2 * WIDTH), jnp.bfloat16),
        jax.ShapeDtypeStruct((tiles, 2 * (region_size + QUAD)), jnp.int32),
        jax.ShapeDtypeStruct((tiles, 2), jnp.int32),
    ]
    in_hbm = pl.BlockSpec(memory_space=pltpu.HBM)
    rows_a, line_a, many_a, pan_here = call(
        functools.partial(form_own_kernel, (total, region_size)),
        "form_own",
        formed + [jax.ShapeDtypeStruct(panels.shape, panels.dtype)],
        [pltpu.VMEM(curvature.shape, jnp.float32), pltpu.SemaphoreType.DMA((tiles + 1,))],
        in_specs=[SMEM, in_hbm, in_hbm],
        out_specs=[VMEM, SMEM, SMEM, VMEM],
    )(table_a, panels, curvature)
    rows_b, line_b, many_b = call(
        functools.partial(form_kernel, (total, region_size)),
        "form_other",
        formed,
        in_specs=[SMEM, VMEM, VMEM],
        out_specs=[VMEM, SMEM, SMEM],
    )(table_b, pan_other, cur_other)

    def scratch(pairs):
        return [
            pltpu.VMEM(((pairs + 1) * LANES, 2 * WIDTH), jnp.bfloat16),
            pltpu.SMEM((pairs + 1,), jnp.int32),
        ]

    def sums(kernel, name, base, pairs, regions, outs, more, tables):
        plan = (base, pairs, regions, region_size)
        side = [SMEM] * 3 + [VMEM] * 2
        return call(
            functools.partial(kernel, plan),
            name,
            outs,
            scratch(pairs) + more,
            in_specs=side * 2,
            out_specs=[VMEM] * len(outs),
        )(tables[0], line_a, many_a, pan_here, rows_a, tables[1], line_b, many_b, pan_other, rows_b)

    tables = (table_a, table_b)
    pairs = columns // LANES
    sum_shape = ((region_size + 1) * CB, columns + LANES)
    sends = sums(
        send_kernel,
        "send",
        0,
        pairs,
        [0],
        [coded(halves * half_blocks, columns)] * 2,
        [pltpu.VMEM(sum_shape, jnp.float32)],
        tables,
    )
    tables = lax.optimization_barrier((tables, sends))[0]
    acc, to_right, to_left = sums(
        chain_kernel,
        "chain",
        n_cam * per,
        n_cam,
        [0, 1],
        [exact((2 * region_size + 1) * CB, (n_cam + 1) * LANES)]
        + [coded(2 * region_size, LANES)] * 2,
        [],
        tables,
    )
    tables = lax.optimization_barrier((tables, acc))[0]
    (keep,) = sums(keep_kernel, "keep", 0, pairs, [1], [exact(*sum_shape)], [], tables)

    links = []
    for step in range(n_cam - 1):
        from_left = lax.ppermute(to_right, "cam", [(i, i + 1) for i in range(step + 1)])
        from_right = lax.ppermute(
            to_left, "cam", [(i, i - 1) for i in range(n_cam - 1 - step, n_cam)]
        )
        links.append((from_left, from_right))
        if step < n_cam - 2:
            groups = (n_cam - 2 - step, step + 2)
            to_right, to_left = call(
                functools.partial(link_kernel, groups),
                "link",
                [coded(2 * region_size, LANES)] * 2,
                in_specs=[VMEM] * 3,
                out_specs=[VMEM] * 2,
            )(acc, from_left, from_right)

    came = [[], []]
    firsts = [half * halves * half_blocks * CB for half in range(2)]
    for stage in range(bits):
        for half in range(2):
            came[half].append(swap(sends[half], 2 << orders[half][stage]))
        size = chips >> (stage + 1)
        if size == 1:
            break
        keep_now = lax.optimization_barrier((keep, links[min(n_cam - 3, 1)]))[0]
        sends = [
            call(
                functools.partial(relay_kernel, (firsts[half], half_blocks, size)),
                "relay",
                coded(size // 2 * half_blocks, columns),
                in_specs=[VMEM] * (1 + len(came[half])),
                out_specs=VMEM,
            )(keep_now, *came[half])
            for half in range(2)
        ]

    near = came[0] + came[1]
    sizes = (row_blocks, col_blocks)
    crossed = call(
        functools.partial(cross_kernel, (firsts, half_blocks, bits)),
        "cross",
        [coded(row_blocks, large)] * (n_cam - 1),
        in_specs=[VMEM] * (1 + len(near)),
        out_specs=[VMEM] * (n_cam - 1),
    )(keep, *near)
    far = [
        lax.ppermute(value, "cam", [(i, i ^ (pos + 1)) for i in range(n_cam)])
        for pos, value in enumerate(crossed)
    ]
    base = call(
        functools.partial(base_kernel, (sizes, firsts, half_blocks, bits)),
        "base",
        exact(extent, large),
        in_specs=[SMEM] + [VMEM] * (2 + len(near)),
        out_specs=VMEM,
    )(me, wide, keep, *near)

    spots = [
        [place_of(spot, block, orders, half_blocks, halves) for block in range(row_blocks)]
        for spot in range(chips)
    ]
    ends = lax.optimization_barrier((links[-1], crossed))[0]
    own, *spread = call(
        functools.partial(spread_kernel, spots),
        "spread",
        [exact(extent, LANES)] + [coded(row_blocks, LANES)] * (chips - 1),
        in_specs=[VMEM] * 3,
        out_specs=[VMEM] * chips,
    )(acc, *ends)
    others = [swap(value, 2 * (pos + 1)) for pos, value in enumerate(spread)]
    small = call(
        functools.partial(small_kernel, (sizes, large)),
        "small",
        exact(extent, LANES),
        in_specs=[SMEM] + [VMEM] * (2 + len(others)),
        out_specs=VMEM,
    )(me, wide, own, *others)
    return call(
        functools.partial(finish_kernel, row_blocks),
        "finish",
        exact(extent, col_blocks * CB),
        grid=(col_blocks * CB // LANES,),
        in_specs=[VMEM] * (1 + n_cam),
        out_specs=pl.BlockSpec((extent, LANES), lambda step: (0, step)),
    )(base, small, *far)


def solution(mesh):
    return jax.shard_map(
        body,
        mesh=mesh,
        in_specs=(
            P(("lm", "cam"), None, None, None),
            P(None, None, ("lm", "cam")),
            P(("lm", "cam"), None),
            P(("lm", "cam")),
            P("lm", None, None),
        ),
        out_specs=P("lm", "cam"),
        check_vma=False,
    )
```

```python
import functools
import math

import jax
import jax.numpy as jnp
from jax import lax
from jax.experimental import pallas as pl
from jax.experimental.pallas import tpu as pltpu
from jax.sharding import PartitionSpec as P

CB = 64
LMB = 128
K = 16
WIDTH = 3 * LMB
LANES = 128
QUAD = 4
VMEM = pl.BlockSpec(memory_space=pltpu.VMEM)
SMEM = pl.BlockSpec(memory_space=pltpu.SMEM)
PARAMS = pltpu.CompilerParams(vmem_limit_bytes=32 * 1024 * 1024)


def invert_rows(cur_ref, start):
    lanes = pl.ds(start, LMB)
    entry = [[cur_ref[row, col : col + 1, lanes] for col in range(3)] for row in range(3)]
    cofactor = [
        [
            entry[(row + 1) % 3][(col + 1) % 3] * entry[(row + 2) % 3][(col + 2) % 3]
            - entry[(row + 1) % 3][(col + 2) % 3] * entry[(row + 2) % 3][(col + 1) % 3]
            for col in range(3)
        ]
        for row in range(3)
    ]
    determ = (
        entry[0][0] * cofactor[0][0] + entry[0][1] * cofactor[0][1] + entry[0][2] * cofactor[0][2]
    )
    return [[cofactor[col][row] / determ for col in range(3)] for row in range(3)]


def strip_of(blocks):
    return -(-blocks // 16) * 16


def encode(dst, lanes, parts):
    blocks = len(parts)
    strip = strip_of(blocks)
    width = lanes.size
    row = lax.broadcasted_iota(jnp.int32, (strip, width), 0)
    tops = jnp.full((strip, width), 2.0**-100, jnp.float32)
    for block, part in enumerate(parts):
        top = jnp.max(jnp.abs(part()), axis=0, keepdims=True)
        tops = jnp.where(row == block, jnp.maximum(top, tops), tops)
    power = jnp.ceil(jnp.log2(tops) - 14.99)
    inverse = jnp.exp2(-power)
    for block, part in enumerate(parts):
        coded = jnp.floor(part() * inverse[block : block + 1] + 0.5)
        dst[pl.ds(block * CB, CB), lanes] = coded.astype(jnp.int32).astype(jnp.int16)
    dst[pl.ds(blocks * CB, strip), lanes] = power.astype(jnp.int32).astype(jnp.int16)


def scales(src, lanes):
    blocks = src.shape[0] // CB
    strip = src[pl.ds(blocks * CB, strip_of(blocks)), lanes]
    return jnp.exp2(strip.astype(jnp.int32).astype(jnp.float32))


def decode(src, lanes, scale, block):
    coded = src[pl.ds(block * CB, CB), lanes].astype(jnp.int32).astype(jnp.float32)
    return coded * scale[block : block + 1]


def gathered(keep, came, lanes, first, place, blocks):
    parts = [keep[pl.ds(first + block * CB, CB), lanes] for block in range(blocks)]
    for src in came:
        scale = scales(src, lanes)
        parts = [
            part + decode(src, lanes, scale, place * blocks + block)
            for block, part in enumerate(parts)
        ]
    return parts


def given(values):
    return [functools.partial(lambda value: value, value) for value in values]


def index_of(spot, order):
    bits = len(order)
    return sum(((spot >> bit) & 1) << (bits - 1 - pos) for pos, bit in enumerate(order))


def place_of(spot, block, orders, half_blocks, halves):
    half = block // half_blocks
    index = index_of(spot, orders[half])
    region = 0 if index >= halves else 1
    row = (half * halves + index % halves) * half_blocks + block % half_blocks
    return region * 2 * halves * half_blocks + row


def form_tile(plan, table, tile, pan, cur, rows, line_at, many):
    total, region_size = plan
    inverse = invert_rows(cur, tile * LMB)
    for region in range(2):
        list_at = region * (region_size + QUAD)

        def one_form(place, slot, count):
            line_at[tile, list_at + count] = place * CB
            lines = pl.ds(pl.multiple_of((region * region_size + count) * CB, CB), CB)
            wide = pan[tile, slot].astype(jnp.float32)
            split = [wide[:, c * LMB : (c + 1) * LMB] for c in range(3)]
            for q in range(3):
                formed = (
                    split[0] * inverse[0][q] + split[1] * inverse[1][q] + split[2] * inverse[2][q]
                )
                high = formed.astype(jnp.bfloat16)
                low = (formed - high.astype(jnp.float32)).astype(jnp.bfloat16)
                at = q * LMB
                rows[tile, lines, at : at + LMB] = high
                rows[tile, lines, WIDTH + at : WIDTH + at + LMB] = low

        def some_places(few, count):
            places = [region * region_size + few * QUAD + place for place in range(QUAD)]
            slots = [table[tile, total + place] for place in places]
            counts = [count]
            for slot in slots:
                counts.append(counts[-1] + jnp.where(slot >= 0, 1, 0))

            @pl.when(counts[-1] > count)
            def some():
                for place, slot, at in zip(places, slots, counts):
                    pl.when(slot >= 0)(functools.partial(one_form, place, slot, at))

            return counts[-1]

        count = lax.fori_loop(0, region_size // QUAD, some_places, jnp.int32(0))
        many[tile, region] = (count + QUAD - 1) // QUAD
        for extra in range(QUAD):
            line_at[tile, list_at + count + extra] = 2 * region_size * CB


def form_own_kernel(plan, table, pan_ref, cur_ref, rows, line_at, many, pan, cur, sems):
    tiles = rows.shape[0]
    copies = [
        pltpu.make_async_copy(pan_ref.at[tile], pan.at[tile], sems.at[tile])
        for tile in range(tiles)
    ]
    small = pltpu.make_async_copy(cur_ref, cur, sems.at[tiles])
    small.start()
    for copy in copies:
        copy.start()
    small.wait()
    for tile, copy in enumerate(copies):
        copy.wait()
        form_tile(plan, table, tile, pan, cur, rows, line_at, many)


def form_kernel(plan, table, pan, cur, rows, line_at, many):
    for tile in range(rows.shape[0]):
        form_tile(plan, table, tile, pan, cur, rows, line_at, many)


def joint_of(pairs):
    return 4 if pairs % 4 == 0 and pairs >= 8 else 2


def accumulate(plan, sides, right, pair_at, acc):
    base, pairs, regions, region_size = plan
    joint = joint_of(pairs)
    acc[...] = jnp.zeros_like(acc)
    dump = acc.shape[0] - CB
    for table, line_at, many, pan, rows in sides:

        def one_tile(tile, carry):
            used = functools.reduce(jnp.maximum, [many[tile, region] for region in regions])

            @pl.when(used > 0)
            def some():
                def one_pair(pair, count):
                    slots = [table[tile, base + 2 * pair + side] for side in range(2)]
                    live = jnp.maximum(slots[0], slots[1]) >= 0

                    @pl.when(live)
                    def stage():
                        pair_at[count] = pair * LANES
                        for side, slot in enumerate(slots):
                            first = pl.multiple_of(count * LANES + side * CB, CB)
                            lines = pl.ds(first, CB)

                            @pl.when(slot >= 0)
                            def fill():
                                panel = pan[tile, slot]
                                right[lines, :WIDTH] = panel
                                right[lines, WIDTH:] = panel

                            @pl.when(slot < 0)
                            def blank():
                                right[lines, :] = jnp.zeros((CB, 2 * WIDTH), jnp.bfloat16)

                    return count + jnp.where(live, 1, 0)

                count = lax.fori_loop(0, pairs, one_pair, jnp.int32(0))
                for extra in range(joint - 1):
                    pair_at[count + extra] = pairs * LANES
                for region in regions:
                    shift = region * region_size * CB if len(regions) == 1 else 0

                    def one_group(group, carry):
                        start = (region * region_size + group * QUAD) * CB
                        lines = pl.ds(pl.multiple_of(start, QUAD * CB), QUAD * CB)
                        list_at = region * (region_size + QUAD) + group * QUAD

                        def one_dot(few, carry):
                            first = pl.multiple_of(few * joint * LANES, joint * LANES)
                            result = lax.dot_general(
                                rows[tile, lines, :],
                                right[pl.ds(first, joint * LANES), :],
                                (((1,), (1,)), ((), ())),
                                preferred_element_type=jnp.float32,
                            )
                            for block in range(QUAD):
                                line = jnp.minimum(line_at[tile, list_at + block] - shift, dump)
                                line = pl.multiple_of(line, CB)
                                for side in range(joint):
                                    lane = pl.multiple_of(pair_at[few * joint + side], LANES)
                                    acc[pl.ds(line, CB), pl.ds(lane, LANES)] += result[
                                        block * CB : (block + 1) * CB,
                                        side * LANES : (side + 1) * LANES,
                                    ]
                            return carry

                        return lax.fori_loop(0, (count + joint - 1) // joint, one_dot, carry)

                    lax.fori_loop(0, many[tile, region], one_group, 0)

            return carry

        lax.fori_loop(0, rows.shape[0], one_tile, 0)


def each_tile(columns, work, most=4):
    width = max(w * LANES for w in range(1, most + 1) if columns % (w * LANES) == 0)

    def one(start, carry):
        work(pl.ds(pl.multiple_of(start * width, width), width))
        return carry

    lax.fori_loop(0, columns // width, one, 0)


def blocks_at(acc, first, blocks, lanes):
    return [
        functools.partial(lambda block: acc[pl.ds(first + block * CB, CB), lanes], block)
        for block in range(blocks)
    ]


def sides_of(refs):
    return [refs[:5], refs[5:10]]


def send_kernel(plan, *refs):
    outs, (right, pair_at, acc) = refs[10:12], refs[12:]
    accumulate(plan, sides_of(refs), right, pair_at, acc)
    blocks = plan[3] // 2

    def code(lanes):
        for half, out in enumerate(outs):
            encode(out, lanes, blocks_at(acc, half * blocks * CB, blocks, lanes))

    each_tile(outs[0].shape[1], code)


def keep_kernel(plan, *refs):
    acc, right, pair_at = refs[10:]
    accumulate(plan, sides_of(refs), right, pair_at, acc)


def chain_kernel(plan, *refs):
    acc, to_right, to_left, right, pair_at = refs[10:]
    accumulate(plan, sides_of(refs), right, pair_at, acc)
    _, n_cam, _, region_size = plan
    for group, out in ((n_cam - 1, to_right), (1, to_left)):
        lanes = pl.ds(group * LANES, LANES)
        encode(out, pl.ds(0, LANES), blocks_at(acc, 0, 2 * region_size, lanes))


def link_kernel(groups, acc, from_left, from_right, to_right, to_left):
    for group, src, out in zip(groups, (from_left, from_right), (to_right, to_left)):
        blocks = src.shape[0] // CB
        here = pl.ds(0, LANES)
        lanes = pl.ds(group * LANES, LANES)
        scale = scales(src, here)
        parts = [
            functools.partial(
                lambda block, src, lanes, scale: acc[pl.ds(block * CB, CB), lanes]
                + decode(src, here, scale, block),
                block,
                src,
                lanes,
                scale,
            )
            for block in range(blocks)
        ]
        encode(out, here, parts)


def spread_kernel(places, acc, from_left, from_right, *outs):
    here = pl.ds(0, LANES)
    left, right = scales(from_left, here), scales(from_right, here)
    for spot, out in enumerate(outs):
        parts = [
            acc[pl.ds(place * CB, CB), here]
            + decode(from_left, here, left, place)
            + decode(from_right, here, right, place)
            for place in places[spot]
        ]
        if spot:
            encode(out, here, given(parts))
        else:
            for block, part in enumerate(parts):
                out[pl.ds(block * CB, CB), :] = part


def relay_kernel(plan, keep, *rest):
    first, blocks, size = plan
    dst = rest[-1]

    def code(lanes):
        parts = []
        for place in range(size // 2, size):
            line = first + place * blocks * CB
            parts += given(gathered(keep, rest[:-1], lanes, line, place, blocks))
        encode(dst, lanes, parts)

    each_tile(dst.shape[1], code, 2)


def own_rows(firsts, blocks, keep, came, lanes):
    parts = []
    for first, arrays in zip(firsts, came):
        parts += gathered(keep, arrays, lanes, first, 0, blocks)
    return parts


def cross_kernel(plan, keep, *rest):
    firsts, blocks, arrays = plan
    came = [rest[half * arrays : (half + 1) * arrays] for half in range(2)]
    dsts = rest[2 * arrays :]
    group = dsts[0].shape[1]
    for other, dst in enumerate(dsts):

        for start in range(0, group, LANES):
            lanes = pl.ds((other + 1) * group + start, LANES)
            encode(dst, pl.ds(start, LANES), given(own_rows(firsts, blocks, keep, came, lanes)))


def hessian_part(me_ref, wide_ref, plan, start, block):
    row_blocks, col_blocks = plan
    row = (me_ref[0] * 2 + me_ref[1]) * row_blocks + block
    lane = lax.broadcasted_iota(jnp.int32, (CB, LANES), 1) // CB
    return jnp.where(me_ref[2] * col_blocks + start // CB + lane == row, wide_ref[block], 0.0)


def base_kernel(plan, me_ref, wide_ref, keep, *rest):
    sizes, firsts, blocks, arrays = plan
    came = [rest[half * arrays : (half + 1) * arrays] for half in range(2)]
    out = rest[-1]
    for start in range(0, out.shape[1], LANES):
        lanes = pl.ds(start, LANES)
        for block, part in enumerate(own_rows(firsts, blocks, keep, came, lanes)):
            out[pl.ds(block * CB, CB), lanes] = (
                hessian_part(me_ref, wide_ref, sizes, start, block) - part
            )


def small_kernel(plan, me_ref, wide_ref, own, *rest):
    sizes, start = plan
    out = rest[-1]
    here = pl.ds(0, LANES)
    parts = gathered(own, rest[:-1], here, 0, 0, sizes[0])
    for block, part in enumerate(parts):
        out[pl.ds(block * CB, CB), :] = hessian_part(me_ref, wide_ref, sizes, start, block) - part


def finish_kernel(blocks, base, small, *rest):
    out = rest[-1]
    step = pl.program_id(0)
    last = base.shape[1] // LANES

    @pl.when(step < last)
    def large():
        lanes = pl.ds(pl.multiple_of(step * LANES, LANES), LANES)
        factors = [scales(src, lanes) for src in rest[:-1]]
        for block in range(blocks):
            total = base[pl.ds(block * CB, CB), lanes]
            for src, scale in zip(rest[:-1], factors):
                total = total - decode(src, lanes, scale, block)
            out[pl.ds(block * CB, CB), :] = total

    @pl.when(step == last)
    def rest_of_it():
        out[...] = small[...]


def body(panels, curvature, visible_blocks, counts, camera_hessian):
    tiles = panels.shape[0]
    n_lm, n_cam = lax.axis_size("lm"), lax.axis_size("cam")
    chips = n_lm // 2
    halves = chips // 2
    bits = int(math.log2(chips))
    row_blocks = camera_hessian.shape[0]
    half_blocks = row_blocks // 2
    extent = row_blocks * CB
    total = row_blocks * n_lm
    col_blocks = total // n_cam
    large = col_blocks * CB - LANES
    per = large // CB
    columns = large * n_cam
    region_size = chips * half_blocks
    orders = [list(range(bits)), list(reversed(range(bits)))]
    lm, cam = lax.axis_index("lm"), lax.axis_index("cam")
    me = jnp.stack([lm // 2, lm % 2, cam]).astype(jnp.int32)

    live = jnp.arange(K, dtype=jnp.int32)[None, :] < counts[:, None]
    ids = jnp.where(live, visible_blocks, -1)

    def swap(value, step):
        return lax.ppermute(value, "lm", [(i, i ^ step) for i in range(n_lm)])

    pan_other, cur_other, ids_other = swap(panels, 1), swap(curvature, 1), swap(ids, 1)
    wide = jnp.concatenate([camera_hessian, camera_hessian], axis=-1)
    slots = jnp.arange(K, dtype=jnp.int32)[None, :, None]
    places = jnp.arange(total + 2 * region_size, dtype=jnp.int32)

    def table_of(ids):
        inner, owner = ids % col_blocks, ids // col_blocks
        spot = jnp.where(
            inner < per,
            (owner ^ cam) * per + inner,
            n_cam * per + ((owner - cam) % n_cam) * (col_blocks - per) + inner - per,
        )
        owner = ids // row_blocks
        group, block = (owner // 2) ^ (lm // 2), ids % row_blocks
        half = block // half_blocks
        index = jnp.where(half == 0, index_of(group, orders[0]), index_of(group, orders[1]))
        line = (half * halves + index % halves) * half_blocks + block % half_blocks
        line = total + line + jnp.where(index >= halves, 0, region_size)
        spot = jnp.where(ids >= 0, spot, -1)
        line = jnp.where((ids >= 0) & (owner % 2 == lm % 2), line, -1)
        found = (spot[:, :, None] == places) | (line[:, :, None] == places)
        return jnp.max(jnp.where(found, slots, -1), axis=1)

    def call(kernel, name, outs, scratch=(), **options):
        return pl.pallas_call(
            kernel,
            out_shape=outs,
            scratch_shapes=list(scratch),
            compiler_params=PARAMS,
            name=name,
            **options,
        )

    def coded(blocks, columns):
        return jax.ShapeDtypeStruct((blocks * CB + strip_of(blocks), columns), jnp.int16)

    def exact(rows, columns):
        return jax.ShapeDtypeStruct((rows, columns), jnp.float32)

    table_a, table_b = table_of(ids), table_of(ids_other)
    formed = [
        jax.ShapeDtypeStruct((tiles, 2 * region_size * CB, 2 * WIDTH), jnp.bfloat16),
        jax.ShapeDtypeStruct((tiles, 2 * (region_size + QUAD)), jnp.int32),
        jax.ShapeDtypeStruct((tiles, 2), jnp.int32),
    ]
    in_hbm = pl.BlockSpec(memory_space=pltpu.HBM)
    rows_a, line_a, many_a, pan_here = call(
        functools.partial(form_own_kernel, (total, region_size)),
        "form_own",
        formed + [jax.ShapeDtypeStruct(panels.shape, panels.dtype)],
        [pltpu.VMEM(curvature.shape, jnp.float32), pltpu.SemaphoreType.DMA((tiles + 1,))],
        in_specs=[SMEM, in_hbm, in_hbm],
        out_specs=[VMEM, SMEM, SMEM, VMEM],
    )(table_a, panels, curvature)
    rows_b, line_b, many_b = call(
        functools.partial(form_kernel, (total, region_size)),
        "form_other",
        formed,
        in_specs=[SMEM, VMEM, VMEM],
        out_specs=[VMEM, SMEM, SMEM],
    )(table_b, pan_other, cur_other)

    def scratch(pairs):
        return [
            pltpu.VMEM(((pairs + 1) * LANES, 2 * WIDTH), jnp.bfloat16),
            pltpu.SMEM((pairs + joint_of(pairs),), jnp.int32),
        ]

    def sums(kernel, name, base, pairs, regions, outs, more, tables):
        plan = (base, pairs, regions, region_size)
        side = [SMEM] * 3 + [VMEM] * 2
        return call(
            functools.partial(kernel, plan),
            name,
            outs,
            scratch(pairs) + more,
            in_specs=side * 2,
            out_specs=[VMEM] * len(outs),
        )(tables[0], line_a, many_a, pan_here, rows_a, tables[1], line_b, many_b, pan_other, rows_b)

    tables = (table_a, table_b)
    pairs = columns // LANES
    sum_shape = ((region_size + 1) * CB, columns + LANES)
    sends = sums(
        send_kernel,
        "send",
        0,
        pairs,
        [0],
        [coded(halves * half_blocks, columns)] * 2,
        [pltpu.VMEM(sum_shape, jnp.float32)],
        tables,
    )
    tables = lax.optimization_barrier((tables, sends))[0]
    acc, to_right, to_left = sums(
        chain_kernel,
        "chain",
        n_cam * per,
        n_cam,
        [0, 1],
        [exact((2 * region_size + 1) * CB, (n_cam + 1) * LANES)]
        + [coded(2 * region_size, LANES)] * 2,
        [],
        tables,
    )
    tables = lax.optimization_barrier((tables, acc))[0]
    (keep,) = sums(keep_kernel, "keep", 0, pairs, [1], [exact(*sum_shape)], [], tables)

    links = []
    for step in range(n_cam - 1):
        from_left = lax.ppermute(to_right, "cam", [(i, i + 1) for i in range(step + 1)])
        from_right = lax.ppermute(
            to_left, "cam", [(i, i - 1) for i in range(n_cam - 1 - step, n_cam)]
        )
        if not links:
            from_left, from_right = lax.optimization_barrier((from_left, from_right, keep))[:2]
        links.append((from_left, from_right))
        if step < n_cam - 2:
            groups = (n_cam - 2 - step, step + 2)
            to_right, to_left = call(
                functools.partial(link_kernel, groups),
                "link",
                [coded(2 * region_size, LANES)] * 2,
                in_specs=[VMEM] * 3,
                out_specs=[VMEM] * 2,
            )(acc, from_left, from_right)

    came = [[], []]
    firsts = [half * halves * half_blocks * CB for half in range(2)]
    for stage in range(bits):
        for half in range(2):
            came[half].append(swap(sends[half], 2 << orders[half][stage]))
        size = chips >> (stage + 1)
        if size == 1:
            break
        keep_now = lax.optimization_barrier((keep, links[0]))[0]
        sends = [
            call(
                functools.partial(relay_kernel, (firsts[half], half_blocks, size)),
                "relay",
                coded(size // 2 * half_blocks, columns),
                in_specs=[VMEM] * (1 + len(came[half])),
                out_specs=VMEM,
            )(keep_now, *came[half])
            for half in range(2)
        ]

    near = came[0] + came[1]
    sizes = (row_blocks, col_blocks)
    crossed = call(
        functools.partial(cross_kernel, (firsts, half_blocks, bits)),
        "cross",
        [coded(row_blocks, large)] * (n_cam - 1),
        in_specs=[VMEM] * (1 + len(near)),
        out_specs=[VMEM] * (n_cam - 1),
    )(keep, *near)
    far = [
        lax.ppermute(value, "cam", [(i, i ^ (pos + 1)) for i in range(n_cam)])
        for pos, value in enumerate(crossed)
    ]
    base = call(
        functools.partial(base_kernel, (sizes, firsts, half_blocks, bits)),
        "base",
        exact(extent, large),
        in_specs=[SMEM] + [VMEM] * (2 + len(near)),
        out_specs=VMEM,
    )(me, wide, keep, *near)

    spots = [
        [place_of(spot, block, orders, half_blocks, halves) for block in range(row_blocks)]
        for spot in range(chips)
    ]
    ends = lax.optimization_barrier((links[-1], crossed))[0]
    own, *spread = call(
        functools.partial(spread_kernel, spots),
        "spread",
        [exact(extent, LANES)] + [coded(row_blocks, LANES)] * (chips - 1),
        in_specs=[VMEM] * 3,
        out_specs=[VMEM] * chips,
    )(acc, *ends)
    others = [swap(value, 2 * (pos + 1)) for pos, value in enumerate(spread)]
    small = call(
        functools.partial(small_kernel, (sizes, large)),
        "small",
        exact(extent, LANES),
        in_specs=[SMEM] + [VMEM] * (2 + len(others)),
        out_specs=VMEM,
    )(me, wide, own, *others)
    return call(
        functools.partial(finish_kernel, row_blocks),
        "finish",
        exact(extent, col_blocks * CB),
        grid=(col_blocks * CB // LANES,),
        in_specs=[VMEM] * (1 + n_cam),
        out_specs=pl.BlockSpec((extent, LANES), lambda step: (0, step)),
    )(base, small, *far)


def solution(mesh):
    return jax.shard_map(
        body,
        mesh=mesh,
        in_specs=(
            P(("lm", "cam"), None, None, None),
            P(None, None, ("lm", "cam")),
            P(("lm", "cam"), None),
            P(("lm", "cam")),
            P("lm", None, None),
        ),
        out_specs=P("lm", "cam"),
        check_vma=False,
    )
```

```python
import functools
import math

import jax
import jax.numpy as jnp
from jax import lax
from jax.experimental import pallas as pl
from jax.experimental.pallas import tpu as pltpu
from jax.sharding import PartitionSpec as P

CB = 64
LMB = 128
K = 16
WIDTH = 3 * LMB
LANES = 128
QUAD = 4
VMEM = pl.BlockSpec(memory_space=pltpu.VMEM)
SMEM = pl.BlockSpec(memory_space=pltpu.SMEM)
PARAMS = pltpu.CompilerParams(vmem_limit_bytes=32 * 1024 * 1024)


def invert_rows(cur_ref, start):
    lanes = pl.ds(start, LMB)
    entry = [[cur_ref[row, col : col + 1, lanes] for col in range(3)] for row in range(3)]
    cofactor = [
        [
            entry[(row + 1) % 3][(col + 1) % 3] * entry[(row + 2) % 3][(col + 2) % 3]
            - entry[(row + 1) % 3][(col + 2) % 3] * entry[(row + 2) % 3][(col + 1) % 3]
            for col in range(3)
        ]
        for row in range(3)
    ]
    determ = (
        entry[0][0] * cofactor[0][0] + entry[0][1] * cofactor[0][1] + entry[0][2] * cofactor[0][2]
    )
    return [[cofactor[col][row] / determ for col in range(3)] for row in range(3)]


def strip_of(blocks):
    return -(-blocks // 16) * 16


def encode(dst, lanes, parts):
    blocks = len(parts)
    strip = strip_of(blocks)
    width = lanes.size
    row = lax.broadcasted_iota(jnp.int32, (strip, width), 0)
    tops = jnp.full((strip, width), 2.0**-100, jnp.float32)
    for block, part in enumerate(parts):
        top = jnp.max(jnp.abs(part()), axis=0, keepdims=True)
        tops = jnp.where(row == block, jnp.maximum(top, tops), tops)
    power = jnp.ceil(jnp.log2(tops) - 14.99)
    inverse = jnp.exp2(-power)
    for block, part in enumerate(parts):
        coded = jnp.floor(part() * inverse[block : block + 1] + 0.5)
        dst[pl.ds(block * CB, CB), lanes] = coded.astype(jnp.int32).astype(jnp.int16)
    dst[pl.ds(blocks * CB, strip), lanes] = power.astype(jnp.int32).astype(jnp.int16)


def scales(src, lanes):
    blocks = src.shape[0] // CB
    strip = src[pl.ds(blocks * CB, strip_of(blocks)), lanes]
    return jnp.exp2(strip.astype(jnp.int32).astype(jnp.float32))


def decode(src, lanes, scale, block):
    coded = src[pl.ds(block * CB, CB), lanes].astype(jnp.int32).astype(jnp.float32)
    return coded * scale[block : block + 1]


def gathered(keep, came, lanes, first, place, blocks):
    parts = [keep[pl.ds(first + block * CB, CB), lanes] for block in range(blocks)]
    for src in came:
        scale = scales(src, lanes)
        parts = [
            part + decode(src, lanes, scale, place * blocks + block)
            for block, part in enumerate(parts)
        ]
    return parts


def given(values):
    return [functools.partial(lambda value: value, value) for value in values]


def index_of(spot, order):
    bits = len(order)
    return sum(((spot >> bit) & 1) << (bits - 1 - pos) for pos, bit in enumerate(order))


def place_of(spot, block, orders, half_blocks, halves):
    half = block // half_blocks
    index = index_of(spot, orders[half])
    region = 0 if index >= halves else 1
    row = (half * halves + index % halves) * half_blocks + block % half_blocks
    return region * 2 * halves * half_blocks + row


def form_tile(plan, table, tile, pan, cur, rows, line_at, many):
    total, region_size = plan
    inverse = invert_rows(cur, tile * LMB)
    for region in range(2):
        list_at = region * (region_size + QUAD)

        def one_form(place, slot, count):
            line_at[tile, list_at + count] = place * CB
            lines = pl.ds(pl.multiple_of((region * region_size + count) * CB, CB), CB)
            wide = pan[tile, slot].astype(jnp.float32)
            split = [wide[:, c * LMB : (c + 1) * LMB] for c in range(3)]
            for q in range(3):
                formed = (
                    split[0] * inverse[0][q] + split[1] * inverse[1][q] + split[2] * inverse[2][q]
                )
                high = formed.astype(jnp.bfloat16)
                low = (formed - high.astype(jnp.float32)).astype(jnp.bfloat16)
                at = q * LMB
                rows[tile, lines, at : at + LMB] = high
                rows[tile, lines, WIDTH + at : WIDTH + at + LMB] = low

        def some_places(few, count):
            places = [region * region_size + few * QUAD + place for place in range(QUAD)]
            slots = [table[tile, total + place] for place in places]
            counts = [count]
            for slot in slots:
                counts.append(counts[-1] + jnp.where(slot >= 0, 1, 0))

            @pl.when(counts[-1] > count)
            def some():
                for place, slot, at in zip(places, slots, counts):
                    pl.when(slot >= 0)(functools.partial(one_form, place, slot, at))

            return counts[-1]

        count = lax.fori_loop(0, region_size // QUAD, some_places, jnp.int32(0))
        many[tile, region] = (count + QUAD - 1) // QUAD
        for extra in range(QUAD):
            line_at[tile, list_at + count + extra] = 2 * region_size * CB


def form_own_kernel(plan, table, pan_ref, cur_ref, rows, line_at, many, pan, cur, sems):
    tiles = rows.shape[0]
    copies = [
        pltpu.make_async_copy(pan_ref.at[tile], pan.at[tile], sems.at[tile])
        for tile in range(tiles)
    ]
    small = pltpu.make_async_copy(cur_ref, cur, sems.at[tiles])
    small.start()
    for copy in copies:
        copy.start()
    small.wait()
    for tile, copy in enumerate(copies):
        copy.wait()
        form_tile(plan, table, tile, pan, cur, rows, line_at, many)


def form_kernel(plan, table, pan, cur, rows, line_at, many):
    for tile in range(rows.shape[0]):
        form_tile(plan, table, tile, pan, cur, rows, line_at, many)


def joint_of(pairs):
    return 4 if pairs % 4 == 0 and pairs >= 8 else 2


def accumulate(plan, sides, right, pair_at, acc):
    base, pairs, regions, region_size = plan
    joint = joint_of(pairs)
    acc[...] = jnp.zeros_like(acc)
    dump = acc.shape[0] - CB
    for table, line_at, many, pan, rows in sides:

        def one_tile(tile, carry):
            used = functools.reduce(jnp.maximum, [many[tile, region] for region in regions])

            @pl.when(used > 0)
            def some():
                def one_pair(pair, count):
                    slots = [table[tile, base + 2 * pair + side] for side in range(2)]
                    live = jnp.maximum(slots[0], slots[1]) >= 0

                    @pl.when(live)
                    def stage():
                        pair_at[count] = pair * LANES
                        for side, slot in enumerate(slots):
                            first = pl.multiple_of(count * LANES + side * CB, CB)
                            lines = pl.ds(first, CB)

                            @pl.when(slot >= 0)
                            def fill():
                                panel = pan[tile, slot]
                                right[lines, :WIDTH] = panel
                                right[lines, WIDTH:] = panel

                            @pl.when(slot < 0)
                            def blank():
                                right[lines, :] = jnp.zeros((CB, 2 * WIDTH), jnp.bfloat16)

                    return count + jnp.where(live, 1, 0)

                count = lax.fori_loop(0, pairs, one_pair, jnp.int32(0))
                for extra in range(joint - 1):
                    pair_at[count + extra] = pairs * LANES
                for region in regions:
                    shift = region * region_size * CB if len(regions) == 1 else 0

                    def one_group(group, carry):
                        start = (region * region_size + group * QUAD) * CB
                        lines = pl.ds(pl.multiple_of(start, QUAD * CB), QUAD * CB)
                        list_at = region * (region_size + QUAD) + group * QUAD

                        def one_dot(few, carry):
                            first = pl.multiple_of(few * joint * LANES, joint * LANES)
                            result = lax.dot_general(
                                rows[tile, lines, :],
                                right[pl.ds(first, joint * LANES), :],
                                (((1,), (1,)), ((), ())),
                                preferred_element_type=jnp.float32,
                            )
                            for block in range(QUAD):
                                line = jnp.minimum(line_at[tile, list_at + block] - shift, dump)
                                line = pl.multiple_of(line, CB)
                                for side in range(joint):
                                    lane = pl.multiple_of(pair_at[few * joint + side], LANES)
                                    acc[pl.ds(line, CB), pl.ds(lane, LANES)] += result[
                                        block * CB : (block + 1) * CB,
                                        side * LANES : (side + 1) * LANES,
                                    ]
                            return carry

                        return lax.fori_loop(0, (count + joint - 1) // joint, one_dot, carry)

                    lax.fori_loop(0, many[tile, region], one_group, 0)

            return carry

        lax.fori_loop(0, rows.shape[0], one_tile, 0)


def each_tile(columns, work, most=4):
    width = max(w * LANES for w in range(1, most + 1) if columns % (w * LANES) == 0)

    def one(start, carry):
        work(pl.ds(pl.multiple_of(start * width, width), width))
        return carry

    lax.fori_loop(0, columns // width, one, 0)


def blocks_at(acc, first, blocks, lanes):
    return [
        functools.partial(lambda block: acc[pl.ds(first + block * CB, CB), lanes], block)
        for block in range(blocks)
    ]


def sides_of(refs):
    return [refs[:5], refs[5:10]]


def send_kernel(plan, *refs):
    outs, (right, pair_at, acc) = refs[10:12], refs[12:]
    accumulate(plan, sides_of(refs), right, pair_at, acc)
    blocks = plan[3] // 2

    def code(lanes):
        for half, out in enumerate(outs):
            encode(out, lanes, blocks_at(acc, half * blocks * CB, blocks, lanes))

    each_tile(outs[0].shape[1], code)


def keep_kernel(plan, *refs):
    acc, right, pair_at = refs[10:]
    accumulate(plan, sides_of(refs), right, pair_at, acc)


def chain_kernel(plan, *refs):
    acc, to_right, to_left, right, pair_at = refs[10:]
    accumulate(plan, sides_of(refs), right, pair_at, acc)
    _, n_cam, _, region_size = plan
    for group, out in ((n_cam - 1, to_right), (1, to_left)):
        lanes = pl.ds(group * LANES, LANES)
        encode(out, pl.ds(0, LANES), blocks_at(acc, 0, 2 * region_size, lanes))


def link_kernel(groups, acc, from_left, from_right, to_right, to_left):
    for group, src, out in zip(groups, (from_left, from_right), (to_right, to_left)):
        blocks = src.shape[0] // CB
        here = pl.ds(0, LANES)
        lanes = pl.ds(group * LANES, LANES)
        scale = scales(src, here)
        parts = [
            functools.partial(
                lambda block, src, lanes, scale: acc[pl.ds(block * CB, CB), lanes]
                + decode(src, here, scale, block),
                block,
                src,
                lanes,
                scale,
            )
            for block in range(blocks)
        ]
        encode(out, here, parts)


def spread_kernel(places, acc, from_left, from_right, *outs):
    here = pl.ds(0, LANES)
    left, right = scales(from_left, here), scales(from_right, here)
    for spot, out in enumerate(outs):
        parts = [
            acc[pl.ds(place * CB, CB), here]
            + decode(from_left, here, left, place)
            + decode(from_right, here, right, place)
            for place in places[spot]
        ]
        if spot:
            encode(out, here, given(parts))
        else:
            for block, part in enumerate(parts):
                out[pl.ds(block * CB, CB), :] = part


def relay_kernel(plan, keep, *rest):
    first, blocks, size = plan
    dst = rest[-1]

    def code(lanes):
        parts = []
        for place in range(size // 2, size):
            line = first + place * blocks * CB
            parts += given(gathered(keep, rest[:-1], lanes, line, place, blocks))
        encode(dst, lanes, parts)

    each_tile(dst.shape[1], code, 2)


def own_rows(firsts, blocks, keep, came, lanes):
    parts = []
    for first, arrays in zip(firsts, came):
        parts += gathered(keep, arrays, lanes, first, 0, blocks)
    return parts


def cross_kernel(plan, keep, *rest):
    firsts, blocks, arrays = plan
    came = [rest[half * arrays : (half + 1) * arrays] for half in range(2)]
    dsts = rest[2 * arrays :]
    group = dsts[0].shape[1]
    for other, dst in enumerate(dsts):

        for start in range(0, group, LANES):
            lanes = pl.ds((other + 1) * group + start, LANES)
            encode(dst, pl.ds(start, LANES), given(own_rows(firsts, blocks, keep, came, lanes)))


def hessian_part(me_ref, wide_ref, plan, start, block):
    row_blocks, col_blocks = plan
    row = (me_ref[0] * 2 + me_ref[1]) * row_blocks + block
    lane = lax.broadcasted_iota(jnp.int32, (CB, LANES), 1) // CB
    return jnp.where(me_ref[2] * col_blocks + start // CB + lane == row, wide_ref[block], 0.0)


def base_kernel(plan, me_ref, wide_ref, keep, *rest):
    sizes, firsts, blocks, arrays = plan
    came = [rest[half * arrays : (half + 1) * arrays] for half in range(2)]
    out = rest[-1]
    for start in range(0, out.shape[1], LANES):
        lanes = pl.ds(start, LANES)
        for block, part in enumerate(own_rows(firsts, blocks, keep, came, lanes)):
            out[pl.ds(block * CB, CB), lanes] = (
                hessian_part(me_ref, wide_ref, sizes, start, block) - part
            )


def small_kernel(plan, me_ref, wide_ref, own, *rest):
    sizes, start = plan
    out = rest[-1]
    here = pl.ds(0, LANES)
    parts = gathered(own, rest[:-1], here, 0, 0, sizes[0])
    for block, part in enumerate(parts):
        out[pl.ds(block * CB, CB), :] = hessian_part(me_ref, wide_ref, sizes, start, block) - part


def finish_kernel(blocks, base, small, *rest):
    out = rest[-1]
    large = base.shape[1]
    for step in range(2):

        @pl.when(pl.program_id(0) == step)
        def rows():
            for start in range(0, large, LANES):
                lanes = pl.ds(start, LANES)
                factors = [scales(src, lanes) for src in rest[:-1]]
                for block in range(blocks // 2):
                    here = step * (blocks // 2) + block
                    total = base[pl.ds(here * CB, CB), lanes]
                    for src, scale in zip(rest[:-1], factors):
                        total = total - decode(src, lanes, scale, here)
                    out[pl.ds(block * CB, CB), lanes] = total
            lines = pl.ds(step * (blocks // 2) * CB, blocks // 2 * CB)
            out[:, pl.ds(large, LANES)] = small[lines, :]


def body(panels, curvature, visible_blocks, counts, camera_hessian):
    tiles = panels.shape[0]
    n_lm, n_cam = lax.axis_size("lm"), lax.axis_size("cam")
    chips = n_lm // 2
    halves = chips // 2
    bits = int(math.log2(chips))
    row_blocks = camera_hessian.shape[0]
    half_blocks = row_blocks // 2
    extent = row_blocks * CB
    total = row_blocks * n_lm
    col_blocks = total // n_cam
    large = col_blocks * CB - LANES
    per = large // CB
    columns = large * n_cam
    region_size = chips * half_blocks
    orders = [list(range(bits)), list(reversed(range(bits)))]
    lm, cam = lax.axis_index("lm"), lax.axis_index("cam")
    me = jnp.stack([lm // 2, lm % 2, cam]).astype(jnp.int32)

    live = jnp.arange(K, dtype=jnp.int32)[None, :] < counts[:, None]
    ids = jnp.where(live, visible_blocks, -1)

    def swap(value, step):
        return lax.ppermute(value, "lm", [(i, i ^ step) for i in range(n_lm)])

    pan_other, cur_other, ids_other = swap(panels, 1), swap(curvature, 1), swap(ids, 1)
    wide = jnp.concatenate([camera_hessian, camera_hessian], axis=-1)
    slots = jnp.arange(K, dtype=jnp.int32)[None, :, None]
    places = jnp.arange(total + 2 * region_size, dtype=jnp.int32)

    def table_of(ids):
        inner, owner = ids % col_blocks, ids // col_blocks
        spot = jnp.where(
            inner < per,
            (owner ^ cam) * per + inner,
            n_cam * per + ((owner - cam) % n_cam) * (col_blocks - per) + inner - per,
        )
        owner = ids // row_blocks
        group, block = (owner // 2) ^ (lm // 2), ids % row_blocks
        half = block // half_blocks
        index = jnp.where(half == 0, index_of(group, orders[0]), index_of(group, orders[1]))
        line = (half * halves + index % halves) * half_blocks + block % half_blocks
        line = total + line + jnp.where(index >= halves, 0, region_size)
        spot = jnp.where(ids >= 0, spot, -1)
        line = jnp.where((ids >= 0) & (owner % 2 == lm % 2), line, -1)
        found = (spot[:, :, None] == places) | (line[:, :, None] == places)
        return jnp.max(jnp.where(found, slots, -1), axis=1)

    def call(kernel, name, outs, scratch=(), **options):
        return pl.pallas_call(
            kernel,
            out_shape=outs,
            scratch_shapes=list(scratch),
            compiler_params=PARAMS,
            name=name,
            **options,
        )

    def coded(blocks, columns):
        return jax.ShapeDtypeStruct((blocks * CB + strip_of(blocks), columns), jnp.int16)

    def exact(rows, columns):
        return jax.ShapeDtypeStruct((rows, columns), jnp.float32)

    table_a, table_b = table_of(ids), table_of(ids_other)
    formed = [
        jax.ShapeDtypeStruct((tiles, 2 * region_size * CB, 2 * WIDTH), jnp.bfloat16),
        jax.ShapeDtypeStruct((tiles, 2 * (region_size + QUAD)), jnp.int32),
        jax.ShapeDtypeStruct((tiles, 2), jnp.int32),
    ]
    in_hbm = pl.BlockSpec(memory_space=pltpu.HBM)
    rows_a, line_a, many_a, pan_here = call(
        functools.partial(form_own_kernel, (total, region_size)),
        "form_own",
        formed + [jax.ShapeDtypeStruct(panels.shape, panels.dtype)],
        [pltpu.VMEM(curvature.shape, jnp.float32), pltpu.SemaphoreType.DMA((tiles + 1,))],
        in_specs=[SMEM, in_hbm, in_hbm],
        out_specs=[VMEM, SMEM, SMEM, VMEM],
    )(table_a, panels, curvature)
    rows_b, line_b, many_b = call(
        functools.partial(form_kernel, (total, region_size)),
        "form_other",
        formed,
        in_specs=[SMEM, VMEM, VMEM],
        out_specs=[VMEM, SMEM, SMEM],
    )(table_b, pan_other, cur_other)

    def scratch(pairs):
        return [
            pltpu.VMEM(((pairs + 1) * LANES, 2 * WIDTH), jnp.bfloat16),
            pltpu.SMEM((pairs + joint_of(pairs),), jnp.int32),
        ]

    def sums(kernel, name, base, pairs, regions, outs, more, tables):
        plan = (base, pairs, regions, region_size)
        side = [SMEM] * 3 + [VMEM] * 2
        return call(
            functools.partial(kernel, plan),
            name,
            outs,
            scratch(pairs) + more,
            in_specs=side * 2,
            out_specs=[VMEM] * len(outs),
        )(tables[0], line_a, many_a, pan_here, rows_a, tables[1], line_b, many_b, pan_other, rows_b)

    tables = (table_a, table_b)
    pairs = columns // LANES
    sum_shape = ((region_size + 1) * CB, columns + LANES)
    acc, to_right, to_left = sums(
        chain_kernel,
        "chain",
        n_cam * per,
        n_cam,
        [0, 1],
        [exact((2 * region_size + 1) * CB, (n_cam + 1) * LANES)]
        + [coded(2 * region_size, LANES)] * 2,
        [],
        tables,
    )
    tables = lax.optimization_barrier((tables, acc))[0]
    sends = sums(
        send_kernel,
        "send",
        0,
        pairs,
        [0],
        [coded(halves * half_blocks, columns)] * 2,
        [pltpu.VMEM(sum_shape, jnp.float32)],
        tables,
    )
    tables = lax.optimization_barrier((tables, sends))[0]

    keep, linked = None, None
    for step in range(n_cam - 1):
        from_left = lax.ppermute(to_right, "cam", [(i, i + 1) for i in range(step + 1)])
        from_right = lax.ppermute(
            to_left, "cam", [(i, i - 1) for i in range(n_cam - 1 - step, n_cam)]
        )
        if step == 0:
            from_left, from_right, sends = lax.optimization_barrier((from_left, from_right, sends))
        if step == 1:
            from_left, from_right = lax.optimization_barrier((from_left, from_right, keep))[:2]
        if step < n_cam - 2:
            groups = (n_cam - 2 - step, step + 2)
            to_right, to_left = call(
                functools.partial(link_kernel, groups),
                "link",
                [coded(2 * region_size, LANES)] * 2,
                in_specs=[VMEM] * 3,
                out_specs=[VMEM] * 2,
            )(acc, from_left, from_right)
            linked = (to_right, to_left) if step < 2 else linked
        if keep is None:
            tables = lax.optimization_barrier((tables, to_right))[0]
            (keep,) = sums(keep_kernel, "keep", 0, pairs, [1], [exact(*sum_shape)], [], tables)

    came = [[], []]
    firsts = [half * halves * half_blocks * CB for half in range(2)]
    for stage in range(bits):
        for half in range(2):
            came[half].append(swap(sends[half], 2 << orders[half][stage]))
        size = chips >> (stage + 1)
        if size == 1:
            break
        keeps = [
            lax.optimization_barrier((keep, linked))[0],
            lax.optimization_barrier((keep, from_left, from_right))[0],
        ]
        sends = [
            call(
                functools.partial(relay_kernel, (firsts[half], half_blocks, size)),
                "relay",
                coded(size // 2 * half_blocks, columns),
                in_specs=[VMEM] * (1 + len(came[half])),
                out_specs=VMEM,
            )(keeps[half], *came[half])
            for half in range(2)
        ]

    spots = [
        [place_of(spot, block, orders, half_blocks, halves) for block in range(row_blocks)]
        for spot in range(chips)
    ]
    own, *spread = call(
        functools.partial(spread_kernel, spots),
        "spread",
        [exact(extent, LANES)] + [coded(row_blocks, LANES)] * (chips - 1),
        in_specs=[VMEM] * 3,
        out_specs=[VMEM] * chips,
    )(acc, from_left, from_right)
    others = [swap(value, 2 * (pos + 1)) for pos, value in enumerate(spread)]
    near = came[0] + came[1]
    sizes = (row_blocks, col_blocks)
    crossed = call(
        functools.partial(cross_kernel, (firsts, half_blocks, bits)),
        "cross",
        [coded(row_blocks, large)] * (n_cam - 1),
        in_specs=[VMEM] * (1 + len(near)),
        out_specs=[VMEM] * (n_cam - 1),
    )(lax.optimization_barrier((keep, others))[0], *near)
    far = [
        lax.ppermute(value, "cam", [(i, i ^ (pos + 1)) for i in range(n_cam)])
        for pos, value in enumerate(crossed)
    ]
    base = call(
        functools.partial(base_kernel, (sizes, firsts, half_blocks, bits)),
        "base",
        exact(extent, large),
        in_specs=[SMEM] + [VMEM] * (2 + len(near)),
        out_specs=VMEM,
    )(me, wide, keep, *near)

    small = call(
        functools.partial(small_kernel, (sizes, large)),
        "small",
        exact(extent, LANES),
        in_specs=[SMEM] + [VMEM] * (2 + len(others)),
        out_specs=VMEM,
    )(me, wide, own, *others)
    return call(
        functools.partial(finish_kernel, row_blocks),
        "finish",
        exact(extent, col_blocks * CB),
        grid=(2,),
        in_specs=[VMEM] * (1 + n_cam),
        out_specs=pl.BlockSpec((extent // 2, col_blocks * CB), lambda step: (step, 0)),
    )(base, small, *far)


def solution(mesh):
    return jax.shard_map(
        body,
        mesh=mesh,
        in_specs=(
            P(("lm", "cam"), None, None, None),
            P(None, None, ("lm", "cam")),
            P(("lm", "cam"), None),
            P(("lm", "cam")),
            P("lm", None, None),
        ),
        out_specs=P("lm", "cam"),
        check_vma=False,
    )
```

```python
import functools
import math

import jax
import jax.numpy as jnp
from jax import lax
from jax.experimental import pallas as pl
from jax.experimental.pallas import tpu as pltpu
from jax.sharding import PartitionSpec as P

CB = 64
LMB = 128
K = 16
WIDTH = 3 * LMB
STRIP = 16
LANES = 128
WIDE = 256
VMEM = pl.BlockSpec(memory_space=pltpu.VMEM)
SMEM = pl.BlockSpec(memory_space=pltpu.SMEM)
PARAMS = pltpu.CompilerParams(vmem_limit_bytes=32 * 1024 * 1024)


def invert_rows(cur_ref, start):
    lanes = pl.ds(start, LMB)
    entry = [[cur_ref[row, col : col + 1, lanes] for col in range(3)] for row in range(3)]
    cofactor = [
        [
            entry[(row + 1) % 3][(col + 1) % 3] * entry[(row + 2) % 3][(col + 2) % 3]
            - entry[(row + 1) % 3][(col + 2) % 3] * entry[(row + 2) % 3][(col + 1) % 3]
            for col in range(3)
        ]
        for row in range(3)
    ]
    determ = (
        entry[0][0] * cofactor[0][0] + entry[0][1] * cofactor[0][1] + entry[0][2] * cofactor[0][2]
    )
    return [[cofactor[col][row] / determ for col in range(3)] for row in range(3)]


def encode(dst, lanes, parts):
    blocks = len(parts)
    row = lax.broadcasted_iota(jnp.int32, (STRIP, lanes.size), 0)
    tops = jnp.full((STRIP, lanes.size), 2.0**-100, jnp.float32)
    for block, part in enumerate(parts):
        top = jnp.max(jnp.abs(part()), axis=0, keepdims=True)
        tops = jnp.where(row == block, jnp.maximum(top, tops), tops)
    power = jnp.ceil(jnp.log2(tops) - 14.99)
    inverse = jnp.exp2(-power)
    for block, part in enumerate(parts):
        coded = jnp.floor(part() * inverse[block : block + 1] + 0.5)
        dst[pl.ds(block * CB, CB), lanes] = coded.astype(jnp.int32).astype(jnp.int16)
    dst[pl.ds(blocks * CB, STRIP), lanes] = power.astype(jnp.int32).astype(jnp.int16)


def decode(src, lanes, first, blocks):
    below = src.shape[0] - STRIP
    strip = src[pl.ds(below, STRIP), lanes].astype(jnp.int32).astype(jnp.float32)
    scale = jnp.exp2(strip)
    return [
        src[pl.ds(block * CB, CB), lanes].astype(jnp.int32).astype(jnp.float32)
        * scale[block : block + 1]
        for block in range(first, first + blocks)
    ]


def gathered(place, keep, came, lanes, blocks):
    parts = [keep[place, pl.ds(block * CB, CB), lanes] for block in range(blocks)]
    for src in came:
        here = decode(src, lanes, place * blocks, blocks)
        parts = [part + other for part, other in zip(parts, here)]
    return parts


def given(values):
    return [functools.partial(lambda value: value, value) for value in values]


def spot_of(index, order):
    bits = len(order)
    return sum(((index >> (bits - 1 - pos)) & 1) << bit for pos, bit in enumerate(order))


def form_tile(plan, table, tile, pan, cur, rows):
    total, row_blocks = plan
    inverse = invert_rows(cur, tile * LMB)

    def one_group(group, carry):
        places = [group * row_blocks + block for block in range(row_blocks)]
        slots = [table[tile, total + place] for place in places]

        @pl.when(functools.reduce(jnp.maximum, slots) >= 0)
        def some():
            for place, slot in zip(places, slots):
                lines = pl.ds(pl.multiple_of(place * CB, CB), CB)

                @pl.when(slot >= 0)
                def form():
                    wide = pan[tile, slot].astype(jnp.float32)
                    split = [wide[:, c * LMB : (c + 1) * LMB] for c in range(3)]
                    for q in range(3):
                        formed = (
                            split[0] * inverse[0][q]
                            + split[1] * inverse[1][q]
                            + split[2] * inverse[2][q]
                        )
                        high = formed.astype(jnp.bfloat16)
                        low = (formed - high.astype(jnp.float32)).astype(jnp.bfloat16)
                        at = q * LMB
                        rows[tile, lines, at : at + LMB] = high
                        rows[tile, lines, WIDTH + at : WIDTH + at + LMB] = low

                @pl.when(slot < 0)
                def blank():
                    rows[tile, lines, :] = jnp.zeros((CB, 2 * WIDTH), jnp.bfloat16)

        return carry

    lax.fori_loop(0, rows.shape[1] // (row_blocks * CB), one_group, 0)


def form_own_kernel(plan, table, pan_ref, cur_ref, rows, pan, cur, pan_sem, cur_sem):
    tiles = rows.shape[0]
    copies = [
        pltpu.make_async_copy(pan_ref.at[tile], pan.at[tile], pan_sem.at[tile])
        for tile in range(tiles)
    ]
    small = pltpu.make_async_copy(cur_ref, cur, cur_sem)
    small.start()
    for copy in copies:
        copy.start()
    small.wait()
    for tile, copy in enumerate(copies):
        copy.wait()
        form_tile(plan, table, tile, pan, cur, rows)


def form_kernel(plan, table, pan, cur, rows):
    for tile in range(rows.shape[0]):
        form_tile(plan, table, tile, pan, cur, rows)


def round_kernel(plan, table_a, table_b, pan_a, pan_b, rows_a, rows_b, *rest):
    sending, bases, orders, total, row_blocks, halves, tiles, pairs = plan
    outs, right, pair_at, acc = rest[:2], rest[2], rest[3], rest[4]
    extent = row_blocks * CB
    columns = pairs * LANES
    for base, order, out in zip(bases, orders, outs):
        acc[...] = jnp.zeros_like(acc)
        spots = [spot_of(half + (halves if sending else 0), order) for half in range(halves)]
        for table, pan, rows in ((table_a, pan_a, rows_a), (table_b, pan_b, rows_b)):

            def one_tile(tile, carry):
                used = [
                    functools.reduce(
                        jnp.maximum,
                        [
                            table[tile, total + spot * row_blocks + block]
                            for block in range(row_blocks)
                        ],
                    )
                    for spot in spots
                ]

                @pl.when(functools.reduce(jnp.maximum, used) >= 0)
                def some():
                    def one_pair(pair, count):
                        slots = [table[tile, base + 2 * pair + side] for side in range(2)]
                        live = jnp.maximum(slots[0], slots[1]) >= 0

                        @pl.when(live)
                        def stage():
                            pair_at[count] = pair * LANES
                            for side, slot in enumerate(slots):
                                first = pl.multiple_of(count * LANES + side * CB, CB)
                                lines = pl.ds(first, CB)

                                @pl.when(slot >= 0)
                                def fill():
                                    panel = pan[tile, slot]
                                    right[lines, :WIDTH] = panel
                                    right[lines, WIDTH:] = panel

                                @pl.when(slot < 0)
                                def blank():
                                    right[lines, :] = jnp.zeros((CB, 2 * WIDTH), jnp.bfloat16)

                        return count + jnp.where(live, 1, 0)

                    count = lax.fori_loop(0, pairs, one_pair, jnp.int32(0))
                    pair_at[count] = columns

                    def one_dot(double, carry):
                        first = pl.multiple_of(double * 2 * LANES, 2 * LANES)
                        for half, spot in enumerate(spots):

                            @pl.when(used[half] >= 0)
                            def add():
                                result = lax.dot_general(
                                    rows[tile, spot * extent : (spot + 1) * extent, :],
                                    right[pl.ds(first, 2 * LANES), :],
                                    (((1,), (1,)), ((), ())),
                                    preferred_element_type=jnp.float32,
                                )
                                for side in range(2):
                                    at = pl.multiple_of(pair_at[2 * double + side], LANES)
                                    acc[half, :, pl.ds(at, LANES)] += result[
                                        :, side * LANES : (side + 1) * LANES
                                    ]

                        return carry

                    lax.fori_loop(0, (count + 1) // 2, one_dot, 0)

                return carry

            lax.fori_loop(0, tiles, one_tile, 0)

        def store(start, carry):
            lanes = pl.ds(pl.multiple_of(start * WIDE, WIDE), WIDE)
            if sending:
                parts = [
                    functools.partial(
                        lambda half, block: acc[half, pl.ds(block * CB, CB), lanes], half, block
                    )
                    for half in range(halves)
                    for block in range(row_blocks)
                ]
                encode(out, lanes, parts)
            else:
                for half in range(halves):
                    out[half, :, lanes] = acc[half, :, lanes]
            return carry

        lax.fori_loop(0, columns // WIDE, store, 0)


def relay_kernel(plan, keep, *rest):
    row_blocks, size = plan
    dst = rest[-1]

    def code(start, carry):
        lanes = pl.ds(pl.multiple_of(start * WIDE, WIDE), WIDE)
        parts = []
        for place in range(size // 2, size):
            parts += given(gathered(place, keep, rest[:-1], lanes, row_blocks))
        encode(dst, lanes, parts)
        return carry

    lax.fori_loop(0, dst.shape[1] // WIDE, code, 0)


def cross_kernel(row_blocks, group, arrays, *rest):
    dsts = rest[2 * arrays :]
    for other, dst in enumerate(dsts):
        for start in range(0, group, LANES):
            parts = []
            for piece in range(2):
                keep, *came = rest[piece * arrays : (piece + 1) * arrays]
                lanes = pl.ds((other + 1) * group + start, LANES)
                parts += given(gathered(0, keep, came, lanes, row_blocks))
            encode(dst, pl.ds(start, LANES), parts)


def base_kernel(plan, me_ref, wide_ref, *rest):
    turn, row_blocks, col_blocks, arrays = plan
    out_ref = rest[-1]
    group = out_ref.shape[1] // 2
    first_row = (me_ref[0] * 2 + me_ref[1]) * row_blocks
    first_col = me_ref[2] * col_blocks
    lane = lax.broadcasted_iota(jnp.int32, (CB, LANES), 1) // CB
    for piece in range(2):
        keep, *came = rest[piece * arrays : (piece + 1) * arrays]
        for start in range(0, group, LANES):
            parts = gathered(0, keep, came, pl.ds(start, LANES), row_blocks)
            base = first_col + ((2 * turn + piece) * group + start) // CB
            for block in range(row_blocks):
                wide = jnp.where(base + lane == first_row + block, wide_ref[block], 0.0)
                out_ref[pl.ds(block * CB, CB), pl.ds(piece * group + start, LANES)] = (
                    wide - parts[block]
                )


def finish_kernel(row_blocks, far, base_ref, *rest):
    out_ref = rest[-1]
    group = out_ref.shape[1] // 2
    for piece in range(2):
        for start in range(0, group, LANES):
            total = [0.0] * row_blocks
            for src in rest[:far]:
                parts = decode(src, pl.ds(start, LANES), piece * row_blocks, row_blocks)
                total = [left + right for left, right in zip(total, parts)]
            lanes = pl.ds(piece * group + start, LANES)
            for block in range(row_blocks):
                lines = pl.ds(block * CB, CB)
                out_ref[lines, lanes] = base_ref[lines, lanes] - total[block]


def body(panels, curvature, visible_blocks, counts, camera_hessian):
    tiles = panels.shape[0]
    n_lm, n_cam = lax.axis_size("lm"), lax.axis_size("cam")
    chips = n_lm // 2
    bits = int(math.log2(chips))
    row_blocks = camera_hessian.shape[0]
    extent = row_blocks * CB
    col_blocks = row_blocks * n_lm // n_cam
    turns = col_blocks * CB // (2 * LANES)
    pieces = 2 * turns
    group = col_blocks * CB // pieces
    columns = group * n_cam
    total = row_blocks * n_lm
    orders = [list(range(bits)), list(reversed(range(bits)))]
    lm, cam = lax.axis_index("lm"), lax.axis_index("cam")
    me = jnp.stack([lm // 2, lm % 2, cam]).astype(jnp.int32)

    live = jnp.arange(K, dtype=jnp.int32)[None, :] < counts[:, None]
    ids = jnp.where(live, visible_blocks, -1)

    def swap(value, bit):
        return lax.ppermute(value, "lm", [(i, i ^ (1 << bit)) for i in range(n_lm)])

    pan_other, cur_other, ids_other = swap(panels, 0), swap(curvature, 0), swap(ids, 0)
    wide = jnp.concatenate([camera_hessian, camera_hessian], axis=-1)
    per = group // CB
    slots = jnp.arange(K, dtype=jnp.int32)[None, :, None]
    places = jnp.arange(total + chips * row_blocks, dtype=jnp.int32)

    def table_of(ids):
        inner = ids % col_blocks
        spot = ((inner // per) * n_cam + ((ids // col_blocks) ^ cam)) * per + inner % per
        owner = ids // row_blocks
        line = total + ((owner // 2) ^ (lm // 2)) * row_blocks + ids % row_blocks
        spot = jnp.where(ids >= 0, spot, -1)
        line = jnp.where((ids >= 0) & (owner % 2 == lm % 2), line, -1)
        found = (spot[:, :, None] == places) | (line[:, :, None] == places)
        return jnp.max(jnp.where(found, slots, -1), axis=1)

    table_a, table_b = table_of(ids), table_of(ids_other)
    formed = jax.ShapeDtypeStruct((tiles, chips * extent, 2 * WIDTH), jnp.bfloat16)
    whole = pl.BlockSpec(memory_space=pltpu.HBM)
    rows_a, pan_here = pl.pallas_call(
        functools.partial(form_own_kernel, (total, row_blocks)),
        in_specs=[SMEM, whole, whole],
        out_specs=[VMEM, VMEM],
        out_shape=[formed, jax.ShapeDtypeStruct(panels.shape, panels.dtype)],
        scratch_shapes=[
            pltpu.VMEM(curvature.shape, jnp.float32),
            pltpu.SemaphoreType.DMA((tiles,)),
            pltpu.SemaphoreType.DMA,
        ],
        compiler_params=PARAMS,
        name="form_own",
    )(table_a, panels, curvature)
    rows_b = pl.pallas_call(
        functools.partial(form_kernel, (total, row_blocks)),
        in_specs=[SMEM, VMEM, VMEM],
        out_specs=VMEM,
        out_shape=formed,
        compiler_params=PARAMS,
        name="form_other",
    )(table_b, pan_other, cur_other)

    def round_call(sending, turn, tables):
        if sending:
            made = jax.ShapeDtypeStruct((chips // 2 * extent + STRIP, columns), jnp.int16)
        else:
            made = jax.ShapeDtypeStruct((chips // 2, extent, columns), jnp.float32)
        bases = [(2 * turn + which) * n_cam * per for which in range(2)]
        pairs = columns // LANES
        plan = (sending, bases, orders, total, row_blocks, chips // 2, tiles, pairs)
        return pl.pallas_call(
            functools.partial(round_kernel, plan),
            in_specs=[SMEM] * 2 + [VMEM] * 4,
            out_specs=[VMEM] * 2,
            out_shape=[made] * 2,
            scratch_shapes=[
                pltpu.VMEM((columns + LANES, 2 * WIDTH), jnp.bfloat16),
                pltpu.SMEM((pairs + 1,), jnp.int32),
                pltpu.VMEM((chips // 2, extent, columns + LANES), jnp.float32),
            ],
            compiler_params=PARAMS,
            name="send" if sending else "keep",
        )(*tables, pan_here, pan_other, rows_a, rows_b)

    tables = (table_a, table_b)
    sends, keeps = [], []
    for turn in range(turns):
        for sending, made in ((True, sends), (False, keeps)):
            made.append(list(round_call(sending, turn, tables)))
            tables = lax.optimization_barrier((tables, made[-1]))[0]

    came = [[[], []] for _ in range(turns)]
    result = None
    for turn in range(turns):
        if turn:
            sends[turn] = lax.optimization_barrier((sends[turn], crossed))[0]
        for stage in range(bits):
            for piece in range(2):
                came[turn][piece].append(swap(sends[turn][piece], orders[piece][stage] + 1))
            size = chips >> (stage + 1)
            if size == 1:
                break
            for piece in range(2):
                keep = keeps[turn][piece]
                if turn:
                    keep = lax.optimization_barrier((keep, far))[0]
                arrays = [keep] + came[turn][piece]
                sends[turn][piece] = pl.pallas_call(
                    functools.partial(relay_kernel, (row_blocks, size)),
                    in_specs=[VMEM] * len(arrays),
                    out_specs=VMEM,
                    out_shape=jax.ShapeDtypeStruct((size // 2 * extent + STRIP, columns), jnp.int16),
                    compiler_params=PARAMS,
                    name="relay",
                )(*arrays)

        near = [array for piece in range(2) for array in [keeps[turn][piece]] + came[turn][piece]]
        arrays = len(near) // 2
        crossed = pl.pallas_call(
            functools.partial(cross_kernel, row_blocks, group, arrays),
            in_specs=[VMEM] * len(near),
            out_specs=[VMEM] * (n_cam - 1),
            out_shape=[jax.ShapeDtypeStruct((2 * extent + STRIP, group), jnp.int16)] * (n_cam - 1),
            compiler_params=PARAMS,
            name="cross",
        )(*near)
        far = [
            lax.ppermute(value, "cam", [(i, i ^ (pos + 1)) for i in range(n_cam)])
            for pos, value in enumerate(crossed)
        ]
        base = pl.pallas_call(
            functools.partial(base_kernel, (turn, row_blocks, col_blocks, arrays)),
            in_specs=[SMEM, VMEM] + [VMEM] * len(near),
            out_specs=VMEM,
            out_shape=jax.ShapeDtypeStruct((extent, 2 * group), jnp.float32),
            compiler_params=PARAMS,
            name="base",
        )(me, wide, *near)
        before = [] if result is None else [result]
        result = pl.pallas_call(
            functools.partial(finish_kernel, row_blocks, n_cam - 1),
            grid=(1,),
            in_specs=[VMEM] * n_cam + [pl.BlockSpec(memory_space=pl.ANY)] * len(before),
            out_specs=pl.BlockSpec((extent, 2 * group), lambda step, turn=turn: (0, turn)),
            out_shape=jax.ShapeDtypeStruct((extent, col_blocks * CB), jnp.float32),
            input_output_aliases={n_cam: 0} if before else {},
            compiler_params=PARAMS,
            name="finish",
        )(base, *far, *before)
    return result


def solution(mesh):
    return jax.shard_map(
        body,
        mesh=mesh,
        in_specs=(
            P(("lm", "cam"), None, None, None),
            P(None, None, ("lm", "cam")),
            P(("lm", "cam"), None),
            P(("lm", "cam")),
            P("lm", None, None),
        ),
        out_specs=P("lm", "cam"),
        check_vma=False,
    )
```

```python
import functools
import math

import jax
import jax.numpy as jnp
from jax import lax
from jax.experimental import pallas as pl
from jax.experimental.pallas import tpu as pltpu
from jax.sharding import PartitionSpec as P

CB = 64
LMB = 128
K = 16
WIDTH = 3 * LMB
STRIP = 16
LANES = 128
WIDE = 256
VMEM = pl.BlockSpec(memory_space=pltpu.VMEM)
SMEM = pl.BlockSpec(memory_space=pltpu.SMEM)
PARAMS = pltpu.CompilerParams(vmem_limit_bytes=32 * 1024 * 1024)


def invert_rows(cur_ref, start):
    lanes = pl.ds(start, LMB)
    entry = [[cur_ref[row, col : col + 1, lanes] for col in range(3)] for row in range(3)]
    cofactor = [
        [
            entry[(row + 1) % 3][(col + 1) % 3] * entry[(row + 2) % 3][(col + 2) % 3]
            - entry[(row + 1) % 3][(col + 2) % 3] * entry[(row + 2) % 3][(col + 1) % 3]
            for col in range(3)
        ]
        for row in range(3)
    ]
    determ = (
        entry[0][0] * cofactor[0][0] + entry[0][1] * cofactor[0][1] + entry[0][2] * cofactor[0][2]
    )
    return [[cofactor[col][row] / determ for col in range(3)] for row in range(3)]


def encode(dst, lanes, parts):
    blocks = len(parts)
    row = lax.broadcasted_iota(jnp.int32, (STRIP, lanes.size), 0)
    tops = jnp.full((STRIP, lanes.size), 2.0**-100, jnp.float32)
    for block, part in enumerate(parts):
        top = jnp.max(jnp.abs(part()), axis=0, keepdims=True)
        tops = jnp.where(row == block, jnp.maximum(top, tops), tops)
    power = jnp.ceil(jnp.log2(tops) - 14.99)
    inverse = jnp.exp2(-power)
    for block, part in enumerate(parts):
        coded = jnp.floor(part() * inverse[block : block + 1] + 0.5)
        dst[pl.ds(block * CB, CB), lanes] = coded.astype(jnp.int32).astype(jnp.int16)
    dst[pl.ds(blocks * CB, STRIP), lanes] = power.astype(jnp.int32).astype(jnp.int16)


def decode(src, lanes, first, blocks):
    below = src.shape[0] - STRIP
    strip = src[pl.ds(below, STRIP), lanes].astype(jnp.int32).astype(jnp.float32)
    scale = jnp.exp2(strip)
    return [
        src[pl.ds(block * CB, CB), lanes].astype(jnp.int32).astype(jnp.float32)
        * scale[block : block + 1]
        for block in range(first, first + blocks)
    ]


def gathered(place, keep, came, lanes, blocks):
    parts = [keep[place, pl.ds(block * CB, CB), lanes] for block in range(blocks)]
    for src in came:
        here = decode(src, lanes, place * blocks, blocks)
        parts = [part + other for part, other in zip(parts, here)]
    return parts


def given(values):
    return [functools.partial(lambda value: value, value) for value in values]


def spot_of(index, order):
    bits = len(order)
    return sum(((index >> (bits - 1 - pos)) & 1) << bit for pos, bit in enumerate(order))


def form_tile(plan, table, tile, pan, cur, rows):
    total, row_blocks = plan
    inverse = invert_rows(cur, tile * LMB)

    def one_group(group, carry):
        places = [group * row_blocks + block for block in range(row_blocks)]
        slots = [table[tile, total + place] for place in places]

        @pl.when(functools.reduce(jnp.maximum, slots) >= 0)
        def some():
            for place, slot in zip(places, slots):
                lines = pl.ds(pl.multiple_of(place * CB, CB), CB)

                @pl.when(slot >= 0)
                def form():
                    wide = pan[tile, slot].astype(jnp.float32)
                    split = [wide[:, c * LMB : (c + 1) * LMB] for c in range(3)]
                    for q in range(3):
                        formed = (
                            split[0] * inverse[0][q]
                            + split[1] * inverse[1][q]
                            + split[2] * inverse[2][q]
                        )
                        high = formed.astype(jnp.bfloat16)
                        low = (formed - high.astype(jnp.float32)).astype(jnp.bfloat16)
                        at = q * LMB
                        rows[tile, lines, at : at + LMB] = high
                        rows[tile, lines, WIDTH + at : WIDTH + at + LMB] = low

                @pl.when(slot < 0)
                def blank():
                    rows[tile, lines, :] = jnp.zeros((CB, 2 * WIDTH), jnp.bfloat16)

        return carry

    lax.fori_loop(0, rows.shape[1] // (row_blocks * CB), one_group, 0)


def form_own_kernel(plan, table, pan_ref, cur_ref, rows, pan, cur, pan_sem, cur_sem):
    tiles = rows.shape[0]
    copies = [
        pltpu.make_async_copy(pan_ref.at[tile], pan.at[tile], pan_sem.at[tile])
        for tile in range(tiles)
    ]
    small = pltpu.make_async_copy(cur_ref, cur, cur_sem)
    small.start()
    for copy in copies:
        copy.start()
    small.wait()
    for tile, copy in enumerate(copies):
        copy.wait()
        form_tile(plan, table, tile, pan, cur, rows)


def form_kernel(plan, table, pan, cur, rows):
    for tile in range(rows.shape[0]):
        form_tile(plan, table, tile, pan, cur, rows)


def round_kernel(plan, table_a, table_b, pan_a, pan_b, rows_a, rows_b, *rest):
    sending, bases, orders, total, row_blocks, halves, tiles, pairs = plan
    outs, right, pair_at, acc = rest[:2], rest[2], rest[3], rest[4]
    extent = row_blocks * CB
    columns = pairs * LANES
    for base, order, out in zip(bases, orders, outs):
        acc[...] = jnp.zeros_like(acc)
        spots = [spot_of(half + (halves if sending else 0), order) for half in range(halves)]
        for table, pan, rows in ((table_a, pan_a, rows_a), (table_b, pan_b, rows_b)):

            def one_tile(tile, carry):
                used = [
                    functools.reduce(
                        jnp.maximum,
                        [
                            table[tile, total + spot * row_blocks + block]
                            for block in range(row_blocks)
                        ],
                    )
                    for spot in spots
                ]

                @pl.when(functools.reduce(jnp.maximum, used) >= 0)
                def some():
                    def one_pair(pair, count):
                        slots = [table[tile, base + 2 * pair + side] for side in range(2)]
                        live = jnp.maximum(slots[0], slots[1]) >= 0

                        @pl.when(live)
                        def stage():
                            pair_at[count] = pair * LANES
                            for side, slot in enumerate(slots):
                                first = pl.multiple_of(count * LANES + side * CB, CB)
                                lines = pl.ds(first, CB)

                                @pl.when(slot >= 0)
                                def fill():
                                    panel = pan[tile, slot]
                                    right[lines, :WIDTH] = panel
                                    right[lines, WIDTH:] = panel

                                @pl.when(slot < 0)
                                def blank():
                                    right[lines, :] = jnp.zeros((CB, 2 * WIDTH), jnp.bfloat16)

                        return count + jnp.where(live, 1, 0)

                    count = lax.fori_loop(0, pairs, one_pair, jnp.int32(0))
                    pair_at[count] = columns

                    def one_dot(double, carry):
                        first = pl.multiple_of(double * 2 * LANES, 2 * LANES)
                        for half, spot in enumerate(spots):

                            @pl.when(used[half] >= 0)
                            def add():
                                result = lax.dot_general(
                                    rows[tile, spot * extent : (spot + 1) * extent, :],
                                    right[pl.ds(first, 2 * LANES), :],
                                    (((1,), (1,)), ((), ())),
                                    preferred_element_type=jnp.float32,
                                )
                                for side in range(2):
                                    at = pl.multiple_of(pair_at[2 * double + side], LANES)
                                    acc[half, :, pl.ds(at, LANES)] += result[
                                        :, side * LANES : (side + 1) * LANES
                                    ]

                        return carry

                    lax.fori_loop(0, (count + 1) // 2, one_dot, 0)

                return carry

            lax.fori_loop(0, tiles, one_tile, 0)

        def store(start, carry):
            lanes = pl.ds(pl.multiple_of(start * WIDE, WIDE), WIDE)
            if sending:
                parts = [
                    functools.partial(
                        lambda half, block: acc[half, pl.ds(block * CB, CB), lanes], half, block
                    )
                    for half in range(halves)
                    for block in range(row_blocks)
                ]
                encode(out, lanes, parts)
            else:
                for half in range(halves):
                    out[half, :, lanes] = acc[half, :, lanes]
            return carry

        lax.fori_loop(0, columns // WIDE, store, 0)


def relay_kernel(plan, keep, *rest):
    row_blocks, size = plan
    dst = rest[-1]

    def code(start, carry):
        lanes = pl.ds(pl.multiple_of(start * WIDE, WIDE), WIDE)
        parts = []
        for place in range(size // 2, size):
            parts += given(gathered(place, keep, rest[:-1], lanes, row_blocks))
        encode(dst, lanes, parts)
        return carry

    lax.fori_loop(0, dst.shape[1] // WIDE, code, 0)


def cross_kernel(row_blocks, group, arrays, *rest):
    dsts = rest[2 * arrays :]
    for other, dst in enumerate(dsts):
        for start in range(0, group, LANES):
            parts = []
            for piece in range(2):
                keep, *came = rest[piece * arrays : (piece + 1) * arrays]
                lanes = pl.ds((other + 1) * group + start, LANES)
                parts += given(gathered(0, keep, came, lanes, row_blocks))
            encode(dst, pl.ds(start, LANES), parts)


def cross_all_kernel(row_blocks, group, arrays, me_ref, *rest):
    out = rest[-1]
    out[me_ref[2]] = jnp.zeros(out.shape[1:], jnp.int16)
    for other in range(out.shape[0] - 1):
        dst = out.at[me_ref[2] ^ (other + 1)]
        for start in range(0, group, LANES):
            parts = []
            for piece in range(2):
                keep, *came = rest[piece * arrays : (piece + 1) * arrays]
                lanes = pl.ds((other + 1) * group + start, LANES)
                parts += given(gathered(0, keep, came, lanes, row_blocks))
            encode(dst, pl.ds(start, LANES), parts)


def base_kernel(plan, me_ref, wide_ref, *rest):
    turn, row_blocks, col_blocks, arrays = plan
    out_ref = rest[-1]
    group = out_ref.shape[1] // 2
    first_row = (me_ref[0] * 2 + me_ref[1]) * row_blocks
    first_col = me_ref[2] * col_blocks
    lane = lax.broadcasted_iota(jnp.int32, (CB, LANES), 1) // CB
    for piece in range(2):
        keep, *came = rest[piece * arrays : (piece + 1) * arrays]
        for start in range(0, group, LANES):
            parts = gathered(0, keep, came, pl.ds(start, LANES), row_blocks)
            base = first_col + ((2 * turn + piece) * group + start) // CB
            for block in range(row_blocks):
                wide = jnp.where(base + lane == first_row + block, wide_ref[block], 0.0)
                out_ref[pl.ds(block * CB, CB), pl.ds(piece * group + start, LANES)] = (
                    wide - parts[block]
                )


def finish_kernel(row_blocks, far, base_ref, *rest):
    out_ref = rest[-1]
    group = out_ref.shape[1] // 2
    for piece in range(2):
        for start in range(0, group, LANES):
            total = [0.0] * row_blocks
            for src in rest[:far]:
                parts = decode(src, pl.ds(start, LANES), piece * row_blocks, row_blocks)
                total = [left + right for left, right in zip(total, parts)]
            lanes = pl.ds(piece * group + start, LANES)
            for block in range(row_blocks):
                lines = pl.ds(block * CB, CB)
                out_ref[lines, lanes] = base_ref[lines, lanes] - total[block]


def finish_all_kernel(row_blocks, me_ref, base_ref, all_ref, *rest):
    far = [all_ref.at[me_ref[2] ^ (other + 1)] for other in range(all_ref.shape[0] - 1)]
    out_ref = rest[-1]
    group = out_ref.shape[1] // 2
    for piece in range(2):
        for start in range(0, group, LANES):
            total = [0.0] * row_blocks
            for src in far:
                parts = decode(src, pl.ds(start, LANES), piece * row_blocks, row_blocks)
                total = [left + right for left, right in zip(total, parts)]
            lanes = pl.ds(piece * group + start, LANES)
            for block in range(row_blocks):
                lines = pl.ds(block * CB, CB)
                out_ref[lines, lanes] = base_ref[lines, lanes] - total[block]


def body(panels, curvature, visible_blocks, counts, camera_hessian):
    tiles = panels.shape[0]
    n_lm, n_cam = lax.axis_size("lm"), lax.axis_size("cam")
    chips = n_lm // 2
    bits = int(math.log2(chips))
    row_blocks = camera_hessian.shape[0]
    extent = row_blocks * CB
    col_blocks = row_blocks * n_lm // n_cam
    turns = col_blocks * CB // (2 * LANES)
    pieces = 2 * turns
    group = col_blocks * CB // pieces
    columns = group * n_cam
    total = row_blocks * n_lm
    orders = [list(range(bits)), list(reversed(range(bits)))]
    lm, cam = lax.axis_index("lm"), lax.axis_index("cam")
    me = jnp.stack([lm // 2, lm % 2, cam]).astype(jnp.int32)

    live = jnp.arange(K, dtype=jnp.int32)[None, :] < counts[:, None]
    ids = jnp.where(live, visible_blocks, -1)

    def swap(value, bit):
        return lax.ppermute(value, "lm", [(i, i ^ (1 << bit)) for i in range(n_lm)])

    pan_other, cur_other, ids_other = swap(panels, 0), swap(curvature, 0), swap(ids, 0)
    wide = jnp.concatenate([camera_hessian, camera_hessian], axis=-1)
    per = group // CB
    slots = jnp.arange(K, dtype=jnp.int32)[None, :, None]
    places = jnp.arange(total + chips * row_blocks, dtype=jnp.int32)

    def table_of(ids):
        inner = ids % col_blocks
        spot = ((inner // per) * n_cam + ((ids // col_blocks) ^ cam)) * per + inner % per
        owner = ids // row_blocks
        line = total + ((owner // 2) ^ (lm // 2)) * row_blocks + ids % row_blocks
        spot = jnp.where(ids >= 0, spot, -1)
        line = jnp.where((ids >= 0) & (owner % 2 == lm % 2), line, -1)
        found = (spot[:, :, None] == places) | (line[:, :, None] == places)
        return jnp.max(jnp.where(found, slots, -1), axis=1)

    table_a, table_b = table_of(ids), table_of(ids_other)
    formed = jax.ShapeDtypeStruct((tiles, chips * extent, 2 * WIDTH), jnp.bfloat16)
    whole = pl.BlockSpec(memory_space=pltpu.HBM)
    rows_a, pan_here = pl.pallas_call(
        functools.partial(form_own_kernel, (total, row_blocks)),
        in_specs=[SMEM, whole, whole],
        out_specs=[VMEM, VMEM],
        out_shape=[formed, jax.ShapeDtypeStruct(panels.shape, panels.dtype)],
        scratch_shapes=[
            pltpu.VMEM(curvature.shape, jnp.float32),
            pltpu.SemaphoreType.DMA((tiles,)),
            pltpu.SemaphoreType.DMA,
        ],
        compiler_params=PARAMS,
        name="form_own",
    )(table_a, panels, curvature)
    rows_b = pl.pallas_call(
        functools.partial(form_kernel, (total, row_blocks)),
        in_specs=[SMEM, VMEM, VMEM],
        out_specs=VMEM,
        out_shape=formed,
        compiler_params=PARAMS,
        name="form_other",
    )(table_b, pan_other, cur_other)

    def round_call(sending, turn, tables):
        if sending:
            made = jax.ShapeDtypeStruct((chips // 2 * extent + STRIP, columns), jnp.int16)
        else:
            made = jax.ShapeDtypeStruct((chips // 2, extent, columns), jnp.float32)
        bases = [(2 * turn + which) * n_cam * per for which in range(2)]
        pairs = columns // LANES
        plan = (sending, bases, orders, total, row_blocks, chips // 2, tiles, pairs)
        return pl.pallas_call(
            functools.partial(round_kernel, plan),
            in_specs=[SMEM] * 2 + [VMEM] * 4,
            out_specs=[VMEM] * 2,
            out_shape=[made] * 2,
            scratch_shapes=[
                pltpu.VMEM((columns + LANES, 2 * WIDTH), jnp.bfloat16),
                pltpu.SMEM((pairs + 1,), jnp.int32),
                pltpu.VMEM((chips // 2, extent, columns + LANES), jnp.float32),
            ],
            compiler_params=PARAMS,
            name="send" if sending else "keep",
        )(*tables, pan_here, pan_other, rows_a, rows_b)

    tables = (table_a, table_b)
    sends, keeps = [], []
    for turn in range(turns):
        for sending, made in ((True, sends), (False, keeps)):
            made.append(list(round_call(sending, turn, tables)))
            tables = lax.optimization_barrier((tables, made[-1]))[0]

    came = [[[], []] for _ in range(turns)]
    result = None
    for turn in range(turns):
        if turn:
            sends[turn] = lax.optimization_barrier((sends[turn], crossed))[0]
        for stage in range(bits):
            for piece in range(2):
                came[turn][piece].append(swap(sends[turn][piece], orders[piece][stage] + 1))
            size = chips >> (stage + 1)
            if size == 1:
                break
            for piece in range(2):
                keep = keeps[turn][piece]
                if turn:
                    keep = lax.optimization_barrier((keep, far))[0]
                arrays = [keep] + came[turn][piece]
                sends[turn][piece] = pl.pallas_call(
                    functools.partial(relay_kernel, (row_blocks, size)),
                    in_specs=[VMEM] * len(arrays),
                    out_specs=VMEM,
                    out_shape=jax.ShapeDtypeStruct((size // 2 * extent + STRIP, columns), jnp.int16),
                    compiler_params=PARAMS,
                    name="relay",
                )(*arrays)

        near = [array for piece in range(2) for array in [keeps[turn][piece]] + came[turn][piece]]
        arrays = len(near) // 2
        part = (2 * extent + STRIP, group)
        last = turn == turns - 1
        if last:
            crossed = pl.pallas_call(
                functools.partial(cross_all_kernel, row_blocks, group, arrays),
                in_specs=[SMEM] + [VMEM] * len(near),
                out_specs=VMEM,
                out_shape=jax.ShapeDtypeStruct((n_cam, *part), jnp.int16),
                compiler_params=PARAMS,
                name="cross_all",
            )(me, *near)
            far = [lax.all_to_all(crossed, "cam", 0, 0, tiled=True)]
        else:
            crossed = pl.pallas_call(
                functools.partial(cross_kernel, row_blocks, group, arrays),
                in_specs=[VMEM] * len(near),
                out_specs=[VMEM] * (n_cam - 1),
                out_shape=[jax.ShapeDtypeStruct((2 * extent + STRIP, group), jnp.int16)] * (n_cam - 1),
                compiler_params=PARAMS,
                name="cross",
            )(*near)
            far = [
                lax.ppermute(value, "cam", [(i, i ^ (pos + 1)) for i in range(n_cam)])
                for pos, value in enumerate(crossed)
            ]
        base = pl.pallas_call(
            functools.partial(base_kernel, (turn, row_blocks, col_blocks, arrays)),
            in_specs=[SMEM, VMEM] + [VMEM] * len(near),
            out_specs=VMEM,
            out_shape=jax.ShapeDtypeStruct((extent, 2 * group), jnp.float32),
            compiler_params=PARAMS,
            name="base",
        )(me, wide, *near)
        before = [] if result is None else [result]
        result = pl.pallas_call(
            functools.partial(finish_all_kernel, row_blocks)
            if last
            else functools.partial(finish_kernel, row_blocks, n_cam - 1),
            grid=(1,),
            in_specs=[SMEM] * last
            + [VMEM] * (1 + len(far))
            + [pl.BlockSpec(memory_space=pl.ANY)] * len(before),
            out_specs=pl.BlockSpec((extent, 2 * group), lambda step, turn=turn: (0, turn)),
            out_shape=jax.ShapeDtypeStruct((extent, col_blocks * CB), jnp.float32),
            input_output_aliases={1 + last + len(far): 0} if before else {},
            compiler_params=PARAMS,
            name="finish",
        )(*[me] * last, base, *far, *before)
    return result


def solution(mesh):
    return jax.shard_map(
        body,
        mesh=mesh,
        in_specs=(
            P(("lm", "cam"), None, None, None),
            P(None, None, ("lm", "cam")),
            P(("lm", "cam"), None),
            P(("lm", "cam")),
            P("lm", None, None),
        ),
        out_specs=P("lm", "cam"),
        check_vma=False,
    )
```

```python
import functools
import math

import jax
import jax.numpy as jnp
from jax import lax
from jax.experimental import pallas as pl
from jax.experimental.pallas import tpu as pltpu
from jax.sharding import PartitionSpec as P

CB = 64
LMB = 128
K = 16
WIDTH = 3 * LMB
STRIP = 16
LANES = 128
WIDE = 256
VMEM = pl.BlockSpec(memory_space=pltpu.VMEM)
SMEM = pl.BlockSpec(memory_space=pltpu.SMEM)
PARAMS = pltpu.CompilerParams(vmem_limit_bytes=32 * 1024 * 1024)


def invert_rows(cur_ref, start):
    lanes = pl.ds(start, LMB)
    entry = [[cur_ref[row, col : col + 1, lanes] for col in range(3)] for row in range(3)]
    cofactor = [
        [
            entry[(row + 1) % 3][(col + 1) % 3] * entry[(row + 2) % 3][(col + 2) % 3]
            - entry[(row + 1) % 3][(col + 2) % 3] * entry[(row + 2) % 3][(col + 1) % 3]
            for col in range(3)
        ]
        for row in range(3)
    ]
    determ = (
        entry[0][0] * cofactor[0][0] + entry[0][1] * cofactor[0][1] + entry[0][2] * cofactor[0][2]
    )
    return [[cofactor[col][row] / determ for col in range(3)] for row in range(3)]


def encode(dst, lanes, parts):
    blocks = len(parts)
    row = lax.broadcasted_iota(jnp.int32, (STRIP, lanes.size), 0)
    tops = jnp.full((STRIP, lanes.size), 2.0**-100, jnp.float32)
    for block, part in enumerate(parts):
        top = jnp.max(jnp.abs(part()), axis=0, keepdims=True)
        tops = jnp.where(row == block, jnp.maximum(top, tops), tops)
    power = jnp.ceil(jnp.log2(tops) - 14.99)
    inverse = jnp.exp2(-power)
    for block, part in enumerate(parts):
        coded = jnp.floor(part() * inverse[block : block + 1] + 0.5)
        dst[pl.ds(block * CB, CB), lanes] = coded.astype(jnp.int32).astype(jnp.int16)
    dst[pl.ds(blocks * CB, STRIP), lanes] = power.astype(jnp.int32).astype(jnp.int16)


def decode(src, lanes, first, blocks):
    below = src.shape[0] - STRIP
    strip = src[pl.ds(below, STRIP), lanes].astype(jnp.int32).astype(jnp.float32)
    scale = jnp.exp2(strip)
    return [
        src[pl.ds(block * CB, CB), lanes].astype(jnp.int32).astype(jnp.float32)
        * scale[block : block + 1]
        for block in range(first, first + blocks)
    ]


def gathered(place, keep, came, lanes, blocks):
    parts = [keep[place, pl.ds(block * CB, CB), lanes] for block in range(blocks)]
    for src in came:
        here = decode(src, lanes, place * blocks, blocks)
        parts = [part + other for part, other in zip(parts, here)]
    return parts


def given(values):
    return [functools.partial(lambda value: value, value) for value in values]


def spot_of(index, order):
    bits = len(order)
    return sum(((index >> (bits - 1 - pos)) & 1) << bit for pos, bit in enumerate(order))


def form_tile(plan, table, tile, pan, cur, rows):
    total, row_blocks = plan
    inverse = invert_rows(cur, tile * LMB)

    def one_group(group, carry):
        places = [group * row_blocks + block for block in range(row_blocks)]
        slots = [table[tile, total + place] for place in places]

        @pl.when(functools.reduce(jnp.maximum, slots) >= 0)
        def some():
            for place, slot in zip(places, slots):
                lines = pl.ds(pl.multiple_of(place * CB, CB), CB)

                @pl.when(slot >= 0)
                def form():
                    wide = pan[tile, slot].astype(jnp.float32)
                    split = [wide[:, c * LMB : (c + 1) * LMB] for c in range(3)]
                    for q in range(3):
                        formed = (
                            split[0] * inverse[0][q]
                            + split[1] * inverse[1][q]
                            + split[2] * inverse[2][q]
                        )
                        high = formed.astype(jnp.bfloat16)
                        low = (formed - high.astype(jnp.float32)).astype(jnp.bfloat16)
                        at = q * LMB
                        rows[tile, lines, at : at + LMB] = high
                        rows[tile, lines, WIDTH + at : WIDTH + at + LMB] = low

                @pl.when(slot < 0)
                def blank():
                    rows[tile, lines, :] = jnp.zeros((CB, 2 * WIDTH), jnp.bfloat16)

        return carry

    lax.fori_loop(0, rows.shape[1] // (row_blocks * CB), one_group, 0)


def form_own_kernel(plan, table, pan_ref, cur_ref, rows, pan, cur, pan_sem, cur_sem):
    tiles = rows.shape[0]
    copies = [
        pltpu.make_async_copy(pan_ref.at[tile], pan.at[tile], pan_sem.at[tile])
        for tile in range(tiles)
    ]
    small = pltpu.make_async_copy(cur_ref, cur, cur_sem)
    small.start()
    for copy in copies:
        copy.start()
    small.wait()
    for tile, copy in enumerate(copies):
        copy.wait()
        form_tile(plan, table, tile, pan, cur, rows)


def form_kernel(plan, table, pan, cur, rows):
    for tile in range(rows.shape[0]):
        form_tile(plan, table, tile, pan, cur, rows)


def round_kernel(plan, table_a, table_b, pan_a, pan_b, rows_a, rows_b, *rest):
    sending, bases, orders, total, row_blocks, halves, tiles, pairs = plan
    outs, right, pair_at, acc = rest[:2], rest[2], rest[3], rest[4]
    extent = row_blocks * CB
    columns = pairs * LANES
    for base, order, out in zip(bases, orders, outs):
        acc[...] = jnp.zeros_like(acc)
        spots = [spot_of(half + (halves if sending else 0), order) for half in range(halves)]
        for table, pan, rows in ((table_a, pan_a, rows_a), (table_b, pan_b, rows_b)):

            def one_tile(tile, carry):
                used = [
                    functools.reduce(
                        jnp.maximum,
                        [
                            table[tile, total + spot * row_blocks + block]
                            for block in range(row_blocks)
                        ],
                    )
                    for spot in spots
                ]

                @pl.when(functools.reduce(jnp.maximum, used) >= 0)
                def some():
                    def one_pair(pair, count):
                        slots = [table[tile, base + 2 * pair + side] for side in range(2)]
                        live = jnp.maximum(slots[0], slots[1]) >= 0

                        @pl.when(live)
                        def stage():
                            pair_at[count] = pair * LANES
                            for side, slot in enumerate(slots):
                                first = pl.multiple_of(count * LANES + side * CB, CB)
                                lines = pl.ds(first, CB)

                                @pl.when(slot >= 0)
                                def fill():
                                    panel = pan[tile, slot]
                                    right[lines, :WIDTH] = panel
                                    right[lines, WIDTH:] = panel

                                @pl.when(slot < 0)
                                def blank():
                                    right[lines, :] = jnp.zeros((CB, 2 * WIDTH), jnp.bfloat16)

                        return count + jnp.where(live, 1, 0)

                    count = lax.fori_loop(0, pairs, one_pair, jnp.int32(0))
                    pair_at[count] = columns

                    def one_dot(double, carry):
                        first = pl.multiple_of(double * 2 * LANES, 2 * LANES)
                        for half, spot in enumerate(spots):

                            @pl.when(used[half] >= 0)
                            def add():
                                result = lax.dot_general(
                                    rows[tile, spot * extent : (spot + 1) * extent, :],
                                    right[pl.ds(first, 2 * LANES), :],
                                    (((1,), (1,)), ((), ())),
                                    preferred_element_type=jnp.float32,
                                )
                                for side in range(2):
                                    at = pl.multiple_of(pair_at[2 * double + side], LANES)
                                    acc[half, :, pl.ds(at, LANES)] += result[
                                        :, side * LANES : (side + 1) * LANES
                                    ]

                        return carry

                    lax.fori_loop(0, (count + 1) // 2, one_dot, 0)

                return carry

            lax.fori_loop(0, tiles, one_tile, 0)

        def store(start, carry):
            lanes = pl.ds(pl.multiple_of(start * WIDE, WIDE), WIDE)
            if sending:
                parts = [
                    functools.partial(
                        lambda half, block: acc[half, pl.ds(block * CB, CB), lanes], half, block
                    )
                    for half in range(halves)
                    for block in range(row_blocks)
                ]
                encode(out, lanes, parts)
            else:
                for half in range(halves):
                    out[half, :, lanes] = acc[half, :, lanes]
            return carry

        lax.fori_loop(0, columns // WIDE, store, 0)


def relay_kernel(plan, keep, *rest):
    row_blocks, size = plan
    dst = rest[-1]

    def code(start, carry):
        lanes = pl.ds(pl.multiple_of(start * WIDE, WIDE), WIDE)
        parts = []
        for place in range(size // 2, size):
            parts += given(gathered(place, keep, rest[:-1], lanes, row_blocks))
        encode(dst, lanes, parts)
        return carry

    lax.fori_loop(0, dst.shape[1] // WIDE, code, 0)


def cross_kernel(row_blocks, group, arrays, *rest):
    dsts = rest[2 * arrays :]
    for other, dst in enumerate(dsts):
        for start in range(0, group, LANES):
            parts = []
            for piece in range(2):
                keep, *came = rest[piece * arrays : (piece + 1) * arrays]
                lanes = pl.ds((other + 1) * group + start, LANES)
                parts += given(gathered(0, keep, came, lanes, row_blocks))
            encode(dst, pl.ds(start, LANES), parts)


def base_kernel(plan, me_ref, wide_ref, *rest):
    turn, row_blocks, col_blocks, arrays = plan
    out_ref = rest[-1]
    group = out_ref.shape[1] // 2
    first_row = (me_ref[0] * 2 + me_ref[1]) * row_blocks
    first_col = me_ref[2] * col_blocks
    lane = lax.broadcasted_iota(jnp.int32, (CB, LANES), 1) // CB
    for piece in range(2):
        keep, *came = rest[piece * arrays : (piece + 1) * arrays]
        for start in range(0, group, LANES):
            parts = gathered(0, keep, came, pl.ds(start, LANES), row_blocks)
            base = first_col + ((2 * turn + piece) * group + start) // CB
            for block in range(row_blocks):
                wide = jnp.where(base + lane == first_row + block, wide_ref[block], 0.0)
                out_ref[pl.ds(block * CB, CB), pl.ds(piece * group + start, LANES)] = (
                    wide - parts[block]
                )


def finish_kernel(row_blocks, far, base_ref, *rest):
    out_ref = rest[-1]
    group = out_ref.shape[1] // 2
    for piece in range(2):
        for start in range(0, group, LANES):
            total = [0.0] * row_blocks
            for src in rest[:far]:
                parts = decode(src, pl.ds(start, LANES), piece * row_blocks, row_blocks)
                total = [left + right for left, right in zip(total, parts)]
            lanes = pl.ds(piece * group + start, LANES)
            for block in range(row_blocks):
                lines = pl.ds(block * CB, CB)
                out_ref[lines, lanes] = base_ref[lines, lanes] - total[block]


def body(panels, curvature, visible_blocks, counts, camera_hessian):
    tiles = panels.shape[0]
    n_lm, n_cam = lax.axis_size("lm"), lax.axis_size("cam")
    chips = n_lm // 2
    bits = int(math.log2(chips))
    row_blocks = camera_hessian.shape[0]
    extent = row_blocks * CB
    col_blocks = row_blocks * n_lm // n_cam
    turns = col_blocks * CB // (2 * LANES)
    pieces = 2 * turns
    group = col_blocks * CB // pieces
    columns = group * n_cam
    total = row_blocks * n_lm
    orders = [list(range(bits)), list(reversed(range(bits)))]
    lm, cam = lax.axis_index("lm"), lax.axis_index("cam")
    me = jnp.stack([lm // 2, lm % 2, cam]).astype(jnp.int32)

    live = jnp.arange(K, dtype=jnp.int32)[None, :] < counts[:, None]
    ids = jnp.where(live, visible_blocks, -1)

    def swap(value, bit):
        return lax.ppermute(value, "lm", [(i, i ^ (1 << bit)) for i in range(n_lm)])

    pan_other, cur_other, ids_other = swap(panels, 0), swap(curvature, 0), swap(ids, 0)
    wide = jnp.concatenate([camera_hessian, camera_hessian], axis=-1)
    per = group // CB
    slots = jnp.arange(K, dtype=jnp.int32)[None, :, None]
    places = jnp.arange(total + chips * row_blocks, dtype=jnp.int32)

    def table_of(ids):
        inner = ids % col_blocks
        spot = ((inner // per) * n_cam + ((ids // col_blocks) ^ cam)) * per + inner % per
        owner = ids // row_blocks
        line = total + ((owner // 2) ^ (lm // 2)) * row_blocks + ids % row_blocks
        spot = jnp.where(ids >= 0, spot, -1)
        line = jnp.where((ids >= 0) & (owner % 2 == lm % 2), line, -1)
        found = (spot[:, :, None] == places) | (line[:, :, None] == places)
        return jnp.max(jnp.where(found, slots, -1), axis=1)

    table_a, table_b = table_of(ids), table_of(ids_other)
    formed = jax.ShapeDtypeStruct((tiles, chips * extent, 2 * WIDTH), jnp.bfloat16)
    whole = pl.BlockSpec(memory_space=pltpu.HBM)
    rows_a, pan_here = pl.pallas_call(
        functools.partial(form_own_kernel, (total, row_blocks)),
        in_specs=[SMEM, whole, whole],
        out_specs=[VMEM, VMEM],
        out_shape=[formed, jax.ShapeDtypeStruct(panels.shape, panels.dtype)],
        scratch_shapes=[
            pltpu.VMEM(curvature.shape, jnp.float32),
            pltpu.SemaphoreType.DMA((tiles,)),
            pltpu.SemaphoreType.DMA,
        ],
        compiler_params=PARAMS,
        name="form_own",
    )(table_a, panels, curvature)
    rows_b = pl.pallas_call(
        functools.partial(form_kernel, (total, row_blocks)),
        in_specs=[SMEM, VMEM, VMEM],
        out_specs=VMEM,
        out_shape=formed,
        compiler_params=PARAMS,
        name="form_other",
    )(table_b, pan_other, cur_other)

    def round_call(sending, turn, tables):
        if sending:
            made = jax.ShapeDtypeStruct((chips // 2 * extent + STRIP, columns), jnp.int16)
        else:
            made = jax.ShapeDtypeStruct((chips // 2, extent, columns), jnp.float32)
        bases = [(2 * turn + which) * n_cam * per for which in range(2)]
        pairs = columns // LANES
        plan = (sending, bases, orders, total, row_blocks, chips // 2, tiles, pairs)
        return pl.pallas_call(
            functools.partial(round_kernel, plan),
            in_specs=[SMEM] * 2 + [VMEM] * 4,
            out_specs=[VMEM] * 2,
            out_shape=[made] * 2,
            scratch_shapes=[
                pltpu.VMEM((columns + LANES, 2 * WIDTH), jnp.bfloat16),
                pltpu.SMEM((pairs + 1,), jnp.int32),
                pltpu.VMEM((chips // 2, extent, columns + LANES), jnp.float32),
            ],
            compiler_params=PARAMS,
            name="send" if sending else "keep",
        )(*tables, pan_here, pan_other, rows_a, rows_b)

    tables = (table_a, table_b)
    sends, keeps = [], []
    for turn in range(turns):
        for sending, made in ((True, sends), (False, keeps)):
            made.append(list(round_call(sending, turn, tables)))
            tables = lax.optimization_barrier((tables, made[-1]))[0]

    came = [[[], []] for _ in range(turns)]
    result = None
    for turn in range(turns):
        if turn:
            sends[turn] = lax.optimization_barrier((sends[turn], crossed))[0]
        for stage in range(bits):
            for piece in range(2):
                came[turn][piece].append(swap(sends[turn][piece], orders[piece][stage] + 1))
            size = chips >> (stage + 1)
            if size == 1:
                break
            for piece in range(2):
                keep = keeps[turn][piece]
                if turn:
                    keep = lax.optimization_barrier((keep, far))[0]
                arrays = [keep] + came[turn][piece]
                sends[turn][piece] = pl.pallas_call(
                    functools.partial(relay_kernel, (row_blocks, size)),
                    in_specs=[VMEM] * len(arrays),
                    out_specs=VMEM,
                    out_shape=jax.ShapeDtypeStruct((size // 2 * extent + STRIP, columns), jnp.int16),
                    compiler_params=PARAMS,
                    name="relay",
                )(*arrays)

        near = [array for piece in range(2) for array in [keeps[turn][piece]] + came[turn][piece]]
        arrays = len(near) // 2
        crossed = pl.pallas_call(
            functools.partial(cross_kernel, row_blocks, group, arrays),
            in_specs=[VMEM] * len(near),
            out_specs=[VMEM] * (n_cam - 1),
            out_shape=[jax.ShapeDtypeStruct((2 * extent + STRIP, group), jnp.int16)] * (n_cam - 1),
            compiler_params=PARAMS,
            name="cross",
        )(*near)
        far = [
            lax.ppermute(crossed[pos], "cam", [(i, i ^ (pos + 1)) for i in range(n_cam)])
            for pos in reversed(range(n_cam - 1))
        ]
        base = pl.pallas_call(
            functools.partial(base_kernel, (turn, row_blocks, col_blocks, arrays)),
            in_specs=[SMEM, VMEM] + [VMEM] * len(near),
            out_specs=VMEM,
            out_shape=jax.ShapeDtypeStruct((extent, 2 * group), jnp.float32),
            compiler_params=PARAMS,
            name="base",
        )(me, wide, *near)
        before = [] if result is None else [result]
        result = pl.pallas_call(
            functools.partial(finish_kernel, row_blocks, n_cam - 1),
            grid=(1,),
            in_specs=[VMEM] * n_cam + [pl.BlockSpec(memory_space=pl.ANY)] * len(before),
            out_specs=pl.BlockSpec((extent, 2 * group), lambda step, turn=turn: (0, turn)),
            out_shape=jax.ShapeDtypeStruct((extent, col_blocks * CB), jnp.float32),
            input_output_aliases={n_cam: 0} if before else {},
            compiler_params=PARAMS,
            name="finish",
        )(base, *far, *before)
    return result


def solution(mesh):
    return jax.shard_map(
        body,
        mesh=mesh,
        in_specs=(
            P(("lm", "cam"), None, None, None),
            P(None, None, ("lm", "cam")),
            P(("lm", "cam"), None),
            P(("lm", "cam")),
            P("lm", None, None),
        ),
        out_specs=P("lm", "cam"),
        check_vma=False,
    )
```

```python
import functools
import math

import jax
import jax.numpy as jnp
from jax import lax
from jax.experimental import pallas as pl
from jax.experimental.pallas import tpu as pltpu
from jax.sharding import PartitionSpec as P

CB = 64
LMB = 128
K = 16
WIDTH = 3 * LMB
LANES = 128
QUAD = 4
VMEM = pl.BlockSpec(memory_space=pltpu.VMEM)
SMEM = pl.BlockSpec(memory_space=pltpu.SMEM)
PARAMS = pltpu.CompilerParams(vmem_limit_bytes=32 * 1024 * 1024)


def invert_rows(cur_ref, start):
    lanes = pl.ds(start, LMB)
    entry = [[cur_ref[row, col : col + 1, lanes] for col in range(3)] for row in range(3)]
    cofactor = [
        [
            entry[(row + 1) % 3][(col + 1) % 3] * entry[(row + 2) % 3][(col + 2) % 3]
            - entry[(row + 1) % 3][(col + 2) % 3] * entry[(row + 2) % 3][(col + 1) % 3]
            for col in range(3)
        ]
        for row in range(3)
    ]
    determ = (
        entry[0][0] * cofactor[0][0] + entry[0][1] * cofactor[0][1] + entry[0][2] * cofactor[0][2]
    )
    return [[cofactor[col][row] / determ for col in range(3)] for row in range(3)]


def strip_of(blocks):
    return -(-blocks // 16) * 16


def encode(dst, lanes, parts):
    blocks = len(parts)
    strip = strip_of(blocks)
    width = lanes.size
    row = lax.broadcasted_iota(jnp.int32, (strip, width), 0)
    tops = jnp.full((strip, width), 2.0**-100, jnp.float32)
    for block, part in enumerate(parts):
        top = jnp.max(jnp.abs(part()), axis=0, keepdims=True)
        tops = jnp.where(row == block, jnp.maximum(top, tops), tops)
    power = jnp.ceil(jnp.log2(tops) - 14.99)
    inverse = jnp.exp2(-power)
    for block, part in enumerate(parts):
        coded = jnp.floor(part() * inverse[block : block + 1] + 0.5)
        dst[pl.ds(block * CB, CB), lanes] = coded.astype(jnp.int32).astype(jnp.int16)
    dst[pl.ds(blocks * CB, strip), lanes] = power.astype(jnp.int32).astype(jnp.int16)


def scales(src, lanes):
    blocks = src.shape[0] // CB
    strip = src[pl.ds(blocks * CB, strip_of(blocks)), lanes]
    return jnp.exp2(strip.astype(jnp.int32).astype(jnp.float32))


def decode(src, lanes, scale, block):
    coded = src[pl.ds(block * CB, CB), lanes].astype(jnp.int32).astype(jnp.float32)
    return coded * scale[block : block + 1]


def gathered(keep, came, lanes, first, place, blocks):
    parts = [keep[pl.ds(first + block * CB, CB), lanes] for block in range(blocks)]
    for src in came:
        scale = scales(src, lanes)
        parts = [
            part + decode(src, lanes, scale, place * blocks + block)
            for block, part in enumerate(parts)
        ]
    return parts


def given(values):
    return [functools.partial(lambda value: value, value) for value in values]


def index_of(spot, order):
    bits = len(order)
    return sum(((spot >> bit) & 1) << (bits - 1 - pos) for pos, bit in enumerate(order))


def form_tile(plan, table, tile, pan, cur, rows, line_at, many):
    total, region_size = plan
    inverse = invert_rows(cur, tile * LMB)
    for region in range(2):
        list_at = region * (region_size + QUAD)

        def one_form(place, slot, count):
            line_at[tile, list_at + count] = place * CB
            lines = pl.ds(pl.multiple_of((region * region_size + count) * CB, CB), CB)
            wide = pan[tile, slot].astype(jnp.float32)
            split = [wide[:, c * LMB : (c + 1) * LMB] for c in range(3)]
            for q in range(3):
                formed = (
                    split[0] * inverse[0][q] + split[1] * inverse[1][q] + split[2] * inverse[2][q]
                )
                high = formed.astype(jnp.bfloat16)
                low = (formed - high.astype(jnp.float32)).astype(jnp.bfloat16)
                at = q * LMB
                rows[tile, lines, at : at + LMB] = high
                rows[tile, lines, WIDTH + at : WIDTH + at + LMB] = low

        def some_places(few, count):
            places = [region * region_size + few * QUAD + place for place in range(QUAD)]
            slots = [table[tile, total + place] for place in places]
            counts = [count]
            for slot in slots:
                counts.append(counts[-1] + jnp.where(slot >= 0, 1, 0))

            @pl.when(counts[-1] > count)
            def some():
                for place, slot, at in zip(places, slots, counts):
                    pl.when(slot >= 0)(functools.partial(one_form, place, slot, at))

            return counts[-1]

        count = lax.fori_loop(0, region_size // QUAD, some_places, jnp.int32(0))
        many[tile, region] = (count + QUAD - 1) // QUAD
        for extra in range(QUAD):
            line_at[tile, list_at + count + extra] = 2 * region_size * CB


def form_own_kernel(plan, table, pan_ref, cur_ref, rows, line_at, many, pan, cur, sems):
    tiles = rows.shape[0]
    copies = [
        pltpu.make_async_copy(pan_ref.at[tile], pan.at[tile], sems.at[tile])
        for tile in range(tiles)
    ]
    small = pltpu.make_async_copy(cur_ref, cur, sems.at[tiles])
    small.start()
    for copy in copies:
        copy.start()
    small.wait()
    for tile, copy in enumerate(copies):
        copy.wait()
        form_tile(plan, table, tile, pan, cur, rows, line_at, many)


def form_kernel(plan, table, pan, cur, rows, line_at, many):
    for tile in range(rows.shape[0]):
        form_tile(plan, table, tile, pan, cur, rows, line_at, many)


def joint_of(pairs):
    return 4 if pairs % 4 == 0 and pairs >= 8 else 2


def accumulate(plan, sides, right, pair_at, acc):
    base, pairs, regions, region_size = plan
    joint = joint_of(pairs)
    acc[...] = jnp.zeros_like(acc)
    dump = acc.shape[0] - CB
    for table, line_at, many, pan, rows in sides:

        def one_tile(tile, carry):
            used = functools.reduce(jnp.maximum, [many[tile, region] for region in regions])

            @pl.when(used > 0)
            def some():
                def one_pair(pair, count):
                    slots = [table[tile, base + 2 * pair + side] for side in range(2)]
                    live = jnp.maximum(slots[0], slots[1]) >= 0

                    @pl.when(live)
                    def stage():
                        pair_at[count] = pair * LANES
                        for side, slot in enumerate(slots):
                            first = pl.multiple_of(count * LANES + side * CB, CB)
                            lines = pl.ds(first, CB)

                            @pl.when(slot >= 0)
                            def fill():
                                panel = pan[tile, slot]
                                right[lines, :WIDTH] = panel
                                right[lines, WIDTH:] = panel

                            @pl.when(slot < 0)
                            def blank():
                                right[lines, :] = jnp.zeros((CB, 2 * WIDTH), jnp.bfloat16)

                    return count + jnp.where(live, 1, 0)

                count = lax.fori_loop(0, pairs, one_pair, jnp.int32(0))
                for extra in range(joint - 1):
                    pair_at[count + extra] = pairs * LANES
                for region in regions:
                    shift = region * region_size * CB if len(regions) == 1 else 0

                    def one_group(group, carry):
                        start = (region * region_size + group * QUAD) * CB
                        lines = pl.ds(pl.multiple_of(start, QUAD * CB), QUAD * CB)
                        list_at = region * (region_size + QUAD) + group * QUAD

                        def one_dot(few, carry):
                            first = pl.multiple_of(few * joint * LANES, joint * LANES)
                            result = lax.dot_general(
                                rows[tile, lines, :],
                                right[pl.ds(first, joint * LANES), :],
                                (((1,), (1,)), ((), ())),
                                preferred_element_type=jnp.float32,
                            )
                            for block in range(QUAD):
                                line = jnp.minimum(line_at[tile, list_at + block] - shift, dump)
                                line = pl.multiple_of(line, CB)
                                for side in range(joint):
                                    lane = pl.multiple_of(pair_at[few * joint + side], LANES)
                                    acc[pl.ds(line, CB), pl.ds(lane, LANES)] += result[
                                        block * CB : (block + 1) * CB,
                                        side * LANES : (side + 1) * LANES,
                                    ]
                            return carry

                        return lax.fori_loop(0, (count + joint - 1) // joint, one_dot, carry)

                    lax.fori_loop(0, many[tile, region], one_group, 0)

            return carry

        lax.fori_loop(0, rows.shape[0], one_tile, 0)


def each_tile(columns, work, most=4):
    width = max(w * LANES for w in range(1, most + 1) if columns % (w * LANES) == 0)

    def one(start, carry):
        work(pl.ds(pl.multiple_of(start * width, width), width))
        return carry

    lax.fori_loop(0, columns // width, one, 0)


def blocks_at(acc, first, blocks, lanes):
    return [
        functools.partial(lambda block: acc[pl.ds(first + block * CB, CB), lanes], block)
        for block in range(blocks)
    ]


def sides_of(refs):
    return [refs[:5], refs[5:10]]


def send_kernel(plan, *refs):
    outs, (right, pair_at, acc) = refs[10:12], refs[12:]
    accumulate(plan, sides_of(refs), right, pair_at, acc)
    blocks = plan[3] // 2

    def code(lanes):
        for half, out in enumerate(outs):
            encode(out, lanes, blocks_at(acc, half * blocks * CB, blocks, lanes))

    each_tile(outs[0].shape[1], code)


def keep_kernel(plan, *refs):
    acc, right, pair_at = refs[10:]
    accumulate(plan, sides_of(refs), right, pair_at, acc)


def relay_kernel(plan, keep, *rest):
    first, blocks, size = plan
    dst = rest[-1]

    def code(lanes):
        parts = []
        for place in range(size // 2, size):
            line = first + place * blocks * CB
            parts += given(gathered(keep, rest[:-1], lanes, line, place, blocks))
        encode(dst, lanes, parts)

    each_tile(dst.shape[1], code, 2)


def own_rows(firsts, blocks, keep, came, lanes):
    parts = []
    for first, arrays in zip(firsts, came):
        parts += gathered(keep, arrays, lanes, first, 0, blocks)
    return parts


def cross_kernel(plan, keep, *rest):
    firsts, blocks, arrays = plan
    came = [rest[half * arrays : (half + 1) * arrays] for half in range(2)]
    dsts = rest[2 * arrays :]
    group = dsts[0].shape[1]
    for other, dst in enumerate(dsts):

        for start in range(0, group, LANES):
            lanes = pl.ds((other + 1) * group + start, LANES)
            encode(dst, pl.ds(start, LANES), given(own_rows(firsts, blocks, keep, came, lanes)))


def hessian_part(me_ref, wide_ref, plan, start, block):
    row_blocks, col_blocks = plan
    row = (me_ref[0] * 2 + me_ref[1]) * row_blocks + block
    lane = lax.broadcasted_iota(jnp.int32, (CB, LANES), 1) // CB
    return jnp.where(me_ref[2] * col_blocks + start // CB + lane == row, wide_ref[block], 0.0)


def base_kernel(plan, me_ref, wide_ref, keep, *rest):
    sizes, firsts, blocks, arrays, offset = plan
    came = [rest[half * arrays : (half + 1) * arrays] for half in range(2)]
    out = rest[-1]
    for start in range(0, out.shape[1], LANES):
        lanes = pl.ds(start, LANES)
        for block, part in enumerate(own_rows(firsts, blocks, keep, came, lanes)):
            out[pl.ds(block * CB, CB), lanes] = (
                hessian_part(me_ref, wide_ref, sizes, offset + start, block) - part
            )


def finish_kernel(blocks, *refs):
    out = refs[-1]
    arrays = (len(refs) - 1) // 2
    for step in range(2):

        @pl.when(pl.program_id(0) == step)
        def rows():
            offset = 0
            for share in range(2):
                base, *far = refs[share * arrays : (share + 1) * arrays]
                for start in range(0, base.shape[1], LANES):
                    lanes = pl.ds(start, LANES)
                    factors = [scales(src, lanes) for src in far]
                    for block in range(blocks // 2):
                        here = step * (blocks // 2) + block
                        total = base[pl.ds(here * CB, CB), lanes]
                        for src, scale in zip(far, factors):
                            total = total - decode(src, lanes, scale, here)
                        out[pl.ds(block * CB, CB), pl.ds(offset + start, LANES)] = total
                offset += base.shape[1]


def body(panels, curvature, visible_blocks, counts, camera_hessian):
    tiles = panels.shape[0]
    n_lm, n_cam = lax.axis_size("lm"), lax.axis_size("cam")
    chips = n_lm // 2
    halves = chips // 2
    bits = int(math.log2(chips))
    row_blocks = camera_hessian.shape[0]
    half_blocks = row_blocks // 2
    extent = row_blocks * CB
    total = row_blocks * n_lm
    col_blocks = total // n_cam
    large = col_blocks * CB - LANES
    per = large // CB
    region_size = chips * half_blocks
    orders = [list(range(bits)), list(reversed(range(bits)))]
    lm, cam = lax.axis_index("lm"), lax.axis_index("cam")
    me = jnp.stack([lm // 2, lm % 2, cam]).astype(jnp.int32)

    live = jnp.arange(K, dtype=jnp.int32)[None, :] < counts[:, None]
    ids = jnp.where(live, visible_blocks, -1)

    def swap(value, step):
        return lax.ppermute(value, "lm", [(i, i ^ step) for i in range(n_lm)])

    pan_other, cur_other, ids_other = swap(panels, 1), swap(curvature, 1), swap(ids, 1)
    wide = jnp.concatenate([camera_hessian, camera_hessian], axis=-1)
    slots = jnp.arange(K, dtype=jnp.int32)[None, :, None]
    places = jnp.arange(total + 2 * region_size, dtype=jnp.int32)

    def table_of(ids):
        inner, owner = ids % col_blocks, ids // col_blocks
        spot = jnp.where(
            inner < per,
            (owner ^ cam) * per + inner,
            n_cam * per + (owner ^ cam) * (col_blocks - per) + inner - per,
        )
        owner = ids // row_blocks
        group, block = (owner // 2) ^ (lm // 2), ids % row_blocks
        half = block // half_blocks
        index = jnp.where(half == 0, index_of(group, orders[0]), index_of(group, orders[1]))
        line = (half * halves + index % halves) * half_blocks + block % half_blocks
        line = total + line + jnp.where(index >= halves, 0, region_size)
        spot = jnp.where(ids >= 0, spot, -1)
        line = jnp.where((ids >= 0) & (owner % 2 == lm % 2), line, -1)
        found = (spot[:, :, None] == places) | (line[:, :, None] == places)
        return jnp.max(jnp.where(found, slots, -1), axis=1)

    def call(kernel, name, outs, scratch=(), **options):
        return pl.pallas_call(
            kernel,
            out_shape=outs,
            scratch_shapes=list(scratch),
            compiler_params=PARAMS,
            name=name,
            **options,
        )

    def coded(blocks, columns):
        return jax.ShapeDtypeStruct((blocks * CB + strip_of(blocks), columns), jnp.int16)

    def exact(rows, columns):
        return jax.ShapeDtypeStruct((rows, columns), jnp.float32)

    table_a, table_b = table_of(ids), table_of(ids_other)
    formed = [
        jax.ShapeDtypeStruct((tiles, 2 * region_size * CB, 2 * WIDTH), jnp.bfloat16),
        jax.ShapeDtypeStruct((tiles, 2 * (region_size + QUAD)), jnp.int32),
        jax.ShapeDtypeStruct((tiles, 2), jnp.int32),
    ]
    in_hbm = pl.BlockSpec(memory_space=pltpu.HBM)
    rows_a, line_a, many_a, pan_here = call(
        functools.partial(form_own_kernel, (total, region_size)),
        "form_own",
        formed + [jax.ShapeDtypeStruct(panels.shape, panels.dtype)],
        [pltpu.VMEM(curvature.shape, jnp.float32), pltpu.SemaphoreType.DMA((tiles + 1,))],
        in_specs=[SMEM, in_hbm, in_hbm],
        out_specs=[VMEM, SMEM, SMEM, VMEM],
    )(table_a, panels, curvature)
    rows_b, line_b, many_b = call(
        functools.partial(form_kernel, (total, region_size)),
        "form_other",
        formed,
        in_specs=[SMEM, VMEM, VMEM],
        out_specs=[VMEM, SMEM, SMEM],
    )(table_b, pan_other, cur_other)

    def scratch(pairs):
        return [
            pltpu.VMEM(((pairs + 1) * LANES, 2 * WIDTH), jnp.bfloat16),
            pltpu.SMEM((pairs + joint_of(pairs),), jnp.int32),
        ]

    def sums(kernel, name, base, pairs, regions, outs, more, tables):
        plan = (base, pairs, regions, region_size)
        side = [SMEM] * 3 + [VMEM] * 2
        return call(
            functools.partial(kernel, plan),
            name,
            outs,
            scratch(pairs) + more,
            in_specs=side * 2,
            out_specs=[VMEM] * len(outs),
        )(tables[0], line_a, many_a, pan_here, rows_a, tables[1], line_b, many_b, pan_other, rows_b)

    tables = (table_a, table_b)
    shares = [(0, 0, large), (n_cam * per, large, LANES)]
    made = []
    for base_at, _, group in shares:
        columns = group * n_cam
        sum_shape = ((region_size + 1) * CB, columns + LANES)
        pairs = columns // LANES
        sends = sums(
            send_kernel,
            "send",
            base_at,
            pairs,
            [0],
            [coded(halves * half_blocks, columns)] * 2,
            [pltpu.VMEM(sum_shape, jnp.float32)],
            tables,
        )
        tables = lax.optimization_barrier((tables, sends))[0]
        (keep,) = sums(keep_kernel, "keep", base_at, pairs, [1], [exact(*sum_shape)], [], tables)
        tables = lax.optimization_barrier((tables, keep))[0]
        made.append((sends, keep))

    firsts = [half * halves * half_blocks * CB for half in range(2)]
    sizes = (row_blocks, col_blocks)
    finals, crossed, far = [], None, None
    for (_, offset, group), (sends, keep) in zip(shares, made):
        columns = group * n_cam
        if crossed:
            sends = lax.optimization_barrier((sends, crossed))[0]
        came = [[], []]
        for stage in range(bits):
            for half in range(2):
                came[half].append(swap(sends[half], 2 << orders[half][stage]))
            size = chips >> (stage + 1)
            if size == 1:
                break
            now = lax.optimization_barrier((keep, far[:1]))[0] if far else keep
            sends = [
                call(
                    functools.partial(relay_kernel, (firsts[half], half_blocks, size)),
                    "relay",
                    coded(size // 2 * half_blocks, columns),
                    in_specs=[VMEM] * (1 + len(came[half])),
                    out_specs=VMEM,
                )(now, *came[half])
                for half in range(2)
            ]

        near = came[0] + came[1]
        ready = lax.optimization_barrier((keep, far))[0] if far else keep
        crossed = call(
            functools.partial(cross_kernel, (firsts, half_blocks, bits)),
            "cross",
            [coded(row_blocks, group)] * (n_cam - 1),
            in_specs=[VMEM] * (1 + len(near)),
            out_specs=[VMEM] * (n_cam - 1),
        )(ready, *near)
        far = [
            lax.ppermute(value, "cam", [(i, i ^ (pos + 1)) for i in range(n_cam)])
            for pos, value in enumerate(crossed)
        ]
        base = call(
            functools.partial(base_kernel, (sizes, firsts, half_blocks, bits, offset)),
            "base",
            exact(extent, group),
            in_specs=[SMEM] + [VMEM] * (2 + len(near)),
            out_specs=VMEM,
        )(me, wide, keep, *near)
        finals += [base] + far
    return call(
        functools.partial(finish_kernel, row_blocks),
        "finish",
        exact(extent, col_blocks * CB),
        grid=(2,),
        in_specs=[VMEM] * len(finals),
        out_specs=pl.BlockSpec((extent // 2, col_blocks * CB), lambda step: (step, 0)),
    )(*finals)


def solution(mesh):
    return jax.shard_map(
        body,
        mesh=mesh,
        in_specs=(
            P(("lm", "cam"), None, None, None),
            P(None, None, ("lm", "cam")),
            P(("lm", "cam"), None),
            P(("lm", "cam")),
            P("lm", None, None),
        ),
        out_specs=P("lm", "cam"),
        check_vma=False,
    )
```

```python
import functools
import math

import jax
import jax.numpy as jnp
from jax import lax
from jax.experimental import pallas as pl
from jax.experimental.pallas import tpu as pltpu
from jax.sharding import PartitionSpec as P

CB = 64
LMB = 128
K = 16
WIDTH = 3 * LMB
STRIP = 16
LANES = 128
WIDE = 256
VMEM = pl.BlockSpec(memory_space=pltpu.VMEM)
SMEM = pl.BlockSpec(memory_space=pltpu.SMEM)
PARAMS = pltpu.CompilerParams(vmem_limit_bytes=32 * 1024 * 1024)


def invert_rows(cur_ref, start):
    lanes = pl.ds(start, LMB)
    entry = [[cur_ref[row, col : col + 1, lanes] for col in range(3)] for row in range(3)]
    cofactor = [
        [
            entry[(row + 1) % 3][(col + 1) % 3] * entry[(row + 2) % 3][(col + 2) % 3]
            - entry[(row + 1) % 3][(col + 2) % 3] * entry[(row + 2) % 3][(col + 1) % 3]
            for col in range(3)
        ]
        for row in range(3)
    ]
    determ = (
        entry[0][0] * cofactor[0][0] + entry[0][1] * cofactor[0][1] + entry[0][2] * cofactor[0][2]
    )
    return [[cofactor[col][row] / determ for col in range(3)] for row in range(3)]


def encode(dst, lanes, parts):
    blocks = len(parts)
    row = lax.broadcasted_iota(jnp.int32, (STRIP, lanes.size), 0)
    tops = jnp.full((STRIP, lanes.size), 2.0**-100, jnp.float32)
    for block, part in enumerate(parts):
        top = jnp.max(jnp.abs(part()), axis=0, keepdims=True)
        tops = jnp.where(row == block, jnp.maximum(top, tops), tops)
    power = jnp.ceil(jnp.log2(tops) - 14.99)
    inverse = jnp.exp2(-power)
    for block, part in enumerate(parts):
        coded = jnp.floor(part() * inverse[block : block + 1] + 0.5)
        dst[pl.ds(block * CB, CB), lanes] = coded.astype(jnp.int32).astype(jnp.int16)
    dst[pl.ds(blocks * CB, STRIP), lanes] = power.astype(jnp.int32).astype(jnp.int16)


def decode(src, lanes, first, blocks):
    below = src.shape[0] - STRIP
    strip = src[pl.ds(below, STRIP), lanes].astype(jnp.int32).astype(jnp.float32)
    scale = jnp.exp2(strip)
    return [
        src[pl.ds(block * CB, CB), lanes].astype(jnp.int32).astype(jnp.float32)
        * scale[block : block + 1]
        for block in range(first, first + blocks)
    ]


def gathered(place, keep, came, lanes, blocks):
    parts = [keep[place, pl.ds(block * CB, CB), lanes] for block in range(blocks)]
    for src in came:
        here = decode(src, lanes, place * blocks, blocks)
        parts = [part + other for part, other in zip(parts, here)]
    return parts


def given(values):
    return [functools.partial(lambda value: value, value) for value in values]


def spot_of(index, order):
    bits = len(order)
    return sum(((index >> (bits - 1 - pos)) & 1) << bit for pos, bit in enumerate(order))


def form_tile(plan, table, tile, pan, cur, rows):
    total, row_blocks = plan
    inverse = invert_rows(cur, tile * LMB)

    def one_group(group, carry):
        places = [group * row_blocks + block for block in range(row_blocks)]
        slots = [table[tile, total + place] for place in places]

        @pl.when(functools.reduce(jnp.maximum, slots) >= 0)
        def some():
            for place, slot in zip(places, slots):
                lines = pl.ds(pl.multiple_of(place * CB, CB), CB)

                @pl.when(slot >= 0)
                def form():
                    wide = pan[tile, slot].astype(jnp.float32)
                    split = [wide[:, c * LMB : (c + 1) * LMB] for c in range(3)]
                    for q in range(3):
                        formed = (
                            split[0] * inverse[0][q]
                            + split[1] * inverse[1][q]
                            + split[2] * inverse[2][q]
                        )
                        high = formed.astype(jnp.bfloat16)
                        low = (formed - high.astype(jnp.float32)).astype(jnp.bfloat16)
                        at = q * LMB
                        rows[tile, lines, at : at + LMB] = high
                        rows[tile, lines, WIDTH + at : WIDTH + at + LMB] = low

                @pl.when(slot < 0)
                def blank():
                    rows[tile, lines, :] = jnp.zeros((CB, 2 * WIDTH), jnp.bfloat16)

        return carry

    lax.fori_loop(0, rows.shape[1] // (row_blocks * CB), one_group, 0)


def form_own_kernel(plan, table, pan_ref, cur_ref, rows, pan, cur, pan_sem, cur_sem):
    tiles = rows.shape[0]
    copies = [
        pltpu.make_async_copy(pan_ref.at[tile], pan.at[tile], pan_sem.at[tile])
        for tile in range(tiles)
    ]
    small = pltpu.make_async_copy(cur_ref, cur, cur_sem)
    small.start()
    for copy in copies:
        copy.start()
    small.wait()
    for tile, copy in enumerate(copies):
        copy.wait()
        form_tile(plan, table, tile, pan, cur, rows)


def form_kernel(plan, table, pan, cur, rows):
    for tile in range(rows.shape[0]):
        form_tile(plan, table, tile, pan, cur, rows)


def round_kernel(plan, table_a, table_b, pan_a, pan_b, rows_a, rows_b, *rest):
    sending, bases, orders, total, row_blocks, halves, tiles, pairs = plan
    outs, right, pair_at, acc = rest[:2], rest[2], rest[3], rest[4]
    extent = row_blocks * CB
    columns = pairs * LANES
    slice_size = min(columns, 2 * WIDE)
    for base, order, out in zip(bases, orders, outs):
        acc[...] = jnp.zeros_like(acc)
        spots = [spot_of(half + (halves if sending else 0), order) for half in range(halves)]
        for table, pan, rows in ((table_a, pan_a, rows_a), (table_b, pan_b, rows_b)):

            def one_tile(tile, carry):
                used = [
                    functools.reduce(
                        jnp.maximum,
                        [
                            table[tile, total + spot * row_blocks + block]
                            for block in range(row_blocks)
                        ],
                    )
                    for spot in spots
                ]

                @pl.when(functools.reduce(jnp.maximum, used) >= 0)
                def some():
                    def one_pair(pair, count):
                        slots = [table[tile, base + 2 * pair + side] for side in range(2)]
                        live = jnp.maximum(slots[0], slots[1]) >= 0

                        @pl.when(live)
                        def stage():
                            pair_at[count] = pair * LANES
                            for side, slot in enumerate(slots):
                                first = pl.multiple_of(count * LANES + side * CB, CB)
                                lines = pl.ds(first, CB)

                                @pl.when(slot >= 0)
                                def fill():
                                    panel = pan[tile, slot]
                                    right[lines, :WIDTH] = panel
                                    right[lines, WIDTH:] = panel

                                @pl.when(slot < 0)
                                def blank():
                                    right[lines, :] = jnp.zeros((CB, 2 * WIDTH), jnp.bfloat16)

                        return count + jnp.where(live, 1, 0)

                    count = lax.fori_loop(0, pairs, one_pair, jnp.int32(0))
                    pair_at[count] = columns

                    def one_dot(double, carry):
                        first = pl.multiple_of(double * 2 * LANES, 2 * LANES)
                        for half, spot in enumerate(spots):

                            @pl.when(used[half] >= 0)
                            def add():
                                result = lax.dot_general(
                                    rows[tile, spot * extent : (spot + 1) * extent, :],
                                    right[pl.ds(first, 2 * LANES), :],
                                    (((1,), (1,)), ((), ())),
                                    preferred_element_type=jnp.float32,
                                )
                                for side in range(2):
                                    at = pl.multiple_of(pair_at[2 * double + side], LANES)
                                    acc[half, :, pl.ds(at, LANES)] += result[
                                        :, side * LANES : (side + 1) * LANES
                                    ]

                        return carry

                    lax.fori_loop(0, (count + 1) // 2, one_dot, 0)

                return carry

            lax.fori_loop(0, tiles, one_tile, 0)

        def store(start, carry):
            lanes = pl.ds(pl.multiple_of(start * slice_size, slice_size), slice_size)
            if sending:
                parts = [
                    functools.partial(
                        lambda half, block: acc[half, pl.ds(block * CB, CB), lanes], half, block
                    )
                    for half in range(halves)
                    for block in range(row_blocks)
                ]
                encode(out, lanes, parts)
            else:
                for half in range(halves):
                    out[half, :, lanes] = acc[half, :, lanes]
            return carry

        lax.fori_loop(0, columns // slice_size, store, 0)


def relay_kernel(plan, keep, *rest):
    row_blocks, size = plan
    dst = rest[-1]

    def code(start, carry):
        lanes = pl.ds(pl.multiple_of(start * WIDE, WIDE), WIDE)
        parts = []
        for place in range(size // 2, size):
            parts += given(gathered(place, keep, rest[:-1], lanes, row_blocks))
        encode(dst, lanes, parts)
        return carry

    lax.fori_loop(0, dst.shape[1] // WIDE, code, 0)


def cross_kernel(row_blocks, group, arrays, *rest):
    dsts = rest[2 * arrays :]
    for other, dst in enumerate(dsts):
        for start in range(0, group, LANES):
            parts = []
            for piece in range(2):
                keep, *came = rest[piece * arrays : (piece + 1) * arrays]
                lanes = pl.ds((other + 1) * group + start, LANES)
                parts += given(gathered(0, keep, came, lanes, row_blocks))
            encode(dst, pl.ds(start, LANES), parts)


def base_kernel(plan, me_ref, wide_ref, *rest):
    turn, row_blocks, col_blocks, arrays = plan
    out_ref = rest[-1]
    group = out_ref.shape[1] // 2
    first_row = (me_ref[0] * 2 + me_ref[1]) * row_blocks
    first_col = me_ref[2] * col_blocks
    lane = lax.broadcasted_iota(jnp.int32, (CB, LANES), 1) // CB
    for piece in range(2):
        keep, *came = rest[piece * arrays : (piece + 1) * arrays]
        for start in range(0, group, LANES):
            parts = gathered(0, keep, came, pl.ds(start, LANES), row_blocks)
            base = first_col + ((2 * turn + piece) * group + start) // CB
            for block in range(row_blocks):
                wide = jnp.where(base + lane == first_row + block, wide_ref[block], 0.0)
                out_ref[pl.ds(block * CB, CB), pl.ds(piece * group + start, LANES)] = (
                    wide - parts[block]
                )


def finish_kernel(row_blocks, far, base_ref, *rest):
    out_ref = rest[-1]
    group = out_ref.shape[1] // 2
    for piece in range(2):
        for start in range(0, group, LANES):
            total = [0.0] * row_blocks
            for src in rest[:far]:
                parts = decode(src, pl.ds(start, LANES), piece * row_blocks, row_blocks)
                total = [left + right for left, right in zip(total, parts)]
            lanes = pl.ds(piece * group + start, LANES)
            for block in range(row_blocks):
                lines = pl.ds(block * CB, CB)
                out_ref[lines, lanes] = base_ref[lines, lanes] - total[block]


def body(panels, curvature, visible_blocks, counts, camera_hessian):
    tiles = panels.shape[0]
    n_lm, n_cam = lax.axis_size("lm"), lax.axis_size("cam")
    chips = n_lm // 2
    bits = int(math.log2(chips))
    row_blocks = camera_hessian.shape[0]
    extent = row_blocks * CB
    col_blocks = row_blocks * n_lm // n_cam
    turns = col_blocks * CB // (2 * LANES)
    pieces = 2 * turns
    group = col_blocks * CB // pieces
    columns = group * n_cam
    total = row_blocks * n_lm
    orders = [list(range(bits)), list(reversed(range(bits)))]
    lm, cam = lax.axis_index("lm"), lax.axis_index("cam")
    me = jnp.stack([lm // 2, lm % 2, cam]).astype(jnp.int32)

    live = jnp.arange(K, dtype=jnp.int32)[None, :] < counts[:, None]
    ids = jnp.where(live, visible_blocks, -1)

    def swap(value, bit):
        return lax.ppermute(value, "lm", [(i, i ^ (1 << bit)) for i in range(n_lm)])

    pan_other, cur_other, ids_other = swap(panels, 0), swap(curvature, 0), swap(ids, 0)
    wide = jnp.concatenate([camera_hessian, camera_hessian], axis=-1)
    per = group // CB
    slots = jnp.arange(K, dtype=jnp.int32)[None, :, None]
    places = jnp.arange(total + chips * row_blocks, dtype=jnp.int32)

    def table_of(ids):
        inner = ids % col_blocks
        spot = ((inner // per) * n_cam + ((ids // col_blocks) ^ cam)) * per + inner % per
        owner = ids // row_blocks
        line = total + ((owner // 2) ^ (lm // 2)) * row_blocks + ids % row_blocks
        spot = jnp.where(ids >= 0, spot, -1)
        line = jnp.where((ids >= 0) & (owner % 2 == lm % 2), line, -1)
        found = (spot[:, :, None] == places) | (line[:, :, None] == places)
        return jnp.max(jnp.where(found, slots, -1), axis=1)

    table_a, table_b = table_of(ids), table_of(ids_other)
    formed = jax.ShapeDtypeStruct((tiles, chips * extent, 2 * WIDTH), jnp.bfloat16)
    whole = pl.BlockSpec(memory_space=pltpu.HBM)
    rows_a, pan_here = pl.pallas_call(
        functools.partial(form_own_kernel, (total, row_blocks)),
        in_specs=[SMEM, whole, whole],
        out_specs=[VMEM, VMEM],
        out_shape=[formed, jax.ShapeDtypeStruct(panels.shape, panels.dtype)],
        scratch_shapes=[
            pltpu.VMEM(curvature.shape, jnp.float32),
            pltpu.SemaphoreType.DMA((tiles,)),
            pltpu.SemaphoreType.DMA,
        ],
        compiler_params=PARAMS,
        name="form_own",
    )(table_a, panels, curvature)
    rows_b = pl.pallas_call(
        functools.partial(form_kernel, (total, row_blocks)),
        in_specs=[SMEM, VMEM, VMEM],
        out_specs=VMEM,
        out_shape=formed,
        compiler_params=PARAMS,
        name="form_other",
    )(table_b, pan_other, cur_other)

    def round_call(sending, turn, tables):
        if sending:
            made = jax.ShapeDtypeStruct((chips // 2 * extent + STRIP, columns), jnp.int16)
        else:
            made = jax.ShapeDtypeStruct((chips // 2, extent, columns), jnp.float32)
        bases = [(2 * turn + which) * n_cam * per for which in range(2)]
        pairs = columns // LANES
        plan = (sending, bases, orders, total, row_blocks, chips // 2, tiles, pairs)
        return pl.pallas_call(
            functools.partial(round_kernel, plan),
            in_specs=[SMEM] * 2 + [VMEM] * 4,
            out_specs=[VMEM] * 2,
            out_shape=[made] * 2,
            scratch_shapes=[
                pltpu.VMEM((columns + LANES, 2 * WIDTH), jnp.bfloat16),
                pltpu.SMEM((pairs + 1,), jnp.int32),
                pltpu.VMEM((chips // 2, extent, columns + LANES), jnp.float32),
            ],
            compiler_params=PARAMS,
            name="send" if sending else "keep",
        )(*tables, pan_here, pan_other, rows_a, rows_b)

    tables = (table_a, table_b)
    sends, keeps = [], []
    for turn in range(turns):
        for sending, made in ((True, sends), (False, keeps)):
            made.append(list(round_call(sending, turn, tables)))
            tables = lax.optimization_barrier((tables, made[-1]))[0]

    came = [[[], []] for _ in range(turns)]
    result = None
    for turn in range(turns):
        if turn:
            sends[turn] = lax.optimization_barrier((sends[turn], crossed))[0]
        for stage in range(bits):
            for piece in range(2):
                came[turn][piece].append(swap(sends[turn][piece], orders[piece][stage] + 1))
            size = chips >> (stage + 1)
            if size == 1:
                break
            for piece in range(2):
                keep = keeps[turn][piece]
                if turn:
                    keep = lax.optimization_barrier((keep, far))[0]
                arrays = [keep] + came[turn][piece]
                sends[turn][piece] = pl.pallas_call(
                    functools.partial(relay_kernel, (row_blocks, size)),
                    in_specs=[VMEM] * len(arrays),
                    out_specs=VMEM,
                    out_shape=jax.ShapeDtypeStruct((size // 2 * extent + STRIP, columns), jnp.int16),
                    compiler_params=PARAMS,
                    name="relay",
                )(*arrays)

        near = [array for piece in range(2) for array in [keeps[turn][piece]] + came[turn][piece]]
        arrays = len(near) // 2
        crossed = pl.pallas_call(
            functools.partial(cross_kernel, row_blocks, group, arrays),
            in_specs=[VMEM] * len(near),
            out_specs=[VMEM] * (n_cam - 1),
            out_shape=[jax.ShapeDtypeStruct((2 * extent + STRIP, group), jnp.int16)] * (n_cam - 1),
            compiler_params=PARAMS,
            name="cross",
        )(*near)
        far = [
            lax.ppermute(value, "cam", [(i, i ^ (pos + 1)) for i in range(n_cam)])
            for pos, value in enumerate(crossed)
        ]
        base = pl.pallas_call(
            functools.partial(base_kernel, (turn, row_blocks, col_blocks, arrays)),
            in_specs=[SMEM, VMEM] + [VMEM] * len(near),
            out_specs=VMEM,
            out_shape=jax.ShapeDtypeStruct((extent, 2 * group), jnp.float32),
            compiler_params=PARAMS,
            name="base",
        )(me, wide, *near)
        before = [] if result is None else [result]
        result = pl.pallas_call(
            functools.partial(finish_kernel, row_blocks, n_cam - 1),
            grid=(1,),
            in_specs=[VMEM] * n_cam + [pl.BlockSpec(memory_space=pl.ANY)] * len(before),
            out_specs=pl.BlockSpec((extent, 2 * group), lambda step, turn=turn: (0, turn)),
            out_shape=jax.ShapeDtypeStruct((extent, col_blocks * CB), jnp.float32),
            input_output_aliases={n_cam: 0} if before else {},
            compiler_params=PARAMS,
            name="finish",
        )(base, *far, *before)
    return result


def solution(mesh):
    return jax.shard_map(
        body,
        mesh=mesh,
        in_specs=(
            P(("lm", "cam"), None, None, None),
            P(None, None, ("lm", "cam")),
            P(("lm", "cam"), None),
            P(("lm", "cam")),
            P("lm", None, None),
        ),
        out_specs=P("lm", "cam"),
        check_vma=False,
    )
```

```python
import functools
import math

import jax
import jax.numpy as jnp
from jax import lax
from jax.experimental import pallas as pl
from jax.experimental.pallas import tpu as pltpu
from jax.sharding import PartitionSpec as P

CB = 64
LMB = 128
K = 16
WIDTH = 3 * LMB
STRIP = 16
LANES = 128
WIDE = 256
VMEM = pl.BlockSpec(memory_space=pltpu.VMEM)
SMEM = pl.BlockSpec(memory_space=pltpu.SMEM)
PARAMS = pltpu.CompilerParams(vmem_limit_bytes=32 * 1024 * 1024)


def invert_rows(cur_ref, start):
    lanes = pl.ds(start, LMB)
    entry = [[cur_ref[row, col : col + 1, lanes] for col in range(3)] for row in range(3)]
    cofactor = [
        [
            entry[(row + 1) % 3][(col + 1) % 3] * entry[(row + 2) % 3][(col + 2) % 3]
            - entry[(row + 1) % 3][(col + 2) % 3] * entry[(row + 2) % 3][(col + 1) % 3]
            for col in range(3)
        ]
        for row in range(3)
    ]
    determ = (
        entry[0][0] * cofactor[0][0] + entry[0][1] * cofactor[0][1] + entry[0][2] * cofactor[0][2]
    )
    return [[cofactor[col][row] / determ for col in range(3)] for row in range(3)]


def encode(dst, lanes, parts):
    blocks = len(parts)
    row = lax.broadcasted_iota(jnp.int32, (STRIP, lanes.size), 0)
    tops = jnp.full((STRIP, lanes.size), 2.0**-100, jnp.float32)
    for block, part in enumerate(parts):
        top = jnp.max(jnp.abs(part()), axis=0, keepdims=True)
        tops = jnp.where(row == block, jnp.maximum(top, tops), tops)
    power = jnp.ceil(jnp.log2(tops) - 14.99)
    inverse = jnp.exp2(-power)
    for block, part in enumerate(parts):
        coded = jnp.floor(part() * inverse[block : block + 1] + 0.5)
        dst[pl.ds(block * CB, CB), lanes] = coded.astype(jnp.int32).astype(jnp.int16)
    dst[pl.ds(blocks * CB, STRIP), lanes] = power.astype(jnp.int32).astype(jnp.int16)


def decode(src, lanes, first, blocks):
    below = src.shape[0] - STRIP
    strip = src[pl.ds(below, STRIP), lanes].astype(jnp.int32).astype(jnp.float32)
    scale = jnp.exp2(strip)
    return [
        src[pl.ds(block * CB, CB), lanes].astype(jnp.int32).astype(jnp.float32)
        * scale[block : block + 1]
        for block in range(first, first + blocks)
    ]


def gathered(place, keep, came, lanes, blocks):
    parts = [keep[place, pl.ds(block * CB, CB), lanes] for block in range(blocks)]
    for src in came:
        here = decode(src, lanes, place * blocks, blocks)
        parts = [part + other for part, other in zip(parts, here)]
    return parts


def given(values):
    return [functools.partial(lambda value: value, value) for value in values]


def spot_of(index, order):
    bits = len(order)
    return sum(((index >> (bits - 1 - pos)) & 1) << bit for pos, bit in enumerate(order))


def form_tile(plan, table, tile, pan, cur, rows):
    total, row_blocks = plan
    inverse = invert_rows(cur, tile * LMB)

    def one_group(group, carry):
        places = [group * row_blocks + block for block in range(row_blocks)]
        slots = [table[tile, total + place] for place in places]

        @pl.when(functools.reduce(jnp.maximum, slots) >= 0)
        def some():
            for place, slot in zip(places, slots):
                lines = pl.ds(pl.multiple_of(place * CB, CB), CB)

                @pl.when(slot >= 0)
                def form():
                    wide = pan[tile, slot].astype(jnp.float32)
                    split = [wide[:, c * LMB : (c + 1) * LMB] for c in range(3)]
                    for q in range(3):
                        formed = (
                            split[0] * inverse[0][q]
                            + split[1] * inverse[1][q]
                            + split[2] * inverse[2][q]
                        )
                        high = formed.astype(jnp.bfloat16)
                        low = (formed - high.astype(jnp.float32)).astype(jnp.bfloat16)
                        at = q * LMB
                        rows[tile, lines, at : at + LMB] = high
                        rows[tile, lines, WIDTH + at : WIDTH + at + LMB] = low

                @pl.when(slot < 0)
                def blank():
                    rows[tile, lines, :] = jnp.zeros((CB, 2 * WIDTH), jnp.bfloat16)

        return carry

    lax.fori_loop(0, rows.shape[1] // (row_blocks * CB), one_group, 0)


def form_kernel(plan, table, pan, cur, rows):
    for tile in range(rows.shape[0]):
        form_tile(plan, table, tile, pan, cur, rows)


def round_kernel(plan, table_a, table_b, pan_a, pan_b, rows_a, rows_b, *rest):
    sending, bases, orders, total, row_blocks, halves, tiles, pairs = plan
    outs, right, pair_at, acc = rest[:2], rest[2], rest[3], rest[4]
    extent = row_blocks * CB
    columns = pairs * LANES
    for base, order, out in zip(bases, orders, outs):
        acc[...] = jnp.zeros_like(acc)
        spots = [spot_of(half + (halves if sending else 0), order) for half in range(halves)]
        for table, pan, rows in ((table_a, pan_a, rows_a), (table_b, pan_b, rows_b)):

            def one_tile(tile, carry):
                used = [
                    functools.reduce(
                        jnp.maximum,
                        [
                            table[tile, total + spot * row_blocks + block]
                            for block in range(row_blocks)
                        ],
                    )
                    for spot in spots
                ]

                @pl.when(functools.reduce(jnp.maximum, used) >= 0)
                def some():
                    def one_pair(pair, count):
                        slots = [table[tile, base + 2 * pair + side] for side in range(2)]
                        live = jnp.maximum(slots[0], slots[1]) >= 0

                        @pl.when(live)
                        def stage():
                            pair_at[count] = pair * LANES
                            for side, slot in enumerate(slots):
                                first = pl.multiple_of(count * LANES + side * CB, CB)
                                lines = pl.ds(first, CB)

                                @pl.when(slot >= 0)
                                def fill():
                                    panel = pan[tile, slot]
                                    right[lines, :WIDTH] = panel
                                    right[lines, WIDTH:] = panel

                                @pl.when(slot < 0)
                                def blank():
                                    right[lines, :] = jnp.zeros((CB, 2 * WIDTH), jnp.bfloat16)

                        return count + jnp.where(live, 1, 0)

                    count = lax.fori_loop(0, pairs, one_pair, jnp.int32(0))
                    pair_at[count] = columns

                    def one_dot(double, carry):
                        first = pl.multiple_of(double * 2 * LANES, 2 * LANES)
                        for half, spot in enumerate(spots):

                            @pl.when(used[half] >= 0)
                            def add():
                                result = lax.dot_general(
                                    rows[tile, spot * extent : (spot + 1) * extent, :],
                                    right[pl.ds(first, 2 * LANES), :],
                                    (((1,), (1,)), ((), ())),
                                    preferred_element_type=jnp.float32,
                                )
                                for side in range(2):
                                    at = pl.multiple_of(pair_at[2 * double + side], LANES)
                                    acc[half, :, pl.ds(at, LANES)] += result[
                                        :, side * LANES : (side + 1) * LANES
                                    ]

                        return carry

                    lax.fori_loop(0, (count + 1) // 2, one_dot, 0)

                return carry

            lax.fori_loop(0, tiles, one_tile, 0)

        def store(start, carry):
            lanes = pl.ds(pl.multiple_of(start * WIDE, WIDE), WIDE)
            if sending:
                parts = [
                    functools.partial(
                        lambda half, block: acc[half, pl.ds(block * CB, CB), lanes], half, block
                    )
                    for half in range(halves)
                    for block in range(row_blocks)
                ]
                encode(out, lanes, parts)
            else:
                for half in range(halves):
                    out[half, :, lanes] = acc[half, :, lanes]
            return carry

        lax.fori_loop(0, columns // WIDE, store, 0)


def relay_kernel(plan, keep, *rest):
    row_blocks, size = plan
    dst = rest[-1]

    def code(start, carry):
        lanes = pl.ds(pl.multiple_of(start * WIDE, WIDE), WIDE)
        parts = []
        for place in range(size // 2, size):
            parts += given(gathered(place, keep, rest[:-1], lanes, row_blocks))
        encode(dst, lanes, parts)
        return carry

    lax.fori_loop(0, dst.shape[1] // WIDE, code, 0)


def cross_kernel(row_blocks, group, arrays, *rest):
    dsts = rest[2 * arrays :]
    for other, dst in enumerate(dsts):
        for start in range(0, group, LANES):
            parts = []
            for piece in range(2):
                keep, *came = rest[piece * arrays : (piece + 1) * arrays]
                lanes = pl.ds((other + 1) * group + start, LANES)
                parts += given(gathered(0, keep, came, lanes, row_blocks))
            encode(dst, pl.ds(start, LANES), parts)


def base_kernel(plan, me_ref, wide_ref, *rest):
    turn, row_blocks, col_blocks, arrays = plan
    out_ref = rest[-1]
    group = out_ref.shape[1] // 2
    first_row = (me_ref[0] * 2 + me_ref[1]) * row_blocks
    first_col = me_ref[2] * col_blocks
    lane = lax.broadcasted_iota(jnp.int32, (CB, LANES), 1) // CB
    for piece in range(2):
        keep, *came = rest[piece * arrays : (piece + 1) * arrays]
        for start in range(0, group, LANES):
            parts = gathered(0, keep, came, pl.ds(start, LANES), row_blocks)
            base = first_col + ((2 * turn + piece) * group + start) // CB
            for block in range(row_blocks):
                wide = jnp.where(base + lane == first_row + block, wide_ref[block], 0.0)
                out_ref[pl.ds(block * CB, CB), pl.ds(piece * group + start, LANES)] = (
                    wide - parts[block]
                )


def finish_kernel(row_blocks, far, base_ref, *rest):
    out_ref = rest[-1]
    group = out_ref.shape[1] // 2
    for piece in range(2):
        for start in range(0, group, LANES):
            total = [0.0] * row_blocks
            for src in rest[:far]:
                parts = decode(src, pl.ds(start, LANES), piece * row_blocks, row_blocks)
                total = [left + right for left, right in zip(total, parts)]
            lanes = pl.ds(piece * group + start, LANES)
            for block in range(row_blocks):
                lines = pl.ds(block * CB, CB)
                out_ref[lines, lanes] = base_ref[lines, lanes] - total[block]


def body(panels, curvature, visible_blocks, counts, camera_hessian):
    tiles = panels.shape[0]
    n_lm, n_cam = lax.axis_size("lm"), lax.axis_size("cam")
    chips = n_lm // 2
    bits = int(math.log2(chips))
    row_blocks = camera_hessian.shape[0]
    extent = row_blocks * CB
    col_blocks = row_blocks * n_lm // n_cam
    turns = col_blocks * CB // (2 * LANES)
    pieces = 2 * turns
    group = col_blocks * CB // pieces
    columns = group * n_cam
    total = row_blocks * n_lm
    orders = [list(range(bits)), list(reversed(range(bits)))]
    lm, cam = lax.axis_index("lm"), lax.axis_index("cam")
    me = jnp.stack([lm // 2, lm % 2, cam]).astype(jnp.int32)

    live = jnp.arange(K, dtype=jnp.int32)[None, :] < counts[:, None]
    ids = jnp.where(live, visible_blocks, -1)

    def swap(value, bit):
        return lax.ppermute(value, "lm", [(i, i ^ (1 << bit)) for i in range(n_lm)])

    pan_other, cur_other, ids_other = swap(panels, 0), swap(curvature, 0), swap(ids, 0)
    wide = jnp.concatenate([camera_hessian, camera_hessian], axis=-1)
    per = group // CB
    slots = jnp.arange(K, dtype=jnp.int32)[None, :, None]
    places = jnp.arange(total + chips * row_blocks, dtype=jnp.int32)

    def table_of(ids):
        inner = ids % col_blocks
        spot = ((inner // per) * n_cam + ((ids // col_blocks) ^ cam)) * per + inner % per
        owner = ids // row_blocks
        line = total + ((owner // 2) ^ (lm // 2)) * row_blocks + ids % row_blocks
        spot = jnp.where(ids >= 0, spot, -1)
        line = jnp.where((ids >= 0) & (owner % 2 == lm % 2), line, -1)
        found = (spot[:, :, None] == places) | (line[:, :, None] == places)
        return jnp.max(jnp.where(found, slots, -1), axis=1)

    table_a, table_b = table_of(ids), table_of(ids_other)
    formed = jax.ShapeDtypeStruct((tiles, chips * extent, 2 * WIDTH), jnp.bfloat16)
    def form_call(table, pan, cur):
        return pl.pallas_call(
            functools.partial(form_kernel, (total, row_blocks)),
            in_specs=[SMEM, VMEM, VMEM],
            out_specs=VMEM,
            out_shape=formed,
            compiler_params=PARAMS,
            name="form",
        )(table, pan, cur)

    rows_a = form_call(table_a, panels, curvature)
    rows_b = form_call(table_b, pan_other, cur_other)

    def round_call(sending, turn, tables):
        if sending:
            made = jax.ShapeDtypeStruct((chips // 2 * extent + STRIP, columns), jnp.int16)
        else:
            made = jax.ShapeDtypeStruct((chips // 2, extent, columns), jnp.float32)
        bases = [(2 * turn + which) * n_cam * per for which in range(2)]
        pairs = columns // LANES
        plan = (sending, bases, orders, total, row_blocks, chips // 2, tiles, pairs)
        return pl.pallas_call(
            functools.partial(round_kernel, plan),
            in_specs=[SMEM] * 2 + [VMEM] * 4,
            out_specs=[VMEM] * 2,
            out_shape=[made] * 2,
            scratch_shapes=[
                pltpu.VMEM((columns + LANES, 2 * WIDTH), jnp.bfloat16),
                pltpu.SMEM((pairs + 1,), jnp.int32),
                pltpu.VMEM((chips // 2, extent, columns + LANES), jnp.float32),
            ],
            compiler_params=PARAMS,
            name="send" if sending else "keep",
        )(*tables, panels, pan_other, rows_a, rows_b)

    tables = (table_a, table_b)
    sends, keeps = [], []
    for turn in range(turns):
        for sending, made in ((True, sends), (False, keeps)):
            made.append(list(round_call(sending, turn, tables)))
            tables = lax.optimization_barrier((tables, made[-1]))[0]

    came = [[[], []] for _ in range(turns)]
    result = None
    for turn in range(turns):
        if turn:
            sends[turn] = lax.optimization_barrier((sends[turn], crossed))[0]
        for stage in range(bits):
            for piece in range(2):
                came[turn][piece].append(swap(sends[turn][piece], orders[piece][stage] + 1))
            size = chips >> (stage + 1)
            if size == 1:
                break
            for piece in range(2):
                keep = keeps[turn][piece]
                if turn:
                    keep = lax.optimization_barrier((keep, far))[0]
                arrays = [keep] + came[turn][piece]
                sends[turn][piece] = pl.pallas_call(
                    functools.partial(relay_kernel, (row_blocks, size)),
                    in_specs=[VMEM] * len(arrays),
                    out_specs=VMEM,
                    out_shape=jax.ShapeDtypeStruct((size // 2 * extent + STRIP, columns), jnp.int16),
                    compiler_params=PARAMS,
                    name="relay",
                )(*arrays)

        near = [array for piece in range(2) for array in [keeps[turn][piece]] + came[turn][piece]]
        arrays = len(near) // 2
        crossed = pl.pallas_call(
            functools.partial(cross_kernel, row_blocks, group, arrays),
            in_specs=[VMEM] * len(near),
            out_specs=[VMEM] * (n_cam - 1),
            out_shape=[jax.ShapeDtypeStruct((2 * extent + STRIP, group), jnp.int16)] * (n_cam - 1),
            compiler_params=PARAMS,
            name="cross",
        )(*near)
        far = [
            lax.ppermute(value, "cam", [(i, i ^ (pos + 1)) for i in range(n_cam)])
            for pos, value in enumerate(crossed)
        ]
        base = pl.pallas_call(
            functools.partial(base_kernel, (turn, row_blocks, col_blocks, arrays)),
            in_specs=[SMEM, VMEM] + [VMEM] * len(near),
            out_specs=VMEM,
            out_shape=jax.ShapeDtypeStruct((extent, 2 * group), jnp.float32),
            compiler_params=PARAMS,
            name="base",
        )(me, wide, *near)
        before = [] if result is None else [result]
        result = pl.pallas_call(
            functools.partial(finish_kernel, row_blocks, n_cam - 1),
            grid=(1,),
            in_specs=[VMEM] * n_cam + [pl.BlockSpec(memory_space=pl.ANY)] * len(before),
            out_specs=pl.BlockSpec((extent, 2 * group), lambda step, turn=turn: (0, turn)),
            out_shape=jax.ShapeDtypeStruct((extent, col_blocks * CB), jnp.float32),
            input_output_aliases={n_cam: 0} if before else {},
            compiler_params=PARAMS,
            name="finish",
        )(base, *far, *before)
    return result


def solution(mesh):
    return jax.shard_map(
        body,
        mesh=mesh,
        in_specs=(
            P(("lm", "cam"), None, None, None),
            P(None, None, ("lm", "cam")),
            P(("lm", "cam"), None),
            P(("lm", "cam")),
            P("lm", None, None),
        ),
        out_specs=P("lm", "cam"),
        check_vma=False,
    )
```
